32 devices in a mesh: dp: 8 (over z, x), tensor: 4 (over y, core).
Axes of the slice: x: 2, y: 2, z: 4, core: 2. Of those that a mesh axis runs over, the one named last changes fastest.
Arguments:
- tokens: bfloat16 [24, 1024, 512], P(None, 'dp'), may hold values from -6 to 6
- cotangent: bfloat16 [24, 1024, 512], P(None, 'dp'), may hold values from -6 to 6
- ln_gain: float32 [512], replicated, may hold values from 0.5 to 1.5
- ln_bias: float32 [512], replicated, may hold values from -3 to 3
- skip_gain: float32 [512], replicated, may hold values from -3 to 3
- in_real: bfloat16 [512, 256], P(None, 'tensor'), may hold values from -0.25 to 0.25
- in_imag: bfloat16 [512, 256], P(None, 'tensor'), may hold values from -0.25 to 0.25
- out_real: bfloat16 [256, 512], P('tensor'), may hold values from -0.25 to 0.25
- out_imag: bfloat16 [256, 512], P('tensor'), may hold values from -0.25 to 0.25
- nu_log: float32 [256], P('tensor'), may hold values from -6.9 to -3
- theta_log: float32 [256], P('tensor'), may hold values from -4 to 0
- gamma_log: float32 [256], P('tensor'), may hold values from -4 to -2
- up_weight: bfloat16 [512, 1024], P(None, 'tensor'), may hold values from -0.25 to 0.25
- gate_weight: bfloat16 [512, 1024], P(None, 'tensor'), may hold values from -0.25 to 0.25
- down_weight: bfloat16 [1024, 512], P('tensor'), may hold values from -0.375 to 0.375
- lengths: int32 [24], replicated, may hold values from 128 to 1024, as said below
Outputs:
- block_out: bfloat16 [24, 1024, 512], P(None, 'dp')
- input_grad: float32 [24, 1024, 512], P(None, 'dp')
- ln_gain_grad: float32 [512], replicated
- ln_bias_grad: float32 [512], replicated
- skip_gain_grad: float32 [512], replicated
- in_real_grad: float32 [512, 256], P(None, 'tensor')
- in_imag_grad: float32 [512, 256], P(None, 'tensor')
- out_real_grad: float32 [256, 512], P('tensor')
- out_imag_grad: float32 [256, 512], P('tensor')
- nu_log_grad: float32 [256], P('tensor')
- theta_log_grad: float32 [256], P('tensor')
- gamma_log_grad: float32 [256], P('tensor')
- up_weight_grad: float32 [512, 1024], P(None, 'tensor')
- gate_weight_grad: float32 [512, 1024], P(None, 'tensor')
- down_weight_grad: float32 [1024, 512], P('tensor')
The draws below stay inside these ranges and needn't reach their ends.
Inputs may be any that keep to these rules, and one draw needn't show every extreme that they name: `lengths`: live positions of each sequence; its other positions up to 1024 are padding.
All inputs are finite; a program needn't handle non-finite values.
Results may differ from the reference program's by a relative error of at most 0.0095.
Values may be sent and summed in bfloat16 or wider, within the bound.
No kernel may reach another device: no remote copies, remote signals or barrier semaphores. Data moves between devices by JAX's collectives and lax.ppermute only.
A program may use at most 192 MiB of HBM per device.

```python
from functools import partial
import jax
import jax.numpy as jnp
from jax import lax

D = 512
N = 256
FF = 1024
LMAX = 1024
SEQS = 24


def draw_lengths(key, part):
    base_key = jax.random.fold_in(key, 17)
    length_key, long_key, short_key = jax.random.split(base_key, 3)
    series = lax.iota(jnp.int32, SEQS)
    drawn_len = jax.random.randint(length_key, (SEQS,), LMAX // 8, LMAX + 1, dtype=jnp.int32)
    longest = jax.random.randint(long_key, (), 0, SEQS, dtype=jnp.int32)
    shortest = (longest + 1 + jax.random.randint(short_key, (), 0, SEQS - 1, dtype=jnp.int32)) % SEQS
    drawn_len = jnp.where(series == longest, LMAX, drawn_len)
    drawn_len = jnp.where(series == shortest, LMAX // 8, drawn_len)
    return drawn_len


def level_of(stream_key, shape, shards, low, top_value):
    loudness = 1.0
    for axis_at, shards_of in shards:
        heights = jax.random.uniform(jax.random.fold_in(jax.random.fold_in(stream_key, 6), axis_at), (shards_of,), jnp.float32, low / len(shards), top_value / len(shards))
        loudness = loudness * jnp.repeat(jnp.exp(heights), shape[axis_at] // shards_of).reshape((-1,) + (1,) * (len(shape) - 1 - axis_at))
    return loudness


def centred(own_key, dims, width, most, shards=(), kind=jnp.bfloat16):
    array = width * jax.random.normal(own_key, dims, jnp.float32)
    if shards:
        array = array * level_of(own_key, dims, shards, -0.22, 0.18)
    return jnp.clip(array, -most, most).astype(kind)


def setup_inputs(seed: int = 0) -> dict:
    key_list = jax.random.split(jax.random.key(seed), 17)
    tokens = centred(key_list[0], (SEQS, LMAX, D), 1.0, 6.0, ((1, 8),))
    cotangent = centred(key_list[1], (SEQS, LMAX, D), 1.0, 6.0, ((1, 8),))
    ln_gain = jnp.clip(1.0 + 0.1 * jax.random.normal(key_list[2], (D,), jnp.float32), 0.5, 1.5)
    ln_bias = centred(key_list[3], (D,), 0.5, 3.0, (), jnp.float32)
    skip_gain = centred(key_list[4], (D,), 0.5, 3.0, (), jnp.float32)
    in_real = centred(key_list[5], (D, N), D ** -0.5, 0.25, ((1, 4),))
    in_imag = centred(key_list[6], (D, N), D ** -0.5, 0.25, ((1, 4),))
    out_real = centred(key_list[7], (N, D), (2 * N) ** -0.5, 0.25, ((0, 4),))
    out_imag = centred(key_list[8], (N, D), (2 * N) ** -0.5, 0.25, ((0, 4),))
    nu_log = jnp.clip(-6.9 + 3.9 * jax.random.uniform(key_list[9], (N,), jnp.float32) ** level_of(key_list[9], (N,), ((0, 4),), -0.2, 0.2), -6.9, -3.0)
    theta_log = jnp.clip(-4.0 + 4.0 * jax.random.uniform(key_list[10], (N,), jnp.float32) ** level_of(key_list[10], (N,), ((0, 4),), -0.2, 0.2), -4.0, 0.0)
    gamma_log = jnp.clip(-4.0 + 2.0 * jax.random.uniform(key_list[11], (N,), jnp.float32) ** level_of(key_list[11], (N,), ((0, 4),), -0.2, 0.2), -4.0, -2.0)
    up_weight = centred(key_list[12], (D, FF), D ** -0.5, 0.25, ((1, 4),))
    gate_weight = centred(key_list[13], (D, FF), D ** -0.5, 0.25, ((1, 4),))
    down_weight = centred(key_list[14], (FF, D), (FF // 4) ** -0.5, 0.375, ((0, 4),))
    lengths = draw_lengths(jax.random.fold_in(key_list[16], 71), 0)
    return dict(tokens=tokens, cotangent=cotangent, ln_gain=ln_gain, ln_bias=ln_bias, skip_gain=skip_gain, in_real=in_real, in_imag=in_imag, out_real=out_real, out_imag=out_imag, nu_log=nu_log, theta_log=theta_log, gamma_log=gamma_log, up_weight=up_weight, gate_weight=gate_weight, down_weight=down_weight, lengths=lengths)


EPSILON = 1e-05

@jax.custom_vjp
def low(v):
    return lax.optimization_barrier(v.astype(jnp.bfloat16)).astype(jnp.float32)

@jax.custom_vjp
def low_back(v):
    return v

def low_keep(v):
    return (low(v), None)

def low_pass(kept, grad):
    return (grad,)

def back_keep(v):
    return (v, None)

def back_low(kept, grad):
    return (low(grad),)
low.defvjp(low_keep, low_pass)
low_back.defvjp(back_keep, back_low)

def product(left, right):
    return jnp.dot(left, right, precision=lax.Precision.HIGHEST, preferred_element_type=jnp.float32)

def sequence_out(weights, token_rows, live_mask):
    ln_gain, ln_bias, skip_gain, in_real, in_imag, out_real, out_imag, nu_log, theta_log, gamma_log, up_weight, gate_weight, down_weight = weights
    centre = lax.optimization_barrier(jnp.mean(token_rows, axis=-1, keepdims=True))
    shifted = token_rows - centre
    variance = lax.optimization_barrier(jnp.mean(shifted * shifted, axis=-1, keepdims=True))
    normed_out = shifted * lax.rsqrt(variance + EPSILON) * ln_gain + ln_bias
    normed_low = low(normed_out)
    drive_real = low_back(product(normed_low, in_real))
    drive_imag = low_back(product(normed_low, in_imag))
    modulus = jnp.exp(-jnp.exp(nu_log))
    angle = jnp.exp(theta_log)
    decay_real = modulus * jnp.cos(angle)
    decay_imag = modulus * jnp.sin(angle)
    input_gain = jnp.exp(gamma_log)

    def advance(state_pair, drive_pair):
        next_real = decay_real * state_pair[0] - decay_imag * state_pair[1] + drive_pair[0]
        next_imag = decay_real * state_pair[1] + decay_imag * state_pair[0] + drive_pair[1]
        return ((next_real, next_imag), (next_real, next_imag))
    start_state = (jnp.zeros_like(decay_real), jnp.zeros_like(decay_real))
    final_state, (state_real, state_imag) = lax.scan(advance, start_state, (input_gain * drive_real, input_gain * drive_imag))
    mixed = low_back(product(low(state_real), out_real) - product(low(state_imag), out_imag)) + skip_gain * normed_out
    act_low = low(jax.nn.gelu(mixed))
    up_proj = low_back(product(act_low, up_weight))
    gate_proj = low_back(product(act_low, gate_weight))
    hidden_low = low(up_proj * jax.nn.sigmoid(gate_proj))
    branch_sum = low_back(product(hidden_low, down_weight))
    return live_mask[:, None] * (token_rows + branch_sum)

def reference(tokens, cotangent, ln_gain, ln_bias, skip_gain, in_real, in_imag, out_real, out_imag, nu_log, theta_log, gamma_log, up_weight, gate_weight, down_weight, lengths):
    weights = (ln_gain.astype(jnp.float32), ln_bias.astype(jnp.float32), skip_gain.astype(jnp.float32), in_real.astype(jnp.float32), in_imag.astype(jnp.float32), out_real.astype(jnp.float32), out_imag.astype(jnp.float32), nu_log.astype(jnp.float32), theta_log.astype(jnp.float32), gamma_log.astype(jnp.float32), up_weight.astype(jnp.float32), gate_weight.astype(jnp.float32), down_weight.astype(jnp.float32))
    live_all = (lax.broadcasted_iota(jnp.int32, (SEQS, LMAX), 1) < lengths[:, None]).astype(jnp.float32)

    def one_sequence(totals, inputs_now):
        token_rows, cot_rows, live_mask = inputs_now
        out_rows, pullback = jax.vjp(partial(sequence_out, live_mask=live_mask), weights, token_rows)
        weight_grads, row_grad = pullback(cot_rows)
        return (jax.tree.map(jnp.add, totals, weight_grads), (out_rows.astype(jnp.bfloat16), row_grad))
    totals, (block_out, input_grad) = lax.scan(one_sequence, jax.tree.map(jnp.zeros_like, weights), (tokens.astype(jnp.float32), cotangent.astype(jnp.float32), live_all))
    return (block_out, input_grad, totals[0], totals[1], totals[2], totals[3], totals[4], totals[5], totals[6], totals[7], totals[8], totals[9], totals[10], totals[11], totals[12])
```

```python
import functools
import math

import jax
import jax.numpy as jnp
from jax import lax
from jax.experimental import pallas as pl
from jax.experimental.pallas import tpu as pltpu
from jax.sharding import PartitionSpec as P

EPSILON = 1e-05
TENSOR = 4
TILE = 8
BLOCK = 256
PARAM_ROWS = 16
F32 = jnp.float32
BF16 = jnp.bfloat16
GELU_K = math.sqrt(2.0 / math.pi)
VMEM_BYTES = 56 * 1024 * 1024


def dot(left, right):
    return jnp.dot(left, right, preferred_element_type=F32)


def dot_nt(left, right):
    return lax.dot_general(left, right, (((1,), (1,)), ((), ())), preferred_element_type=F32)


def dot_tn(left, right):
    return lax.dot_general(left, right, (((0,), (0,)), ((), ())), preferred_element_type=F32)


def layer_norm(rows):
    centre = jnp.mean(rows, axis=-1, keepdims=True)
    shifted = rows - centre
    variance = jnp.mean(shifted * shifted, axis=-1, keepdims=True)
    inv_scale = lax.rsqrt(variance + EPSILON)
    return shifted * inv_scale, inv_scale


def cmul(ar, ai, br, bi):
    return ar * br - ai * bi, ar * bi + ai * br


def read_params(packs, row):
    total = None
    for pack in packs:
        rows = pack[row : row + PARAM_ROWS, :].astype(F32)
        total = rows if total is None else total + rows
    states = total.shape[1] // 2
    at = lambda k: total[k : k + 1, :states] + total[k + 3 : k + 4, :states] + total[k + 6 : k + 7, :states]
    return at(0), at(1), at(2)


def powers_of(decay_real, decay_imag, exponent):
    out_r = jnp.ones(exponent.shape, F32)
    out_i = jnp.zeros(exponent.shape, F32)
    br, bi = decay_real, decay_imag
    for bit in range(4):
        mr, mi = cmul(out_r, out_i, br, bi)
        on = ((exponent >> bit) & 1) == 1
        out_r = jnp.where(on, mr, out_r)
        out_i = jnp.where(on, mi, out_i)
        br, bi = cmul(br, bi, br, bi)
    return out_r, out_i


def fill_tables(decay_real, decay_imag, length, backwards, step_ref, full_ref):
    states = decay_real.shape[1]
    row = lax.broadcasted_iota(jnp.int32, (TILE, states), 0)
    if backwards:
        row = TILE - 1 - row
    zero = jnp.zeros((TILE, states), F32)
    for k, shift in enumerate((1, 2, 4)):
        pr, pi = powers_of(decay_real, decay_imag, jnp.full((TILE, states), shift, jnp.int32))
        step_ref[k, 0] = jnp.where(row >= shift, pr, zero)
        step_ref[k, 1] = jnp.where(row >= shift, pi, zero)
    pr, pi = powers_of(decay_real, decay_imag, row + 1)
    step_ref[3, 0] = pr
    step_ref[3, 1] = pi
    if full_ref is not None:
        er, ei = powers_of(decay_real, decay_imag, jnp.full((TILE, states), TILE, jnp.int32))
        tiles = length // TILE
        for n in range(tiles):
            at = (tiles - 1 - n if backwards else n) * TILE
            full_ref[0, at : at + TILE, :] = pr
            full_ref[1, at : at + TILE, :] = pi
            pr, pi = cmul(pr, pi, er, ei)


def scan_block(drive_ref, out_ref, step_ref, length, backwards, finish):
    rows, lanes = drive_ref.shape
    states = lanes // 2
    tiles = length // TILE
    table = [(step_ref[k, 0], step_ref[k, 1]) for k in range(4)]
    edge = 0 if backwards else TILE - 1
    for s in range(rows // length):
        cr = ci = None
        for n in range(tiles):
            at = s * length + (tiles - 1 - n if backwards else n) * TILE
            hr = drive_ref[at : at + TILE, :states]
            hi = drive_ref[at : at + TILE, states:]
            for k, shift in enumerate((1, 2, 4)):
                turn = TILE - shift if backwards else shift
                sr = pltpu.roll(hr, turn, 0)
                si = pltpu.roll(hi, turn, 0)
                mr, mi = cmul(table[k][0], table[k][1], sr, si)
                hr, hi = hr + mr, hi + mi
            if cr is not None:
                mr, mi = cmul(table[3][0], table[3][1], cr, ci)
                hr, hi = hr + mr, hi + mi
            out_ref[at : at + TILE, :states] = hr
            out_ref[at : at + TILE, states:] = hi
            cr, ci = hr[edge : edge + 1], hi[edge : edge + 1]
        finish(s, cr, ci)


def incoming(ends_ref, place, decay_r, decay_i, backwards, out_ref):
    groups, seqs, lanes = ends_ref.shape
    states = lanes // 2
    sr = jnp.zeros((seqs, states), F32)
    si = jnp.zeros((seqs, states), F32)
    for j in reversed(range(groups)) if backwards else range(groups):
        mr, mi = cmul(decay_r, decay_i, sr, si)
        use = j > place if backwards else j < place
        sr = jnp.where(use, mr + ends_ref[j, :, :states], sr)
        si = jnp.where(use, mi + ends_ref[j, :, states:], si)
    out_ref[:, :states] = sr
    out_ref[:, states:] = si


def assemble_input(packs, shard, out_ref):
    per = packs[0].shape[0] - PARAM_ROWS
    half = per // 2
    states = out_ref.shape[0] // 2
    for k, pack in enumerate(packs):
        at = pl.multiple_of((shard ^ k) * half, half)
        out_ref[pl.ds(at, half), :] = pack[:half, :]
        out_ref[pl.ds(states + at, half), :] = pack[half:per, :]


def drive_kernel(where_ref, tok_ref, a0, a1, a2, a3, gain_ref, bias_ref, local_ref, ends_ref, in_t, step, drive, gam, *, length):
    block = pl.program_id(0)
    packs = (a0, a1, a2, a3)
    states = in_t.shape[0] // 2

    @pl.when(block == 0)
    def _():
        assemble_input(packs, where_ref[2], in_t)
        dr, di, gain = read_params(packs, a0.shape[0] - PARAM_ROWS)
        fill_tables(dr, di, length, False, step, None)
        gam[...] = jnp.concatenate([gain, gain], axis=1)

    normed, _ = layer_norm(tok_ref[...].astype(F32))
    low = (normed * gain_ref[...] + bias_ref[...]).astype(BF16)
    drive[...] = dot_nt(low, in_t[...]) * gam[...]
    per_block = drive.shape[0] // length

    def finish(s, r, i):
        ends_ref[pl.ds(block * per_block + s, 1), :states] = r
        ends_ref[pl.ds(block * per_block + s, 1), states:] = i

    scan_block(drive, local_ref, step, length, False, finish)


def middle_kernel(
    where_ref,
    lens_ref,
    tok_ref,
    cot_ref,
    local_ref,
    ends_ref,
    a0,
    a1,
    a2,
    a3,
    gain_ref,
    bias_ref,
    skip_ref,
    b0,
    b1,
    b2,
    b3,
    out_ref,
    state_ref,
    back_ref,
    backends_ref,
    ylow_ref,
    hid_half_ref,
    cotm_ref,
    act_ref,
    ul_half_ref,
    skip_grad_ref,
    c_all,
    down_all,
    ug_all,
    step,
    full,
    carry,
    hid,
    ul,
    slope,
    eback,
    sems,
    *,
    length,
):
    block = pl.program_id(0)
    place, core, shard = where_ref[0], where_ref[1], where_ref[2]
    states = c_all.shape[0] // 2
    rows, width = tok_ref.shape
    per_block = rows // length
    per_s = states // TENSOR
    per_f = down_all.shape[0] // TENSOR

    @pl.when(block == 0)
    def _():
        copies = []
        for k, pack in enumerate((b0, b1, b2, b3)):
            t = shard ^ k
            moves = (
                (pack.at[pl.ds(0, per_s), :], c_all.at[pl.ds(pl.multiple_of(t * per_s, per_s), per_s), :]),
                (pack.at[pl.ds(per_s, per_s), :], c_all.at[pl.ds(pl.multiple_of(states + t * per_s, per_s), per_s), :]),
                (pack.at[pl.ds(2 * per_s, per_f), :], down_all.at[pl.ds(pl.multiple_of(t * per_f, per_f), per_f), :]),
                (
                    pack.at[pl.ds(2 * per_s + per_f, width), :],
                    ug_all.at[:, pl.ds(pl.multiple_of(t * 2 * per_f, 2 * per_f), 2 * per_f)],
                ),
            )
            for n, (src, dst) in enumerate(moves):
                copies.append(pltpu.make_async_copy(src, dst, sems.at[k, n]))
        for copy in copies:
            copy.start()
        dr, di, _ = read_params((a0, a1, a2, a3), a0.shape[0] - PARAM_ROWS)
        fill_tables(dr, di, length, False, step, full)
        incoming(ends_ref, place, full[0, length - 1 :, :], full[1, length - 1 :, :], False, carry)
        fill_tables(dr, di, length, True, step, None)
        skip_grad_ref[...] = jnp.zeros(skip_grad_ref.shape, F32)
        for copy in copies:
            copy.wait()

    x = tok_ref[...].astype(F32)
    normed, _ = layer_norm(x)
    u = normed * gain_ref[...] + bias_ref[...]
    for s in range(per_block):
        seq = block * per_block + s
        span = slice(s * length, (s + 1) * length)
        sr = carry[pl.ds(seq, 1), :states]
        si = carry[pl.ds(seq, 1), states:]
        mr, mi = cmul(full[0], full[1], sr, si)
        state_ref[span, :states] = (local_ref[span, :states] + mr).astype(BF16)
        state_ref[span, states:] = (-(local_ref[span, states:] + mi)).astype(BF16)
        live = lax.broadcasted_iota(jnp.int32, (length, width), 0) < (lens_ref[core * ends_ref.shape[1] + seq] - place * length)
        cotm_ref[span, :] = jnp.where(live, cot_ref[span, :].astype(F32), 0.0).astype(BF16)
    y = dot(state_ref[...], c_all[...]) + skip_ref[...] * u
    square = y * y
    th = jnp.tanh(GELU_K * y * (1.0 + 0.044715 * square))
    act_ref[...] = (0.5 * y * (1.0 + th)).astype(BF16)
    slope[...] = 0.5 * (1.0 + th) + (0.5 * GELU_K) * y * (1.0 - th * th) * (1.0 + (3 * 0.044715) * square)
    act = act_ref[...]
    cotm = cotm_ref[...]
    for t in range(TENSOR):
        both = dot(act, ug_all[:, 2 * per_f * t : 2 * per_f * (t + 1)])
        up = both[:, :per_f]
        sig = jax.nn.sigmoid(both[:, per_f:])
        hid[:, per_f * t : per_f * (t + 1)] = (up * sig).astype(BF16)
        hid_grad = dot_nt(cotm, down_all[per_f * t : per_f * (t + 1), :])
        up_grad = hid_grad * sig
        ul[:, 2 * per_f * t : 2 * per_f * t + per_f] = up_grad.astype(BF16)
        ul[:, 2 * per_f * t + per_f : 2 * per_f * (t + 1)] = (up_grad * up * (1.0 - sig)).astype(BF16)
    added = dot(hid[...], down_all[...])
    act_grad = dot_nt(ul[...], ug_all[...])
    for s in range(per_block):
        seq = block * per_block + s
        span = slice(s * length, (s + 1) * length)
        live = lax.broadcasted_iota(jnp.int32, (length, width), 0) < (lens_ref[core * ends_ref.shape[1] + seq] - place * length)
        out_ref[span, :] = jnp.where(live, tok_ref[span, :].astype(F32) + added[span, :], 0.0).astype(BF16)
    y_grad = act_grad * slope[...]
    skip_grad_ref[...] += jnp.sum(y_grad * u, axis=0, keepdims=True)
    ylow_ref[...] = y_grad.astype(BF16)
    eback[...] = dot_nt(ylow_ref[...], c_all[...])

    def finish(s, r, i):
        backends_ref[pl.ds(block * per_block + s, 1), :states] = r
        backends_ref[pl.ds(block * per_block + s, 1), states:] = i

    scan_block(eback, back_ref, step, length, True, finish)
    side = shard // 2
    hid_half_ref[...] = hid[:, pl.ds(pl.multiple_of(side * 2 * per_f, 2 * per_f), 2 * per_f)]
    ul_half_ref[...] = ul[:, pl.ds(pl.multiple_of(side * 4 * per_f, 4 * per_f), 4 * per_f)]


def weight_kernel(where_ref, hid_ref, cotm_ref, act_ref, ul_ref, state_ref, ylow_ref, own_ref, sent_ref):
    core, shard = where_ref[1], where_ref[2]
    states = state_ref.shape[1] // 2
    per_s = states // TENSOR
    per_f = hid_ref.shape[1] // 2
    side = shard // 2
    cols = [
        state_ref[:, pl.ds(pl.multiple_of(k * states + side * 2 * per_s, 2 * per_s), 2 * per_s)] for k in range(2)
    ]
    ylow = ylow_ref[...]
    out_grad = [dot_tn(c, ylow) for c in cols]
    for n, ref in ((core, own_ref), (1 - core, sent_ref)):
        for k in range(2):
            part = jnp.where(n == 0, out_grad[k][:per_s], out_grad[k][per_s:])
            ref[k * per_s : (k + 1) * per_s, :] = part.astype(ref.dtype)
        hid = hid_ref[:, pl.ds(pl.multiple_of(n * per_f, per_f), per_f)]
        ref[2 * per_s : 2 * per_s + per_f, :] = dot_tn(hid, cotm_ref[...]).astype(ref.dtype)
        ul = ul_ref[:, pl.ds(pl.multiple_of(n * 2 * per_f, 2 * per_f), 2 * per_f)]
        ref[2 * per_s + per_f :, :] = dot_tn(act_ref[...], ul).astype(ref.dtype)


def last_kernel(
    where_ref,
    tok_ref,
    cotm_ref,
    back_ref,
    state_ref,
    ylow_ref,
    ends_ref,
    skip_grad_ref,
    a0,
    a1,
    a2,
    a3,
    gain_ref,
    bias_ref,
    skip_ref,
    grad_ref,
    own_ref,
    sent_ref,
    in_t,
    step,
    full,
    carry,
    gam,
    dlow,
    in_grad,
    lam_grad,
    gain_grad,
    bias_grad,
    *,
    length,
):
    block = pl.program_id(0)
    place, core, shard = where_ref[0], where_ref[1], where_ref[2]
    states = in_t.shape[0] // 2
    rows, width = tok_ref.shape
    per_block = rows // length
    per_s = states // TENSOR
    packs = (a0, a1, a2, a3)

    @pl.when(block == 0)
    def _():
        assemble_input(packs, shard, in_t)
        dr, di, gain = read_params(packs, a0.shape[0] - PARAM_ROWS)
        fill_tables(dr, di, length, True, step, full)
        incoming(ends_ref, place, full[0, :1, :], full[1, :1, :], True, carry)
        gam[...] = jnp.concatenate([gain, -gain], axis=1)
        in_grad[...] = jnp.zeros(in_grad.shape, F32)
        lam_grad[...] = jnp.zeros(lam_grad.shape, F32)
        gain_grad[...] = jnp.zeros(gain_grad.shape, F32)
        bias_grad[...] = jnp.zeros(bias_grad.shape, F32)

    normed, inv_scale = layer_norm(tok_ref[...].astype(F32))
    low = (normed * gain_ref[...] + bias_ref[...]).astype(BF16)
    for s in range(per_block):
        seq = block * per_block + s
        span = slice(s * length, (s + 1) * length)
        sr = carry[pl.ds(seq, 1), :states]
        si = carry[pl.ds(seq, 1), states:]
        mr, mi = cmul(full[0], full[1], sr, si)
        gr = back_ref[span, :states] + mr
        gi = back_ref[span, states:] + mi
        dlow[span, :states] = (gr * gam[:, :states]).astype(BF16)
        dlow[span, states:] = (gi * gam[:, states:]).astype(BF16)
        nr = jnp.concatenate([gr[1:], sr], axis=0)
        ni = jnp.concatenate([gi[1:], si], axis=0)
        hr = state_ref[span, :states].astype(F32)
        hi = state_ref[span, states:].astype(F32)
        lam_grad[:, :states] += jnp.sum(nr * hr + ni * hi, axis=0, keepdims=True)
        lam_grad[:, states:] += jnp.sum(nr * hi - ni * hr, axis=0, keepdims=True)
    u_grad = dot(dlow[...], in_t[...]) + ylow_ref[...].astype(F32) * skip_ref[...]
    bias_grad[...] += jnp.sum(u_grad, axis=0, keepdims=True)
    gain_grad[...] += jnp.sum(u_grad * normed, axis=0, keepdims=True)
    scaled = u_grad * gain_ref[...]
    grad = (
        scaled
        - jnp.mean(scaled, axis=-1, keepdims=True)
        - normed * jnp.mean(scaled * normed, axis=-1, keepdims=True)
    )
    grad_ref[...] = (cotm_ref[...].astype(F32) + inv_scale * grad).astype(BF16)
    at = pl.multiple_of((shard // 2) * 2 * per_s, 2 * per_s)
    for k in range(2):
        cols = dlow[:, pl.ds(k * states + at, 2 * per_s)]
        in_grad[2 * per_s * k : 2 * per_s * (k + 1), :] += dot_tn(cols, low)

    @pl.when(block == pl.num_programs(0) - 1)
    def _():
        for n, ref in ((core, own_ref), (1 - core, sent_ref)):
            for k in range(2):
                part = in_grad[pl.ds(pl.multiple_of(2 * per_s * k + n * per_s, per_s), per_s), :]
                ref[k * per_s : (k + 1) * per_s, :] = part.astype(BF16)
            small = jnp.concatenate(
                [
                    gain_grad[...],
                    bias_grad[...],
                    skip_grad_ref[...],
                    lam_grad[...],
                    jnp.zeros((PARAM_ROWS - 4, width), F32),
                ],
                axis=0,
            )
            ref[2 * per_s :, :] = small.astype(BF16)


def whole(shape):
    return pl.BlockSpec(shape, lambda *_: (0,) * len(shape))


def call(kernel, grid, prefetch, in_specs, out_specs, out_shape, scratch, cost):
    return pl.pallas_call(
        kernel,
        grid_spec=pltpu.PrefetchScalarGridSpec(
            num_scalar_prefetch=prefetch,
            grid=grid,
            in_specs=in_specs,
            out_specs=out_specs,
            scratch_shapes=scratch,
        ),
        out_shape=out_shape,
        compiler_params=pltpu.CompilerParams(vmem_limit_bytes=VMEM_BYTES),
        cost_estimate=pl.CostEstimate(flops=cost[0], bytes_accessed=cost[1], transcendentals=0),
    )


def split_low(value):
    high = lax.reduce_precision(value, 8, 7)
    middle = lax.reduce_precision(value - high, 8, 7)
    return high, middle, value - high - middle


def core_swap(value):
    return lax.ppermute(value, "tensor", [(t, t ^ 1) for t in range(TENSOR)])


def side_swap(value):
    return lax.ppermute(value, "tensor", [(t, t ^ 2) for t in range(TENSOR)])


def gather_tensor(own):
    across = side_swap(own)
    return own, core_swap(own), across, core_swap(across)


def share_over_dp(value, groups):
    return lax.all_to_all(
        jnp.broadcast_to(value[None], (groups,) + value.shape), "dp", split_axis=0, concat_axis=0, tiled=True
    )


def sum_over_dp(value, groups):
    rows, width = value.shape
    parts = value.reshape(groups, rows // groups, width)
    mine = lax.all_to_all(parts, "dp", split_axis=0, concat_axis=0, tiled=True)
    total = jnp.sum(mine.astype(F32), axis=0).astype(BF16)
    return share_over_dp(total, groups).reshape(rows, width).astype(F32)


def sum_over_dp_small(value, groups):
    bit = 1
    while bit < groups:
        other = lax.ppermute(value, "dp", [(i, i ^ bit) for i in range(groups)])
        value = (value.astype(F32) + other.astype(F32)).astype(BF16)
        bit *= 2
    return value.astype(F32)


def shards(
    tokens,
    cotangent,
    ln_gain,
    ln_bias,
    skip_gain,
    in_real,
    in_imag,
    out_real,
    out_imag,
    nu_log,
    theta_log,
    gamma_log,
    up_weight,
    gate_weight,
    down_weight,
    lengths,
    *,
    groups,
):
    seqs, length, width = tokens.shape
    per_s = in_real.shape[1]
    per_f = up_weight.shape[1]
    states = per_s * TENSOR
    own_seqs = seqs // 2
    rows = own_seqs * length
    blocks = rows // BLOCK
    place = lax.axis_index("dp").astype(jnp.int32)
    shard = lax.axis_index("tensor").astype(jnp.int32)
    core = shard % 2
    where = jnp.stack([place, core, shard])

    modulus = jnp.exp(-jnp.exp(nu_log))
    angle = jnp.exp(theta_log)
    gain = jnp.exp(gamma_log)
    parts = [split_low(v) for v in (modulus * jnp.cos(angle), modulus * jnp.sin(angle), gain)]
    table = jnp.stack([parts[v][k] for k in range(3) for v in range(3)])
    placed = jnp.where(
        lax.broadcasted_iota(jnp.int32, (9, width), 1) // per_s == shard, jnp.tile(table, (1, width // per_s)), 0.0
    )
    pack_a = jnp.concatenate(
        [in_real.T, in_imag.T, placed.astype(BF16), jnp.zeros((PARAM_ROWS - 9, width), BF16)], axis=0
    )
    pack_b = jnp.concatenate(
        [out_real, out_imag, down_weight, jnp.concatenate([up_weight, gate_weight], axis=1)], axis=0
    )
    packs_a = gather_tensor(pack_a)
    packs_b = gather_tensor(pack_b)

    tok_rows = tokens.reshape(seqs * length, width)
    cot_rows = cotangent.reshape(seqs * length, width)
    row = lambda v: v.reshape(1, width)
    half_spec = pl.BlockSpec((BLOCK, width), lambda b, w, *_: (w[1] * blocks + b, 0))
    row_spec = lambda lanes: pl.BlockSpec((BLOCK, lanes), lambda b, *_: (b, 0))
    pack_spec = [whole(pack_a.shape)] * TENSOR
    vec_spec = whole((1, width))
    shape = jax.ShapeDtypeStruct
    lanes = 2 * states

    local, ends = call(
        functools.partial(drive_kernel, length=length),
        (blocks,),
        1,
        [half_spec] + pack_spec + [vec_spec] * 2,
        [row_spec(lanes), whole((own_seqs, lanes))],
        [shape((rows, lanes), F32), shape((own_seqs, lanes), F32)],
        [
            pltpu.VMEM((lanes, width), BF16),
            pltpu.VMEM((4, 2, TILE, states), F32),
            pltpu.VMEM((BLOCK, lanes), F32),
            pltpu.VMEM((1, lanes), F32),
        ],
        (2 * rows * width * lanes, rows * width * 8),
    )(where, tok_rows, *packs_a, row(ln_gain), row(ln_bias))

    all_ends = share_over_dp(ends, groups)

    out_own, state, back, back_ends, y_low, hid_half, cot_m, act, ul_half, skip_grad = call(
        functools.partial(middle_kernel, length=length),
        (blocks,),
        2,
        [half_spec, half_spec, row_spec(lanes), whole((groups, own_seqs, lanes))]
        + pack_spec
        + [vec_spec] * 3
        + [pl.BlockSpec(memory_space=pl.ANY)] * TENSOR,
        [
            row_spec(width),
            row_spec(lanes),
            row_spec(lanes),
            whole((own_seqs, lanes)),
            row_spec(width),
            row_spec(2 * per_f),
            row_spec(width),
            row_spec(width),
            row_spec(4 * per_f),
            vec_spec,
        ],
        [
            shape((rows, width), BF16),
            shape((rows, lanes), BF16),
            shape((rows, lanes), F32),
            shape((own_seqs, lanes), F32),
            shape((rows, width), BF16),
            shape((rows, 2 * per_f), BF16),
            shape((rows, width), BF16),
            shape((rows, width), BF16),
            shape((rows, 4 * per_f), BF16),
            shape((1, width), F32),
        ],
        [
            pltpu.VMEM((lanes, width), BF16),
            pltpu.VMEM((TENSOR * per_f, width), BF16),
            pltpu.VMEM((width, 2 * TENSOR * per_f), BF16),
            pltpu.VMEM((4, 2, TILE, states), F32),
            pltpu.VMEM((2, length, states), F32),
            pltpu.VMEM((own_seqs, lanes), F32),
            pltpu.VMEM((BLOCK, TENSOR * per_f), BF16),
            pltpu.VMEM((BLOCK, 2 * TENSOR * per_f), BF16),
            pltpu.VMEM((BLOCK, width), F32),
            pltpu.VMEM((BLOCK, lanes), F32),
            pltpu.SemaphoreType.DMA((TENSOR, 4)),
        ],
        (2 * rows * width * (2 * lanes + 6 * TENSOR * per_f), rows * width * 24),
    )(
        where,
        lengths,
        tok_rows,
        cot_rows,
        local,
        all_ends,
        *packs_a,
        row(ln_gain),
        row(ln_bias),
        row(skip_gain),
        *packs_b,
    )

    all_back = share_over_dp(back_ends, groups)
    out_other = core_swap(out_own)

    pack_rows = pack_b.shape[0]
    own_b, sent_b = call(
        weight_kernel,
        (1,),
        1,
        [
            whole((rows, 2 * per_f)),
            whole((rows, width)),
            whole((rows, width)),
            whole((rows, 4 * per_f)),
            whole((rows, lanes)),
            whole((rows, width)),
        ],
        [whole((pack_rows, width))] * 2,
        [shape((pack_rows, width), F32), shape((pack_rows, width), BF16)],
        [],
        (4 * rows * width * pack_rows, rows * width * 14),
    )(where, hid_half, cot_m, act, ul_half, state, y_low)
    pair_b = (own_b + core_swap(sent_b).astype(F32)).astype(BF16)
    grads_b = sum_over_dp(pair_b, groups)

    grad_own, own_a, sent_a = call(
        functools.partial(last_kernel, length=length),
        (blocks,),
        1,
        [
            half_spec,
            row_spec(width),
            row_spec(lanes),
            row_spec(lanes),
            row_spec(width),
            whole((groups, own_seqs, lanes)),
            vec_spec,
        ]
        + pack_spec
        + [vec_spec] * 3,
        [row_spec(width), whole(pack_a.shape), whole(pack_a.shape)],
        [shape((rows, width), BF16), shape(pack_a.shape, BF16), shape(pack_a.shape, BF16)],
        [
            pltpu.VMEM((lanes, width), BF16),
            pltpu.VMEM((4, 2, TILE, states), F32),
            pltpu.VMEM((2, length, states), F32),
            pltpu.VMEM((own_seqs, lanes), F32),
            pltpu.VMEM((1, lanes), F32),
            pltpu.VMEM((BLOCK, lanes), BF16),
            pltpu.VMEM((states, width), F32),
            pltpu.VMEM((1, lanes), F32),
            pltpu.VMEM((1, width), F32),
            pltpu.VMEM((1, width), F32),
        ],
        (2 * rows * width * (lanes + states), rows * width * 16),
    )(
        where,
        tok_rows,
        cot_m,
        back,
        state,
        y_low,
        all_back,
        skip_grad,
        *packs_a,
        row(ln_gain),
        row(ln_bias),
        row(skip_gain),
    )
    grad_other = core_swap(grad_own)
    pair_a = (own_a.astype(F32) + core_swap(sent_a).astype(F32)).astype(BF16)
    grads_a = sum_over_dp_small(pair_a, groups)

    def in_order(mine, other):
        first = core == 0
        return jnp.concatenate([jnp.where(first, mine, other), jnp.where(first, other, mine)], axis=0).reshape(
            seqs, length, width
        )

    block_out = in_order(out_own, out_other)
    input_grad = in_order(grad_own, grad_other).astype(F32)

    in_real_grad = grads_a[:per_s].T
    in_imag_grad = grads_a[per_s : 2 * per_s].T
    small = grads_a[2 * per_s :]
    lam_real = lax.dynamic_slice_in_dim(small[3, :states], shard * per_s, per_s)
    lam_imag = lax.dynamic_slice_in_dim(small[3, states:], shard * per_s, per_s)
    cos, sin = jnp.cos(angle), jnp.sin(angle)
    nu_grad = -jnp.exp(nu_log) * modulus * (lam_real * cos + lam_imag * sin)
    theta_grad = angle * modulus * (lam_imag * cos - lam_real * sin)
    gamma_grad = jnp.sum(in_real.astype(F32) * in_real_grad + in_imag.astype(F32) * in_imag_grad, axis=0)
    return (
        block_out,
        input_grad,
        small[0],
        small[1],
        small[2],
        in_real_grad,
        in_imag_grad,
        grads_b[:per_s],
        grads_b[per_s : 2 * per_s],
        nu_grad,
        theta_grad,
        gamma_grad,
        grads_b[2 * per_s + per_f :, :per_f],
        grads_b[2 * per_s + per_f :, per_f:],
        grads_b[2 * per_s : 2 * per_s + per_f],
    )


def solution(mesh):
    rows = P(None, "dp", None)
    columns = P(None, "tensor")
    lines = P("tensor", None)
    vector = P("tensor")
    in_specs = (rows, rows, P(), P(), P(), columns, columns, lines, lines, vector, vector, vector, columns, columns, lines, P())
    out_specs = (rows, rows, P(), P(), P(), columns, columns, lines, lines, vector, vector, vector, columns, columns, lines)
    return jax.shard_map(
        functools.partial(shards, groups=mesh.shape["dp"]),
        mesh=mesh,
        in_specs=in_specs,
        out_specs=out_specs,
        check_vma=False,
    )
```

```python
import functools
import math

import jax
import jax.numpy as jnp
from jax import lax
from jax.experimental import pallas as pl
from jax.experimental.pallas import tpu as pltpu
from jax.sharding import PartitionSpec as P

EPSILON = 1e-05
TENSOR = 4
TILE = 8
BLOCK = 256
PARAM_ROWS = 16
F32 = jnp.float32
BF16 = jnp.bfloat16
GELU_K = math.sqrt(2.0 / math.pi)
MIB = 1024 * 1024


def dot(left, right):
    return jnp.dot(left, right, preferred_element_type=F32)


def dot_nt(left, right):
    return lax.dot_general(left, right, (((1,), (1,)), ((), ())), preferred_element_type=F32)


def dot_tn(left, right):
    return lax.dot_general(left, right, (((0,), (0,)), ((), ())), preferred_element_type=F32)


def layer_norm(rows):
    centre = jnp.mean(rows, axis=-1, keepdims=True)
    shifted = rows - centre
    variance = jnp.mean(shifted * shifted, axis=-1, keepdims=True)
    inv_scale = lax.rsqrt(variance + EPSILON)
    return shifted * inv_scale, inv_scale


def cmul(ar, ai, br, bi):
    return ar * br - ai * bi, ar * bi + ai * br


def read_params(packs, row):
    total = None
    for pack in packs:
        rows = pack[row : row + PARAM_ROWS, :].astype(F32)
        total = rows if total is None else total + rows
    states = total.shape[1] // 2
    at = lambda k: total[k : k + 1, :states] + total[k + 3 : k + 4, :states] + total[k + 6 : k + 7, :states]
    return at(0), at(1), at(2)


def powers_of(decay_real, decay_imag, exponent):
    out_r = jnp.ones(exponent.shape, F32)
    out_i = jnp.zeros(exponent.shape, F32)
    br, bi = decay_real, decay_imag
    for bit in range(4):
        mr, mi = cmul(out_r, out_i, br, bi)
        on = ((exponent >> bit) & 1) == 1
        out_r = jnp.where(on, mr, out_r)
        out_i = jnp.where(on, mi, out_i)
        br, bi = cmul(br, bi, br, bi)
    return out_r, out_i


def fill_steps(decay_real, decay_imag, backwards, step_ref):
    states = decay_real.shape[1]
    row = lax.broadcasted_iota(jnp.int32, (TILE, states), 0)
    if backwards:
        row = TILE - 1 - row
    zero = jnp.zeros((TILE, states), F32)
    for k, shift in enumerate((1, 2, 4)):
        pr, pi = powers_of(decay_real, decay_imag, jnp.full((TILE, states), shift, jnp.int32))
        step_ref[k, 0] = jnp.where(row >= shift, pr, zero)
        step_ref[k, 1] = jnp.where(row >= shift, pi, zero)
    step_ref[3, 0], step_ref[3, 1] = powers_of(decay_real, decay_imag, row + 1)


def fill_powers(decay_real, decay_imag, backwards, first, full_ref):
    states = decay_real.shape[1]
    row = lax.broadcasted_iota(jnp.int32, (TILE, states), 0)
    if backwards:
        row = TILE - 1 - row
    pr, pi = powers_of(decay_real, decay_imag, row + first)
    er, ei = powers_of(decay_real, decay_imag, jnp.full((TILE, states), TILE, jnp.int32))
    tiles = full_ref.shape[1] // TILE
    for n in range(tiles):
        at = (tiles - 1 - n if backwards else n) * TILE
        full_ref[0, at : at + TILE, :] = pr
        full_ref[1, at : at + TILE, :] = pi
        pr, pi = cmul(pr, pi, er, ei)


def scan_block(drive_ref, out_ref, step_ref, length, backwards, finish):
    rows, lanes = drive_ref.shape
    states = lanes // 2
    tiles = length // TILE
    table = [(step_ref[k, 0], step_ref[k, 1]) for k in range(4)]
    edge = 0 if backwards else TILE - 1
    for s in range(rows // length):
        cr = ci = None
        for n in range(tiles):
            at = s * length + (tiles - 1 - n if backwards else n) * TILE
            hr = drive_ref[at : at + TILE, :states]
            hi = drive_ref[at : at + TILE, states:]
            for k, shift in enumerate((1, 2, 4)):
                turn = TILE - shift if backwards else shift
                sr = pltpu.roll(hr, turn, 0)
                si = pltpu.roll(hi, turn, 0)
                mr, mi = cmul(table[k][0], table[k][1], sr, si)
                hr, hi = hr + mr, hi + mi
            if cr is not None:
                mr, mi = cmul(table[3][0], table[3][1], cr, ci)
                hr, hi = hr + mr, hi + mi
            out_ref[at : at + TILE, :states] = hr
            out_ref[at : at + TILE, states:] = hi
            cr, ci = hr[edge : edge + 1], hi[edge : edge + 1]
        finish(s, cr, ci)


def incoming(far_refs, beside_ref, odd, powers_ref, backwards, out_ref):
    states = out_ref.shape[1] // 2
    lr, li = powers_ref[0:1, :states], powers_ref[0:1, states:]
    pr, pi = powers_ref[1:2, :states], powers_ref[1:2, states:]
    sr, si = far_refs[-1][:, :states], far_refs[-1][:, states:]
    for ref in far_refs[-2::-1]:
        mr, mi = cmul(pr, pi, sr, si)
        sr, si = mr + ref[:, :states], mi + ref[:, states:]
    mr, mi = cmul(lr, li, sr, si)
    second = odd == (0 if backwards else 1)
    out_ref[:, :states] = jnp.where(second, mr + beside_ref[:, :states], sr)
    out_ref[:, states:] = jnp.where(second, mi + beside_ref[:, states:], si)


def pair_kernel(where_ref, mine_ref, other_ref, powers_ref, out_ref, *, backwards):
    states = out_ref.shape[1] // 2
    second = where_ref[0] % 2 == (0 if backwards else 1)
    lr, li = powers_ref[0:1, :states], powers_ref[0:1, states:]
    pick = lambda first, part: jnp.where(second == first, other_ref[:, part], mine_ref[:, part])
    early, late = slice(0, states), slice(states, None)
    mr, mi = cmul(lr, li, pick(True, early), pick(True, late))
    out_ref[:, :states] = mr + pick(False, early)
    out_ref[:, states:] = mi + pick(False, late)


def assemble_input(packs, shard, out_ref):
    per = packs[0].shape[0] - PARAM_ROWS
    half = per // 2
    states = out_ref.shape[0] // 2
    for k, pack in enumerate(packs):
        at = pl.multiple_of((shard ^ k) * half, half)
        out_ref[pl.ds(at, half), :] = pack[:half, :]
        out_ref[pl.ds(states + at, half), :] = pack[half:per, :]


def norm_kernel(where_ref, lens_ref, tok_ref, cot_ref, gain_ref, bias_ref, low_ref, normed_ref, inv_ref, cotm_ref, *, length, seqs):
    block = pl.program_id(0)
    normed, inv_scale = layer_norm(tok_ref[...].astype(F32))
    normed_ref[...] = normed
    inv_ref[...] = jnp.broadcast_to(inv_scale, inv_ref.shape)
    low_ref[...] = (normed * gain_ref[...] + bias_ref[...]).astype(BF16)
    rows, width = tok_ref.shape
    per_block = rows // length
    for s in range(per_block):
        span = slice(s * length, (s + 1) * length)
        left = lens_ref[where_ref[1] * seqs + block * per_block + s] - where_ref[0] * length
        live = lax.broadcasted_iota(jnp.int32, (length, width), 0) < left
        cotm_ref[span, :] = jnp.where(live, cot_ref[span, :].astype(F32), 0.0).astype(BF16)


def drive_kernel(where_ref, low_ref, a0, a1, a2, a3, drive_ref, ends_ref, powers_ref, in_t, weigh, gam, *, length):
    block = pl.program_id(0)
    packs = (a0, a1, a2, a3)
    states = in_t.shape[0] // 2

    @pl.when(block == 0)
    def _():
        assemble_input(packs, where_ref[2], in_t)
        dr, di, gain = read_params(packs, a0.shape[0] - PARAM_ROWS)
        fill_powers(dr, di, True, 0, weigh)
        gam[...] = jnp.concatenate([gain, gain], axis=1)
        lr, li = cmul(weigh[0, :1, :], weigh[1, :1, :], dr, di)
        powers_ref[...] = jnp.zeros(powers_ref.shape, F32)
        powers_ref[0:1, :] = jnp.concatenate([lr, li], axis=1)
        powers_ref[1:2, :] = jnp.concatenate(cmul(lr, li, lr, li), axis=1)

    drive_ref[...] = dot_nt(low_ref[...], in_t[...]) * gam[...]
    per_block = low_ref.shape[0] // length
    for s in range(per_block):
        er = ei = jnp.zeros((TILE, states), F32)
        for n in range(length // TILE):
            at = s * length + n * TILE
            mr, mi = cmul(
                weigh[0, n * TILE : (n + 1) * TILE, :],
                weigh[1, n * TILE : (n + 1) * TILE, :],
                drive_ref[at : at + TILE, :states],
                drive_ref[at : at + TILE, states:],
            )
            er, ei = er + mr, ei + mi
        ends_ref[pl.ds(block * per_block + s, 1), :states] = jnp.sum(er, axis=0, keepdims=True)
        ends_ref[pl.ds(block * per_block + s, 1), states:] = jnp.sum(ei, axis=0, keepdims=True)


def scan_kernel(drive_ref, a0, a1, a2, a3, local_ref, step, *, length):
    @pl.when(pl.program_id(0) == 0)
    def _():
        dr, di, _ = read_params((a0, a1, a2, a3), a0.shape[0] - PARAM_ROWS)
        fill_steps(dr, di, False, step)

    scan_block(drive_ref, local_ref, step, length, False, lambda *_: None)


def hidden_kernel(where_ref, cotm_ref, b0, b1, b2, b3, hg_ref, *, per_s):
    shard = where_ref[2]
    per_f = hg_ref.shape[1] // TENSOR
    for k, pack in enumerate((b0, b1, b2, b3)):
        at = pl.multiple_of((shard ^ k) * per_f, per_f)
        hg_ref[:, pl.ds(at, per_f)] = dot_nt(cotm_ref[...], pack[2 * per_s :, :]).astype(BF16)


def middle_kernel(where_ref, *refs, length, ways):
    far_refs, refs = refs[: ways - 1], refs[ways - 1 :]
    beside_ref, powers_ref, local_ref, normed_ref, hg_ref, cotm_ref, a0, a1, a2, a3 = refs[:10]
    gain_ref, bias_ref, skip_ref, b0, b1, b2, b3, g0, g1, g2, g3 = refs[10:21]
    state_ref, back_ref, backends_ref, ylow_ref, hid_ref, own_ref, sent_ref = refs[21:28]
    c_all, ug_all, step, full, carry, act_ref, ul, eback, acc_out, acc_down, acc_ug, sems = refs[28:]
    block = pl.program_id(0)
    place, core, shard = where_ref[0], where_ref[1], where_ref[2]
    states = c_all.shape[0] // 2
    rows, width = normed_ref.shape
    per_block = rows // length
    per_s = states // TENSOR
    per_f = hid_ref.shape[1] // TENSOR

    @pl.when(block == 0)
    def _():
        copies = []
        for k, (pack, gates) in enumerate(((b0, g0), (b1, g1), (b2, g2), (b3, g3))):
            t = shard ^ k
            moves = (
                (pack.at[pl.ds(0, per_s), :], c_all.at[pl.ds(pl.multiple_of(t * per_s, per_s), per_s), :]),
                (pack.at[pl.ds(per_s, per_s), :], c_all.at[pl.ds(pl.multiple_of(states + t * per_s, per_s), per_s), :]),
                (gates, ug_all.at[:, pl.ds(pl.multiple_of(t * 2 * per_f, 2 * per_f), 2 * per_f)]),
            )
            for n, (src, dst) in enumerate(moves):
                copies.append(pltpu.make_async_copy(src, dst, sems.at[k, n]))
        for copy in copies:
            copy.start()
        dr, di, _ = read_params((a0, a1, a2, a3), a0.shape[0] - PARAM_ROWS)
        fill_powers(dr, di, False, 1, full)
        incoming(far_refs, beside_ref, place % 2, powers_ref, False, carry)
        fill_steps(dr, di, True, step)
        acc_out[...] = jnp.zeros(acc_out.shape, F32)
        acc_down[...] = jnp.zeros(acc_down.shape, F32)
        acc_ug[...] = jnp.zeros(acc_ug.shape, F32)
        for copy in copies:
            copy.wait()

    for s in range(per_block):
        seq = block * per_block + s
        span = slice(s * length, (s + 1) * length)
        sr = carry[pl.ds(seq, 1), :states]
        si = carry[pl.ds(seq, 1), states:]
        mr, mi = cmul(full[0], full[1], sr, si)
        state_ref[span, :states] = (local_ref[span, :states] + mr).astype(BF16)
        state_ref[span, states:] = (-(local_ref[span, states:] + mi)).astype(BF16)
    skip = skip_ref[...]
    y = dot(state_ref[...], c_all[...]) + (normed_ref[...] * (gain_ref[...] * skip) + bias_ref[...] * skip)
    square = y * y
    th = jnp.tanh(GELU_K * y * (1.0 + 0.044715 * square))
    act_ref[...] = (0.5 * y * (1.0 + th)).astype(BF16)
    slope = 0.5 * (1.0 + th) + (0.5 * GELU_K) * y * (1.0 - th * th) * (1.0 + (3 * 0.044715) * square)
    act = act_ref[...]
    cotm = cotm_ref[...]
    for t in range(TENSOR):
        both = dot(act, ug_all[:, 2 * per_f * t : 2 * per_f * (t + 1)])
        up = both[:, :per_f]
        sig = jax.nn.sigmoid(both[:, per_f:])
        hid_ref[:, per_f * t : per_f * (t + 1)] = (up * sig).astype(BF16)
        up_grad = hg_ref[:, per_f * t : per_f * (t + 1)].astype(F32) * sig
        ul[:, 2 * per_f * t : 2 * per_f * t + per_f] = up_grad.astype(BF16)
        ul[:, 2 * per_f * t + per_f : 2 * per_f * (t + 1)] = (up_grad * up * (1.0 - sig)).astype(BF16)
    y_grad = dot_nt(ul[...], ug_all[...]) * slope
    ylow_ref[...] = y_grad.astype(BF16)
    eback[...] = dot_nt(ylow_ref[...], c_all[...])

    def finish(s, r, i):
        backends_ref[pl.ds(block * per_block + s, 1), :states] = r
        backends_ref[pl.ds(block * per_block + s, 1), states:] = i

    side = shard // 2
    acc_ug[...] += dot_tn(act, ul[:, pl.ds(pl.multiple_of(side * 4 * per_f, 4 * per_f), 4 * per_f)])
    acc_down[...] += dot_tn(hid_ref[:, pl.ds(pl.multiple_of(side * 2 * per_f, 2 * per_f), 2 * per_f)], cotm)
    for k in range(2):
        cols = state_ref[:, pl.ds(pl.multiple_of(k * states + side * 2 * per_s, 2 * per_s), 2 * per_s)]
        acc_out[k * 2 * per_s : (k + 1) * 2 * per_s, :] += dot_tn(cols, ylow_ref[...])
    scan_block(eback, back_ref, step, length, True, finish)

    @pl.when(block == pl.num_programs(0) - 1)
    def _():
        for n, ref in ((core, own_ref), (1 - core, sent_ref)):
            for k in range(2):
                part = acc_out[pl.ds(pl.multiple_of(2 * per_s * k + n * per_s, per_s), per_s), :]
                ref[k * per_s : (k + 1) * per_s, :] = part.astype(ref.dtype)
            part = acc_down[pl.ds(pl.multiple_of(n * per_f, per_f), per_f), :]
            ref[2 * per_s : 2 * per_s + per_f, :] = part.astype(ref.dtype)
            part = acc_ug[:, pl.ds(pl.multiple_of(n * 2 * per_f, 2 * per_f), 2 * per_f)]
            ref[2 * per_s + per_f : 2 * per_s + per_f + width, :] = part.astype(ref.dtype)


def down_kernel(where_ref, lens_ref, tok_ref, hid_ref, b0, b1, b2, b3, out_ref, down_all, *, length, per_s, seqs):
    block = pl.program_id(0)
    shard = where_ref[2]
    rows, width = tok_ref.shape
    per_block = rows // length
    per_f = down_all.shape[0] // TENSOR

    @pl.when(block == 0)
    def _():
        for k, pack in enumerate((b0, b1, b2, b3)):
            down_all[pl.ds(pl.multiple_of((shard ^ k) * per_f, per_f), per_f), :] = pack[2 * per_s :, :]

    added = dot(hid_ref[...], down_all[...])
    for s in range(per_block):
        span = slice(s * length, (s + 1) * length)
        left = lens_ref[where_ref[1] * seqs + block * per_block + s] - where_ref[0] * length
        live = lax.broadcasted_iota(jnp.int32, (length, width), 0) < left
        out_ref[span, :] = jnp.where(live, tok_ref[span, :].astype(F32) + added[span, :], 0.0).astype(BF16)


def last_kernel(where_ref, *refs, length, ways):
    far_refs, refs = refs[: ways - 1], refs[ways - 1 :]
    beside_ref, powers_ref, low_ref, normed_ref, inv_ref, cotm_ref, back_ref, state_ref, ylow_ref = refs[:9]
    a0, a1, a2, a3, gain_ref, bias_ref, skip_ref, grad_ref, own_ref, sent_ref = refs[9:19]
    in_t, full, carry, gam, dlow, in_grad, lam_grad, vec_grad = refs[19:]
    block = pl.program_id(0)
    place, core, shard = where_ref[0], where_ref[1], where_ref[2]
    states = in_t.shape[0] // 2
    rows, width = low_ref.shape
    per_block = rows // length
    per_s = states // TENSOR
    packs = (a0, a1, a2, a3)

    @pl.when(block == 0)
    def _():
        assemble_input(packs, shard, in_t)
        dr, di, gain = read_params(packs, a0.shape[0] - PARAM_ROWS)
        fill_powers(dr, di, True, 1, full)
        incoming(far_refs, beside_ref, place % 2, powers_ref, True, carry)
        gam[...] = jnp.concatenate([gain, -gain], axis=1)
        in_grad[...] = jnp.zeros(in_grad.shape, F32)
        lam_grad[...] = jnp.zeros(lam_grad.shape, F32)
        vec_grad[...] = jnp.zeros(vec_grad.shape, F32)

    for s in range(per_block):
        seq = block * per_block + s
        span = slice(s * length, (s + 1) * length)
        sr = carry[pl.ds(seq, 1), :states]
        si = carry[pl.ds(seq, 1), states:]
        mr, mi = cmul(full[0], full[1], sr, si)
        gr = back_ref[span, :states] + mr
        gi = back_ref[span, states:] + mi
        dlow[span, :states] = (gr * gam[:, :states]).astype(BF16)
        dlow[span, states:] = (gi * gam[:, states:]).astype(BF16)
        nr = jnp.concatenate([gr[1:], sr], axis=0)
        ni = jnp.concatenate([gi[1:], si], axis=0)
        hr = state_ref[span, :states].astype(F32)
        hi = state_ref[span, states:].astype(F32)
        lam_grad[:, :states] += jnp.sum(nr * hr + ni * hi, axis=0, keepdims=True)
        lam_grad[:, states:] += jnp.sum(nr * hi - ni * hr, axis=0, keepdims=True)
    normed = normed_ref[...]
    ylow = ylow_ref[...].astype(F32)
    u_grad = dot(dlow[...], in_t[...]) + ylow * skip_ref[...]
    vec_grad[0:1, :] += jnp.sum(u_grad * normed, axis=0, keepdims=True)
    vec_grad[1:2, :] += jnp.sum(u_grad, axis=0, keepdims=True)
    vec_grad[2:3, :] += jnp.sum(ylow * (normed * gain_ref[...] + bias_ref[...]), axis=0, keepdims=True)
    scaled = u_grad * gain_ref[...]
    grad = (
        scaled
        - jnp.mean(scaled, axis=-1, keepdims=True)
        - normed * jnp.mean(scaled * normed, axis=-1, keepdims=True)
    )
    grad_ref[...] = (cotm_ref[...].astype(F32) + inv_ref[:, :1] * grad).astype(BF16)
    at = pl.multiple_of((shard // 2) * 2 * per_s, 2 * per_s)
    for k in range(2):
        cols = dlow[:, pl.ds(k * states + at, 2 * per_s)]
        in_grad[2 * per_s * k : 2 * per_s * (k + 1), :] += dot_tn(cols, low_ref[...])

    @pl.when(block == pl.num_programs(0) - 1)
    def _():
        small = jnp.concatenate(
            [vec_grad[:3, :], lam_grad[...], jnp.zeros((PARAM_ROWS - 4, width), F32)], axis=0
        ).astype(BF16)
        for n, ref in ((core, own_ref), (1 - core, sent_ref)):
            for k in range(2):
                part = in_grad[pl.ds(pl.multiple_of(2 * per_s * k + n * per_s, per_s), per_s), :]
                ref[k * per_s : (k + 1) * per_s, :] = part.astype(BF16)
            ref[2 * per_s :, :] = small


def fold_kernel(where_ref, own_ref, other_ref, keep_ref, send_ref):
    half = keep_ref.shape[0]
    odd = where_ref[0] % 2
    at = pl.multiple_of(odd * half, 16)
    keep_ref[...] = own_ref[pl.ds(at, half), :] + other_ref[pl.ds(at, half), :].astype(F32)
    at = pl.multiple_of((1 - odd) * half, 16)
    send_ref[...] = (own_ref[pl.ds(at, half), :] + other_ref[pl.ds(at, half), :].astype(F32)).astype(BF16)


def deal_kernel(where_ref, own_ref, other_ref, keep_ref, *send_refs):
    rows = keep_ref.shape[0]
    for k, ref in enumerate((keep_ref,) + send_refs):
        at = pl.multiple_of(((where_ref[0] // 2) ^ k) * rows, 16)
        ref[...] = (own_ref[pl.ds(at, rows), :] + other_ref[pl.ds(at, rows), :].astype(F32)).astype(ref.dtype)


def unpack_kernel(where_ref, *refs, ways):
    mine, other = refs[:ways], refs[ways : 2 * ways]
    real_ref, imag_ref, up_ref, gate_ref, down_ref, total = refs[2 * ways :]
    place = where_ref[0]
    rows = mine[0].shape[0]
    for k in range(ways):
        at = ((place // 2) ^ k) * rows
        total[pl.ds(pl.multiple_of((place % 2) * ways * rows + at, 16), rows), :] = mine[k][...].astype(F32)
        total[pl.ds(pl.multiple_of((1 - place % 2) * ways * rows + at, 16), rows), :] = other[k][...].astype(F32)
    per_s = real_ref.shape[0]
    per_f = down_ref.shape[0]
    real_ref[...] = total[:per_s, :]
    imag_ref[...] = total[per_s : 2 * per_s, :]
    down_ref[...] = total[2 * per_s : 2 * per_s + per_f, :]
    last = 2 * per_s + per_f + up_ref.shape[0]
    up_ref[...] = total[2 * per_s + per_f : last, :per_f]
    gate_ref[...] = total[2 * per_s + per_f : last, per_f:]


def whole(shape):
    return pl.BlockSpec(shape, lambda *_: (0,) * len(shape))


def near(value):
    return pltpu.with_memory_space_constraint(value, pltpu.VMEM)


def far(value):
    return pltpu.with_memory_space_constraint(value, pltpu.HBM)


def call(kernel, grid, prefetch, in_specs, out_specs, out_shape, scratch, cost, vmem):
    return pl.pallas_call(
        kernel,
        grid_spec=pltpu.PrefetchScalarGridSpec(
            num_scalar_prefetch=prefetch,
            grid=grid,
            in_specs=in_specs,
            out_specs=out_specs,
            scratch_shapes=scratch,
        ),
        out_shape=out_shape,
        compiler_params=pltpu.CompilerParams(vmem_limit_bytes=vmem * MIB),
        cost_estimate=pl.CostEstimate(flops=1, bytes_accessed=int(cost * 3.3e6), transcendentals=0),
    )


def split_low(value):
    high = lax.reduce_precision(value, 8, 7)
    middle = lax.reduce_precision(value - high, 8, 7)
    return high, middle, value - high - middle


def core_swap(value):
    return lax.ppermute(value, "tensor", [(t, t ^ 1) for t in range(TENSOR)])


def side_swap(value):
    return lax.ppermute(value, "tensor", [(t, t ^ 2) for t in range(TENSOR)])


def gather_tensor(own, *first):
    across = after(side_swap(own), *first)
    return own, core_swap(own), across, core_swap(across)


def after(value, *first):
    return lax.optimization_barrier((value,) + first)[0]


def flip_dp(value, bits, groups):
    return lax.ppermute(value, "dp", [(i, i ^ bits) for i in range(groups)])


def shift_dp(value, by, groups):
    return lax.ppermute(value, "dp", [(i, i + by) for i in range(groups) if 0 <= i + by < groups])


def shards(
    tokens,
    cotangent,
    ln_gain,
    ln_bias,
    skip_gain,
    in_real,
    in_imag,
    out_real,
    out_imag,
    nu_log,
    theta_log,
    gamma_log,
    up_weight,
    gate_weight,
    down_weight,
    lengths,
    *,
    groups,
):
    seqs, length, width = tokens.shape
    per_s = in_real.shape[1]
    per_f = up_weight.shape[1]
    states = per_s * TENSOR
    own_seqs = seqs // 2
    rows = own_seqs * length
    blocks = rows // BLOCK
    place = lax.axis_index("dp").astype(jnp.int32)
    shard = lax.axis_index("tensor").astype(jnp.int32)
    core = shard % 2
    where = jnp.stack([place, core, shard])

    modulus = jnp.exp(-jnp.exp(nu_log))
    angle = jnp.exp(theta_log)
    gain = jnp.exp(gamma_log)
    parts = [split_low(v) for v in (modulus * jnp.cos(angle), modulus * jnp.sin(angle), gain)]
    table = jnp.stack([parts[v][k] for k in range(3) for v in range(3)])
    placed = jnp.where(
        lax.broadcasted_iota(jnp.int32, (9, width), 1) // per_s == shard, jnp.tile(table, (1, width // per_s)), 0.0
    )
    pack_a = jnp.concatenate(
        [in_real.T, in_imag.T, placed.astype(BF16), jnp.zeros((PARAM_ROWS - 9, width), BF16)], axis=0
    )
    pack_b = after(jnp.concatenate([out_real, out_imag, down_weight], axis=0), pack_a)
    pack_g = after(jnp.concatenate([up_weight, gate_weight], axis=1), pack_b)
    tok_rows = tokens.reshape(seqs * length, width)
    cot_rows = cotangent.reshape(seqs * length, width)
    row = lambda v: v.reshape(1, width)
    gain_row, bias_row, skip_row = row(ln_gain), row(ln_bias), row(skip_gain)
    half_spec = pl.BlockSpec((BLOCK, width), lambda b, w, *_: (w[1] * blocks + b, 0))
    row_spec = lambda lanes: pl.BlockSpec((BLOCK, lanes), lambda b, *_: (b, 0))
    a_spec = [whole(pack_a.shape)] * TENSOR
    b_spec = [whole(pack_b.shape)] * TENSOR
    any_spec = [pl.BlockSpec(memory_space=pl.ANY)] * TENSOR
    vec_spec = whole((1, width))
    shape = jax.ShapeDtypeStruct
    kept = pltpu.VMEM
    lanes = 2 * states
    units = TENSOR * per_f

    low, normed, inv, cot_m = call(
        functools.partial(norm_kernel, length=length, seqs=own_seqs),
        (blocks,),
        2,
        [half_spec, half_spec, vec_spec, vec_spec],
        [row_spec(width), row_spec(width), row_spec(128), row_spec(width)],
        [kept((rows, width), BF16), kept((rows, width), F32), kept((rows, 128), F32), kept((rows, width), BF16)],
        [],
        3,
        8,
    )(where, lengths, far(tok_rows), far(cot_rows), far(gain_row), far(bias_row))

    packs_a = gather_tensor(pack_a, low)
    near_a = tuple(map(near, packs_a))
    drive, ends, powers = call(
        functools.partial(drive_kernel, length=length),
        (blocks,),
        1,
        [row_spec(width)] + a_spec,
        [row_spec(lanes), whole((own_seqs, lanes)), whole((TILE, lanes))],
        [kept((rows, lanes), F32), shape((own_seqs, lanes), F32), shape((TILE, lanes), F32)],
        [
            pltpu.VMEM((lanes, width), BF16),
            pltpu.VMEM((2, length, states), F32),
            pltpu.VMEM((1, lanes), F32),
        ],
        4,
        8,
    )(where, near(low), *near_a)

    local = call(
        functools.partial(scan_kernel, length=length),
        (blocks,),
        0,
        [row_spec(lanes)] + a_spec,
        row_spec(lanes),
        kept((rows, lanes), F32),
        [pltpu.VMEM((4, 2, TILE, states), F32)],
        4,
        8,
    )(near(drive), *near_a)
    ways = groups // 2
    end_spec = whole((own_seqs, lanes))
    power_spec = whole((TILE, lanes))

    def exchange(mine, backwards, beside_work):
        beside = after(flip_dp(mine, 1, groups), beside_work)
        both = call(
            functools.partial(pair_kernel, backwards=backwards),
            (1,),
            1,
            [end_spec, end_spec, power_spec],
            end_spec,
            shape((own_seqs, lanes), F32),
            [],
            1,
            2,
        )(where, mine, beside, powers)
        return [shift_dp(both, (-2 if backwards else 2) * k, groups) for k in range(1, ways)], beside, both

    far_ends, beside_ends, pair_ends = exchange(ends, False, local)
    packs_b = gather_tensor(pack_b, beside_ends)
    near_b = tuple(map(near, packs_b))

    hid_grad = call(
        functools.partial(hidden_kernel, per_s=per_s),
        (blocks,),
        1,
        [row_spec(width)] + b_spec,
        row_spec(units),
        kept((rows, units), BF16),
        [],
        3,
        10,
    )(where, near(after(cot_m, pair_ends)), *near_b)

    packs_g = gather_tensor(pack_g, hid_grad, *far_ends)
    pack_rows = -(-(2 * per_s + per_f + width) // (16 * groups)) * 16 * groups
    state, back, back_ends, y_low, hid, own_b, sent_b = call(
        functools.partial(middle_kernel, length=length, ways=ways),
        (blocks,),
        1,
        [end_spec] * ways
        + [power_spec, row_spec(lanes), row_spec(width), row_spec(units), row_spec(width)]
        + a_spec
        + [vec_spec] * 3
        + any_spec
        + any_spec,
        [
            row_spec(lanes),
            row_spec(lanes),
            end_spec,
            row_spec(width),
            row_spec(units),
            whole((pack_rows, width)),
            whole((pack_rows, width)),
        ],
        [
            kept((rows, lanes), BF16),
            kept((rows, lanes), F32),
            shape((own_seqs, lanes), F32),
            kept((rows, width), BF16),
            kept((rows, units), BF16),
            shape((pack_rows, width), F32),
            shape((pack_rows, width), BF16),
        ],
        [
            pltpu.VMEM((lanes, width), BF16),
            pltpu.VMEM((width, 2 * units), BF16),
            pltpu.VMEM((4, 2, TILE, states), F32),
            pltpu.VMEM((2, length, states), F32),
            pltpu.VMEM((own_seqs, lanes), F32),
            pltpu.VMEM((BLOCK, width), BF16),
            pltpu.VMEM((BLOCK, 2 * units), BF16),
            pltpu.VMEM((BLOCK, lanes), F32),
            pltpu.VMEM((states, width), F32),
            pltpu.VMEM((2 * per_f, width), F32),
            pltpu.VMEM((width, 4 * per_f), F32),
            pltpu.SemaphoreType.DMA((TENSOR, 3)),
        ],
        21,
        20,
    )(
        where,
        *far_ends,
        beside_ends,
        powers,
        *map(near, (local, normed, hid_grad, cot_m)),
        *near_a,
        gain_row,
        bias_row,
        skip_row,
        *near_b,
        *packs_g,
    )

    half, part = pack_rows // 2, pack_rows // groups
    keep_b, send_b = call(
        fold_kernel,
        (1,),
        1,
        [whole((pack_rows, width))] * 2,
        [whole((half, width))] * 2,
        [shape((half, width), F32), shape((half, width), BF16)],
        [],
        2,
        8,
    )(where, own_b, core_swap(sent_b))
    out_own = call(
        functools.partial(down_kernel, length=length, per_s=per_s, seqs=own_seqs),
        (blocks,),
        2,
        [half_spec, row_spec(units)] + b_spec,
        row_spec(width),
        shape((rows, width), BF16),
        [pltpu.VMEM((units, width), BF16)],
        5,
        8,
    )(where, lengths, far(tok_rows), near(after(hid, send_b)), *near_b)
    far_back, beside_back, pair_back = exchange(back_ends, True, out_own)
    half_b = flip_dp(after(send_b, pair_back), 1, groups)

    dealt = call(
        deal_kernel,
        (1,),
        1,
        [whole((half, width))] * 2,
        [whole((part, width))] * ways,
        [shape((part, width), F32)] + [shape((part, width), BF16)] * (ways - 1),
        [],
        2,
        8,
    )(where, after(keep_b, *far_back), half_b)

    grad_own, own_a, sent_a = call(
        functools.partial(last_kernel, length=length, ways=ways),
        (blocks,),
        1,
        [end_spec] * ways
        + [
            power_spec,
            row_spec(width),
            row_spec(width),
            row_spec(128),
            row_spec(width),
            row_spec(lanes),
            row_spec(lanes),
            row_spec(width),
        ]
        + a_spec
        + [vec_spec] * 3,
        [row_spec(width), whole(pack_a.shape), whole(pack_a.shape)],
        [shape((rows, width), BF16), shape(pack_a.shape, BF16), shape(pack_a.shape, BF16)],
        [
            pltpu.VMEM((lanes, width), BF16),
            pltpu.VMEM((2, length, states), F32),
            pltpu.VMEM((own_seqs, lanes), F32),
            pltpu.VMEM((1, lanes), F32),
            pltpu.VMEM((BLOCK, lanes), BF16),
            pltpu.VMEM((states, width), F32),
            pltpu.VMEM((1, lanes), F32),
            pltpu.VMEM((TILE, width), F32),
        ],
        8,
        14,
    )(
        where,
        *far_back,
        after(beside_back, dealt[0]),
        powers,
        *map(near, (low, normed, inv, cot_m, back, state, y_low)),
        *near_a,
        gain_row,
        bias_row,
        skip_row,
    )

    mine_b = dealt[0]
    for k in range(1, ways):
        mine_b = mine_b + flip_dp(dealt[k], 2 * k, groups).astype(F32)
    mine_b = mine_b.astype(BF16)

    grads_a = own_a.astype(F32) + core_swap(after(sent_a, mine_b)).astype(F32)
    bit = 1
    while bit < groups:
        low_a = grads_a.astype(BF16)
        grads_a = low_a.astype(F32) + flip_dp(low_a, bit, groups).astype(F32)
        bit *= 2

    gathered = [mine_b] + [flip_dp(mine_b, 2 * k, groups) for k in range(1, ways)]
    beside = [flip_dp(piece, 1, groups) for piece in gathered]

    out_other = core_swap(out_own)
    grad_other = core_swap(after(grad_own, mine_b))

    def in_order(mine, other):
        first = core == 0
        return jnp.concatenate([jnp.where(first, mine, other), jnp.where(first, other, mine)], axis=0).reshape(
            seqs, length, width
        )

    block_out = in_order(out_own, out_other)
    input_grad = in_order(grad_own, grad_other).astype(F32)
    beside[-1] = after(beside[-1], block_out, input_grad)

    out_real_grad, out_imag_grad, up_grad, gate_grad, down_grad = call(
        functools.partial(unpack_kernel, ways=ways),
        (1,),
        1,
        [whole((part, width))] * groups,
        [whole((per_s, width))] * 2 + [whole((width, per_f))] * 2 + [whole((per_f, width))],
        [shape((per_s, width), F32)] * 2 + [shape((width, per_f), F32)] * 2 + [shape((per_f, width), F32)],
        [pltpu.VMEM((pack_rows, width), F32)],
        2,
        8,
    )(where, *gathered, *beside)

    in_real_grad = grads_a[:per_s].T
    in_imag_grad = grads_a[per_s : 2 * per_s].T
    small = grads_a[2 * per_s :]
    lam_real = lax.dynamic_slice_in_dim(small[3, :states], shard * per_s, per_s)
    lam_imag = lax.dynamic_slice_in_dim(small[3, states:], shard * per_s, per_s)
    cos, sin = jnp.cos(angle), jnp.sin(angle)
    nu_grad = -jnp.exp(nu_log) * modulus * (lam_real * cos + lam_imag * sin)
    theta_grad = angle * modulus * (lam_imag * cos - lam_real * sin)
    gamma_grad = jnp.sum(in_real.astype(F32) * in_real_grad + in_imag.astype(F32) * in_imag_grad, axis=0)
    return (
        block_out,
        input_grad,
        small[0],
        small[1],
        small[2],
        in_real_grad,
        in_imag_grad,
        out_real_grad,
        out_imag_grad,
        nu_grad,
        theta_grad,
        gamma_grad,
        up_grad,
        gate_grad,
        down_grad,
    )


def solution(mesh):
    rows = P(None, "dp", None)
    columns = P(None, "tensor")
    lines = P("tensor", None)
    vector = P("tensor")
    in_specs = (rows, rows, P(), P(), P(), columns, columns, lines, lines, vector, vector, vector, columns, columns, lines, P())
    out_specs = (rows, rows, P(), P(), P(), columns, columns, lines, lines, vector, vector, vector, columns, columns, lines)
    return jax.shard_map(
        functools.partial(shards, groups=mesh.shape["dp"]),
        mesh=mesh,
        in_specs=in_specs,
        out_specs=out_specs,
        check_vma=False,
    )
```

```python
import functools
import math

import jax
import jax.numpy as jnp
from jax import lax
from jax.experimental import pallas as pl
from jax.experimental.pallas import tpu as pltpu
from jax.sharding import PartitionSpec as P

EPSILON = 1e-05
TENSOR = 4
TILE = 8
BLOCK = 256
PARAM_ROWS = 16
F32 = jnp.float32
BF16 = jnp.bfloat16
GELU_K = math.sqrt(2.0 / math.pi)
MIB = 1024 * 1024


def dot(left, right):
    return jnp.dot(left, right, preferred_element_type=F32)


def dot_nt(left, right):
    return lax.dot_general(left, right, (((1,), (1,)), ((), ())), preferred_element_type=F32)


def dot_tn(left, right):
    return lax.dot_general(left, right, (((0,), (0,)), ((), ())), preferred_element_type=F32)


def layer_norm(rows):
    centre = jnp.mean(rows, axis=-1, keepdims=True)
    shifted = rows - centre
    variance = jnp.mean(shifted * shifted, axis=-1, keepdims=True)
    inv_scale = lax.rsqrt(variance + EPSILON)
    return shifted * inv_scale, inv_scale


def cmul(ar, ai, br, bi):
    return ar * br - ai * bi, ar * bi + ai * br


def read_params(packs, row):
    total = None
    for pack in packs:
        rows = pack[row : row + PARAM_ROWS, :].astype(F32)
        total = rows if total is None else total + rows
    states = total.shape[1] // 2
    at = lambda k: total[k : k + 1, :states] + total[k + 3 : k + 4, :states] + total[k + 6 : k + 7, :states]
    return at(0), at(1), at(2)


def powers_of(decay_real, decay_imag, exponent):
    out_r = jnp.ones(exponent.shape, F32)
    out_i = jnp.zeros(exponent.shape, F32)
    br, bi = decay_real, decay_imag
    for bit in range(4):
        mr, mi = cmul(out_r, out_i, br, bi)
        on = ((exponent >> bit) & 1) == 1
        out_r = jnp.where(on, mr, out_r)
        out_i = jnp.where(on, mi, out_i)
        br, bi = cmul(br, bi, br, bi)
    return out_r, out_i


def fill_steps(decay_real, decay_imag, backwards, step_ref):
    states = decay_real.shape[1]
    row = lax.broadcasted_iota(jnp.int32, (TILE, states), 0)
    if backwards:
        row = TILE - 1 - row
    zero = jnp.zeros((TILE, states), F32)
    for k, shift in enumerate((1, 2, 4)):
        pr, pi = powers_of(decay_real, decay_imag, jnp.full((TILE, states), shift, jnp.int32))
        step_ref[k, 0] = jnp.where(row >= shift, pr, zero)
        step_ref[k, 1] = jnp.where(row >= shift, pi, zero)
    step_ref[3, 0], step_ref[3, 1] = powers_of(decay_real, decay_imag, row + 1)


def fill_powers(decay_real, decay_imag, backwards, first, full_ref):
    states = decay_real.shape[1]
    row = lax.broadcasted_iota(jnp.int32, (TILE, states), 0)
    if backwards:
        row = TILE - 1 - row
    pr, pi = powers_of(decay_real, decay_imag, row + first)
    er, ei = powers_of(decay_real, decay_imag, jnp.full((TILE, states), TILE, jnp.int32))
    tiles = full_ref.shape[1] // TILE
    for n in range(tiles):
        at = (tiles - 1 - n if backwards else n) * TILE
        full_ref[0, at : at + TILE, :] = pr
        full_ref[1, at : at + TILE, :] = pi
        pr, pi = cmul(pr, pi, er, ei)


def scan_block(drive_ref, out_ref, step_ref, length, backwards, finish):
    rows, lanes = drive_ref.shape
    states = lanes // 2
    tiles = length // TILE
    table = [(step_ref[k, 0], step_ref[k, 1]) for k in range(4)]
    edge = 0 if backwards else TILE - 1
    for s in range(rows // length):
        cr = ci = None
        for n in range(tiles):
            at = s * length + (tiles - 1 - n if backwards else n) * TILE
            hr = drive_ref[at : at + TILE, :states]
            hi = drive_ref[at : at + TILE, states:]
            for k, shift in enumerate((1, 2, 4)):
                turn = TILE - shift if backwards else shift
                sr = pltpu.roll(hr, turn, 0)
                si = pltpu.roll(hi, turn, 0)
                mr, mi = cmul(table[k][0], table[k][1], sr, si)
                hr, hi = hr + mr, hi + mi
            if cr is not None:
                mr, mi = cmul(table[3][0], table[3][1], cr, ci)
                hr, hi = hr + mr, hi + mi
            out_ref[at : at + TILE, :states] = hr
            out_ref[at : at + TILE, states:] = hi
            cr, ci = hr[edge : edge + 1], hi[edge : edge + 1]
        finish(s, cr, ci)


def incoming(far_refs, beside_ref, odd, powers_ref, backwards, out_ref):
    states = out_ref.shape[1] // 2
    early, late = slice(0, states), slice(states, None)
    sr, si = far_refs[0][:, early], far_refs[0][:, late]
    for k in range(1, len(far_refs)):
        row = slice(4 + k, 5 + k)
        mr, mi = cmul(powers_ref[row, early], powers_ref[row, late], far_refs[k][:, early], far_refs[k][:, late])
        sr, si = sr + mr, si + mi
    mr, mi = cmul(powers_ref[0:1, early], powers_ref[0:1, late], sr, si)
    second = odd == (0 if backwards else 1)
    out_ref[:, early] = jnp.where(second, mr + beside_ref[:, early], sr)
    out_ref[:, late] = jnp.where(second, mi + beside_ref[:, late], si)


def join_kernel(mine_ref, other_ref, powers_ref, out_ref, *, row):
    states = out_ref.shape[1] // 2
    early, late = slice(0, states), slice(states, None)
    row = slice(row, row + 1)
    mr, mi = cmul(powers_ref[row, early], powers_ref[row, late], other_ref[:, early], other_ref[:, late])
    out_ref[:, early] = mine_ref[:, early] + mr
    out_ref[:, late] = mine_ref[:, late] + mi


def pair_kernel(where_ref, mine_ref, other_ref, powers_ref, out_ref, *, backwards):
    states = out_ref.shape[1] // 2
    second = where_ref[0] % 2 == (0 if backwards else 1)
    lr, li = powers_ref[0:1, :states], powers_ref[0:1, states:]
    pick = lambda first, part: jnp.where(second == first, other_ref[:, part], mine_ref[:, part])
    early, late = slice(0, states), slice(states, None)
    mr, mi = cmul(lr, li, pick(True, early), pick(True, late))
    out_ref[:, :states] = mr + pick(False, early)
    out_ref[:, states:] = mi + pick(False, late)


def assemble_input(packs, shard, out_ref):
    per = packs[0].shape[0] - PARAM_ROWS
    half = per // 2
    states = out_ref.shape[0] // 2
    for k, pack in enumerate(packs):
        at = pl.multiple_of((shard ^ k) * half, half)
        out_ref[pl.ds(at, half), :] = pack[:half, :]
        out_ref[pl.ds(states + at, half), :] = pack[half:per, :]


def input_pack_kernel(where_ref, in_real, in_imag, nu, theta, gamma, a_ref):
    per_s, width = in_real.shape
    a_ref[:per_s, :] = in_real[...]
    a_ref[per_s : 2 * per_s, :] = in_imag[...]
    modulus = jnp.exp(-jnp.exp(nu[...]))
    angle = jnp.exp(theta[...])
    rest = [modulus * jnp.cos(angle), modulus * jnp.sin(angle), jnp.exp(gamma[...])]
    rows = []
    for _ in range(3):
        for n in range(3):
            high = rest[n].astype(BF16).astype(F32)
            rows.append(high)
            rest[n] = rest[n] - high
    table = jnp.concatenate(rows + [jnp.zeros((PARAM_ROWS - 9, per_s), F32)], axis=0)
    table = jnp.concatenate([table] * (width // per_s), axis=1)
    here = lax.broadcasted_iota(jnp.int32, (PARAM_ROWS, width), 1) // per_s == where_ref[2]
    a_ref[2 * per_s :, :] = jnp.where(here, table, 0.0).astype(BF16)


def weight_pack_kernel(out_real, out_imag, up, gate, down, b_ref, g_ref):
    per_s, per_f = out_real.shape[0], down.shape[0]
    b_ref[:per_s, :] = out_real[...]
    b_ref[per_s : 2 * per_s, :] = out_imag[...]
    b_ref[2 * per_s :, :] = down[...]
    g_ref[:, :per_f] = up[...]
    g_ref[:, per_f:] = gate[...]


def norm_kernel(where_ref, lens_ref, tok_ref, cot_ref, gain_ref, bias_ref, low_ref, normed_ref, inv_ref, cotm_ref, *, length, seqs):
    normed, inv_scale = layer_norm(tok_ref[...].astype(F32))
    normed_ref[...] = normed
    inv_ref[...] = jnp.broadcast_to(inv_scale, inv_ref.shape)
    low_ref[...] = (normed * gain_ref[...] + bias_ref[...]).astype(BF16)
    block = pl.program_id(0)
    rows, width = cot_ref.shape
    per_block = rows // length
    for s in range(per_block):
        span = slice(s * length, (s + 1) * length)
        left = lens_ref[where_ref[1] * seqs + block * per_block + s] - where_ref[0] * length
        live = lax.broadcasted_iota(jnp.int32, (length, width), 0) < left
        cotm_ref[span, :] = jnp.where(live, cot_ref[span, :].astype(F32), 0.0).astype(BF16)


def drive_kernel(where_ref, low_ref, a0, a1, a2, a3, drive_ref, ends_ref, powers_ref, in_t, weigh, gam, *, length):
    block = pl.program_id(0)
    packs = (a0, a1, a2, a3)
    states = in_t.shape[0] // 2

    @pl.when(block == 0)
    def _():
        assemble_input(packs, where_ref[2], in_t)
        dr, di, gain = read_params(packs, a0.shape[0] - PARAM_ROWS)
        fill_powers(dr, di, True, 0, weigh)
        gam[...] = jnp.concatenate([gain, gain], axis=1)
        lr, li = cmul(weigh[0, :1, :], weigh[1, :1, :], dr, di)
        rows = [(lr, li)] + [cmul(lr, li, lr, li)]
        for _ in range(2):
            rows.append(cmul(*rows[-1], *rows[-1]))
        rows.append((jnp.ones_like(lr), jnp.zeros_like(lr)))
        for _ in range(3):
            rows.append(cmul(*cmul(*rows[-1], *rows[-1]), *rows[1]))
        for k, (lr, li) in enumerate(rows):
            powers_ref[k : k + 1, :] = jnp.concatenate([lr, li], axis=1)

    drive_ref[...] = dot_nt(low_ref[...], in_t[...]) * gam[...]
    per_block = low_ref.shape[0] // length
    for s in range(per_block):
        er = ei = jnp.zeros((TILE, states), F32)
        for n in range(length // TILE):
            at = s * length + n * TILE
            mr, mi = cmul(
                weigh[0, n * TILE : (n + 1) * TILE, :],
                weigh[1, n * TILE : (n + 1) * TILE, :],
                drive_ref[at : at + TILE, :states],
                drive_ref[at : at + TILE, states:],
            )
            er, ei = er + mr, ei + mi
        ends_ref[pl.ds(block * per_block + s, 1), :states] = jnp.sum(er, axis=0, keepdims=True)
        ends_ref[pl.ds(block * per_block + s, 1), states:] = jnp.sum(ei, axis=0, keepdims=True)


def scan_kernel(drive_ref, a0, a1, a2, a3, local_ref, step, *, length):
    @pl.when(pl.program_id(0) == 0)
    def _():
        dr, di, _ = read_params((a0, a1, a2, a3), a0.shape[0] - PARAM_ROWS)
        fill_steps(dr, di, False, step)

    scan_block(drive_ref, local_ref, step, length, False, lambda *_: None)


def hidden_kernel(where_ref, cotm_ref, b0, b1, b2, b3, hg_ref, *, per_s):
    shard = where_ref[2]
    per_f = hg_ref.shape[1] // TENSOR
    for k, pack in enumerate((b0, b1, b2, b3)):
        at = pl.multiple_of((shard ^ k) * per_f, per_f)
        hg_ref[:, pl.ds(at, per_f)] = dot_nt(cotm_ref[...], pack[2 * per_s :, :]).astype(BF16)


def middle_kernel(where_ref, *refs, length, levels):
    far_refs, refs = refs[:levels], refs[levels:]
    beside_ref, powers_ref, local_ref, normed_ref, hg_ref, cotm_ref, a0, a1, a2, a3 = refs[:10]
    gain_ref, bias_ref, skip_ref, b0, b1, b2, b3, g0, g1, g2, g3 = refs[10:21]
    state_ref, back_ref, backends_ref, ylow_ref, hid_ref, own_ref, sent_ref = refs[21:28]
    c_all, ug_all, step, full, carry, act_ref, ul, eback, acc_out, acc_down, acc_ug, sems = refs[28:]
    block = pl.program_id(0)
    place, core, shard = where_ref[0], where_ref[1], where_ref[2]
    states = c_all.shape[0] // 2
    rows, width = normed_ref.shape
    per_block = rows // length
    per_s = states // TENSOR
    per_f = hid_ref.shape[1] // TENSOR

    @pl.when(block == 0)
    def _():
        copies = []
        for k, (pack, gates) in enumerate(((b0, g0), (b1, g1), (b2, g2), (b3, g3))):
            t = shard ^ k
            moves = (
                (pack.at[pl.ds(0, per_s), :], c_all.at[pl.ds(pl.multiple_of(t * per_s, per_s), per_s), :]),
                (pack.at[pl.ds(per_s, per_s), :], c_all.at[pl.ds(pl.multiple_of(states + t * per_s, per_s), per_s), :]),
                (gates, ug_all.at[:, pl.ds(pl.multiple_of(t * 2 * per_f, 2 * per_f), 2 * per_f)]),
            )
            for n, (src, dst) in enumerate(moves):
                copies.append(pltpu.make_async_copy(src, dst, sems.at[k, n]))
        for copy in copies:
            copy.start()
        dr, di, _ = read_params((a0, a1, a2, a3), a0.shape[0] - PARAM_ROWS)
        fill_powers(dr, di, False, 1, full)
        incoming(far_refs, beside_ref, place % 2, powers_ref, False, carry)
        fill_steps(dr, di, True, step)
        acc_out[...] = jnp.zeros(acc_out.shape, F32)
        acc_down[...] = jnp.zeros(acc_down.shape, F32)
        acc_ug[...] = jnp.zeros(acc_ug.shape, F32)
        for copy in copies:
            copy.wait()

    for s in range(per_block):
        seq = block * per_block + s
        span = slice(s * length, (s + 1) * length)
        sr = carry[pl.ds(seq, 1), :states]
        si = carry[pl.ds(seq, 1), states:]
        mr, mi = cmul(full[0], full[1], sr, si)
        state_ref[span, :states] = (local_ref[span, :states] + mr).astype(BF16)
        state_ref[span, states:] = (-(local_ref[span, states:] + mi)).astype(BF16)
    skip = skip_ref[...]
    y = dot(state_ref[...], c_all[...]) + (normed_ref[...] * (gain_ref[...] * skip) + bias_ref[...] * skip)
    square = y * y
    th = jnp.tanh(GELU_K * y * (1.0 + 0.044715 * square))
    act_ref[...] = (0.5 * y * (1.0 + th)).astype(BF16)
    slope = 0.5 * (1.0 + th) + (0.5 * GELU_K) * y * (1.0 - th * th) * (1.0 + (3 * 0.044715) * square)
    act = act_ref[...]
    cotm = cotm_ref[...]
    for t in range(TENSOR):
        both = dot(act, ug_all[:, 2 * per_f * t : 2 * per_f * (t + 1)])
        up = both[:, :per_f]
        sig = jax.nn.sigmoid(both[:, per_f:])
        hid_ref[:, per_f * t : per_f * (t + 1)] = (up * sig).astype(BF16)
        up_grad = hg_ref[:, per_f * t : per_f * (t + 1)].astype(F32) * sig
        ul[:, 2 * per_f * t : 2 * per_f * t + per_f] = up_grad.astype(BF16)
        ul[:, 2 * per_f * t + per_f : 2 * per_f * (t + 1)] = (up_grad * up * (1.0 - sig)).astype(BF16)
    y_grad = dot_nt(ul[...], ug_all[...]) * slope
    ylow_ref[...] = y_grad.astype(BF16)
    eback[...] = dot_nt(ylow_ref[...], c_all[...])

    def finish(s, r, i):
        backends_ref[pl.ds(block * per_block + s, 1), :states] = r
        backends_ref[pl.ds(block * per_block + s, 1), states:] = i

    side = shard // 2
    acc_ug[...] += dot_tn(act, ul[:, pl.ds(pl.multiple_of(side * 4 * per_f, 4 * per_f), 4 * per_f)])
    acc_down[...] += dot_tn(hid_ref[:, pl.ds(pl.multiple_of(side * 2 * per_f, 2 * per_f), 2 * per_f)], cotm)
    for k in range(2):
        cols = state_ref[:, pl.ds(pl.multiple_of(k * states + side * 2 * per_s, 2 * per_s), 2 * per_s)]
        acc_out[k * 2 * per_s : (k + 1) * 2 * per_s, :] += dot_tn(cols, ylow_ref[...])
    scan_block(eback, back_ref, step, length, True, finish)

    @pl.when(block == pl.num_programs(0) - 1)
    def _():
        for n, ref in ((core, own_ref), (1 - core, sent_ref)):
            for k in range(2):
                part = acc_out[pl.ds(pl.multiple_of(2 * per_s * k + n * per_s, per_s), per_s), :]
                ref[k * per_s : (k + 1) * per_s, :] = part.astype(ref.dtype)
            part = acc_down[pl.ds(pl.multiple_of(n * per_f, per_f), per_f), :]
            ref[2 * per_s : 2 * per_s + per_f, :] = part.astype(ref.dtype)
            part = acc_ug[:, pl.ds(pl.multiple_of(n * 2 * per_f, 2 * per_f), 2 * per_f)]
            ref[2 * per_s + per_f : 2 * per_s + per_f + width, :] = part.astype(ref.dtype)


def down_kernel(where_ref, lens_ref, tok_ref, hid_ref, b0, b1, b2, b3, all_ref, out_ref, down_all, *, length, per_s, seqs):
    block = pl.program_id(0)
    shard = where_ref[2]
    rows, width = tok_ref.shape
    per_block = rows // length
    per_f = down_all.shape[0] // TENSOR

    @pl.when(block == 0)
    def _():
        for k, pack in enumerate((b0, b1, b2, b3)):
            down_all[pl.ds(pl.multiple_of((shard ^ k) * per_f, per_f), per_f), :] = pack[2 * per_s :, :]

    added = dot(hid_ref[...], down_all[...])
    for s in range(per_block):
        span = slice(s * length, (s + 1) * length)
        left = lens_ref[where_ref[1] * seqs + block * per_block + s] - where_ref[0] * length
        live = lax.broadcasted_iota(jnp.int32, (length, width), 0) < left
        out_ref[span, :] = jnp.where(live, tok_ref[span, :].astype(F32) + added[span, :], 0.0).astype(BF16)
    all_ref[...] = out_ref[...]


def last_kernel(where_ref, *refs, length, levels):
    far_refs, refs = refs[:levels], refs[levels:]
    beside_ref, powers_ref, low_ref, normed_ref, inv_ref, cotm_ref, back_ref, state_ref, ylow_ref = refs[:9]
    a0, a1, a2, a3, gain_ref, bias_ref, skip_ref, all_ref, grad_ref, own_ref, sent_ref = refs[9:20]
    in_t, full, carry, gam, dlow, in_grad, lam_grad, vec_grad = refs[20:]
    block = pl.program_id(0)
    place, core, shard = where_ref[0], where_ref[1], where_ref[2]
    states = in_t.shape[0] // 2
    rows, width = low_ref.shape
    per_block = rows // length
    per_s = states // TENSOR
    packs = (a0, a1, a2, a3)

    @pl.when(block == 0)
    def _():
        assemble_input(packs, shard, in_t)
        dr, di, gain = read_params(packs, a0.shape[0] - PARAM_ROWS)
        fill_powers(dr, di, True, 1, full)
        incoming(far_refs, beside_ref, place % 2, powers_ref, True, carry)
        gam[...] = jnp.concatenate([gain, -gain], axis=1)
        in_grad[...] = jnp.zeros(in_grad.shape, F32)
        lam_grad[...] = jnp.zeros(lam_grad.shape, F32)
        vec_grad[...] = jnp.zeros(vec_grad.shape, F32)

    for s in range(per_block):
        seq = block * per_block + s
        span = slice(s * length, (s + 1) * length)
        sr = carry[pl.ds(seq, 1), :states]
        si = carry[pl.ds(seq, 1), states:]
        mr, mi = cmul(full[0], full[1], sr, si)
        gr = back_ref[span, :states] + mr
        gi = back_ref[span, states:] + mi
        dlow[span, :states] = (gr * gam[:, :states]).astype(BF16)
        dlow[span, states:] = (gi * gam[:, states:]).astype(BF16)
        nr = jnp.concatenate([gr[1:], sr], axis=0)
        ni = jnp.concatenate([gi[1:], si], axis=0)
        hr = state_ref[span, :states].astype(F32)
        hi = state_ref[span, states:].astype(F32)
        lam_grad[:, :states] += jnp.sum(nr * hr + ni * hi, axis=0, keepdims=True)
        lam_grad[:, states:] += jnp.sum(nr * hi - ni * hr, axis=0, keepdims=True)
    normed = normed_ref[...]
    ylow = ylow_ref[...].astype(F32)
    u_grad = dot(dlow[...], in_t[...]) + ylow * skip_ref[...]
    vec_grad[0:1, :] += jnp.sum(u_grad * normed, axis=0, keepdims=True)
    vec_grad[1:2, :] += jnp.sum(u_grad, axis=0, keepdims=True)
    vec_grad[2:3, :] += jnp.sum(ylow * (normed * gain_ref[...] + bias_ref[...]), axis=0, keepdims=True)
    scaled = u_grad * gain_ref[...]
    grad = (
        scaled
        - jnp.mean(scaled, axis=-1, keepdims=True)
        - normed * jnp.mean(scaled * normed, axis=-1, keepdims=True)
    )
    grad_ref[...] = (cotm_ref[...].astype(F32) + inv_ref[:, :1] * grad).astype(BF16)
    all_ref[...] = grad_ref[...].astype(F32)
    at = pl.multiple_of((shard // 2) * 2 * per_s, 2 * per_s)
    for k in range(2):
        cols = dlow[:, pl.ds(k * states + at, 2 * per_s)]
        in_grad[2 * per_s * k : 2 * per_s * (k + 1), :] += dot_tn(cols, low_ref[...])

    @pl.when(block == pl.num_programs(0) - 1)
    def _():
        small = jnp.concatenate(
            [vec_grad[:3, :], lam_grad[...], jnp.zeros((PARAM_ROWS - 4, width), F32)], axis=0
        ).astype(BF16)
        for n, ref in ((core, own_ref), (1 - core, sent_ref)):
            for k in range(2):
                part = in_grad[pl.ds(pl.multiple_of(2 * per_s * k + n * per_s, per_s), per_s), :]
                ref[k * per_s : (k + 1) * per_s, :] = part.astype(BF16)
            ref[2 * per_s :, :] = small


def fold_kernel(where_ref, own_ref, other_ref, keep_ref, send_ref):
    half = keep_ref.shape[0]
    odd = where_ref[0] % 2
    at = pl.multiple_of(odd * half, 16)
    keep_ref[...] = own_ref[pl.ds(at, half), :] + other_ref[pl.ds(at, half), :].astype(F32)
    at = pl.multiple_of((1 - odd) * half, 16)
    send_ref[...] = (own_ref[pl.ds(at, half), :] + other_ref[pl.ds(at, half), :].astype(F32)).astype(BF16)


def deal_kernel(where_ref, own_ref, other_ref, keep_ref, *send_refs):
    rows = keep_ref.shape[0]
    for k, ref in enumerate((keep_ref,) + send_refs):
        at = pl.multiple_of(((where_ref[0] // 2) ^ k) * rows, 16)
        ref[...] = (own_ref[pl.ds(at, rows), :] + other_ref[pl.ds(at, rows), :].astype(F32)).astype(ref.dtype)


def place_kernel(where_ref, all_ref, other_ref, out_ref):
    out_ref[...] = other_ref[...].astype(out_ref.dtype)


def finish_kernel(where_ref, *refs, ways):
    parts, refs = refs[: 2 * ways], refs[2 * ways :]
    mine_ref, other_ref, in_real, in_imag, nu, theta = refs[:6]
    vec_refs, (in_real_ref, in_imag_ref, nu_ref, theta_ref, gamma_ref) = refs[6:9], refs[9:14]
    real_ref, imag_ref, up_ref, gate_ref, down_ref, total = refs[14:]
    place = where_ref[0]
    rows = parts[0].shape[0]
    for n, part in enumerate(parts):
        half = place % 2 if n < ways else 1 - place % 2
        at = (half * ways + ((place // 2) ^ (n % ways))) * rows
        total[pl.ds(pl.multiple_of(at, 16), rows), :] = part[...].astype(F32)
    per_s = real_ref.shape[0]
    per_f = down_ref.shape[0]
    last = 2 * per_s + per_f + up_ref.shape[0]
    real_ref[...] = total[:per_s, :]
    imag_ref[...] = total[per_s : 2 * per_s, :]
    down_ref[...] = total[2 * per_s : 2 * per_s + per_f, :]
    up_ref[...] = total[2 * per_s + per_f : last, :per_f]
    gate_ref[...] = total[2 * per_s + per_f : last, per_f:]

    grads = mine_ref[...].astype(F32) + other_ref[...].astype(F32)
    in_real_ref[...] = grads[:per_s, :]
    in_imag_ref[...] = grads[per_s : 2 * per_s, :]
    for n in range(3):
        vec_refs[n][...] = grads[2 * per_s + n : 2 * per_s + n + 1, :]
    lam = [jnp.zeros((1, per_s), F32), jnp.zeros((1, per_s), F32)]
    for t in range(TENSOR):
        for n in range(2):
            at = (n * TENSOR + t) * per_s
            part = grads[2 * per_s + 3 : 2 * per_s + 4, at : at + per_s]
            lam[n] = jnp.where(where_ref[2] == t, part, lam[n])
    decay = jnp.exp(nu[...])
    modulus = jnp.exp(-decay)
    angle = jnp.exp(theta[...])
    cos, sin = jnp.cos(angle), jnp.sin(angle)
    nu_ref[...] = -decay * modulus * (lam[0] * cos + lam[1] * sin)
    theta_ref[...] = angle * modulus * (lam[1] * cos - lam[0] * sin)
    terms = in_real[...].astype(F32) * grads[:per_s, :] + in_imag[...].astype(F32) * grads[per_s : 2 * per_s, :]
    gamma_ref[...] = jnp.sum(terms.T, axis=0, keepdims=True)


def whole(shape):
    return pl.BlockSpec(shape, lambda *_: (0,) * len(shape))


def near(value):
    return pltpu.with_memory_space_constraint(value, pltpu.VMEM)


def far(value):
    return pltpu.with_memory_space_constraint(value, pltpu.HBM)


def call(kernel, grid, prefetch, in_specs, out_specs, out_shape, scratch, cost, vmem, aliases=None):
    return pl.pallas_call(
        kernel,
        grid_spec=pltpu.PrefetchScalarGridSpec(
            num_scalar_prefetch=prefetch,
            grid=grid,
            in_specs=in_specs,
            out_specs=out_specs,
            scratch_shapes=scratch,
        ),
        out_shape=out_shape,
        input_output_aliases=aliases or {},
        compiler_params=pltpu.CompilerParams(vmem_limit_bytes=vmem * MIB),
        cost_estimate=pl.CostEstimate(flops=1, bytes_accessed=int(cost * 3.3e6), transcendentals=0),
    )


def core_swap(value):
    return lax.ppermute(value, "tensor", [(t, t ^ 1) for t in range(TENSOR)])


def side_swap(value):
    return lax.ppermute(value, "tensor", [(t, t ^ 2) for t in range(TENSOR)])


def gather_tensor(own, *first):
    across = after(side_swap(own), *first)
    return own, core_swap(own), across, core_swap(across)


def after(value, *first):
    return lax.optimization_barrier((value,) + first)[0]


def flip_dp(value, bits, groups):
    return lax.ppermute(value, "dp", [(i, i ^ bits) for i in range(groups)])


def shift_dp(value, by, groups):
    return lax.ppermute(value, "dp", [(i, i + by) for i in range(groups) if 0 <= i + by < groups])


def shards(
    tokens,
    cotangent,
    ln_gain,
    ln_bias,
    skip_gain,
    in_real,
    in_imag,
    out_real,
    out_imag,
    nu_log,
    theta_log,
    gamma_log,
    up_weight,
    gate_weight,
    down_weight,
    lengths,
    *,
    groups,
):
    seqs, length, width = tokens.shape
    per_s = in_real.shape[1]
    per_f = up_weight.shape[1]
    states = per_s * TENSOR
    own_seqs = seqs // 2
    rows = own_seqs * length
    blocks = rows // BLOCK
    place = lax.axis_index("dp").astype(jnp.int32)
    shard = lax.axis_index("tensor").astype(jnp.int32)
    core = shard % 2
    where = jnp.stack([place, core, shard])

    tok_rows = tokens.reshape(seqs * length, width)
    cot_rows = cotangent.reshape(seqs * length, width)
    row = lambda v: v.reshape(1, width)
    gain_row, bias_row, skip_row = row(ln_gain), row(ln_bias), row(skip_gain)
    half_spec = pl.BlockSpec((BLOCK, width), lambda b, w, *_: (w[1] * blocks + b, 0))
    row_spec = lambda lanes: pl.BlockSpec((BLOCK, lanes), lambda b, *_: (b, 0))
    a_shape = (2 * per_s + PARAM_ROWS, width)
    b_shape = (2 * per_s + per_f, width)
    a_spec = [whole(a_shape)] * TENSOR
    b_spec = [whole(b_shape)] * TENSOR
    any_spec = [pl.BlockSpec(memory_space=pl.ANY)] * TENSOR
    vec_spec = whole((1, width))
    shape = jax.ShapeDtypeStruct
    kept = pltpu.VMEM
    lanes = 2 * states
    units = TENSOR * per_f

    line = lambda v: v.reshape(1, per_s)
    pack_a = call(
        input_pack_kernel,
        (1,),
        1,
        [whole((per_s, width))] * 2 + [whole((1, per_s))] * 3,
        whole(a_shape),
        shape(a_shape, BF16),
        [],
        1,
        4,
    )(where, *map(far, (in_real.T, in_imag.T, line(nu_log), line(theta_log), line(gamma_log))))
    low, normed, inv, cot_m = call(
        functools.partial(norm_kernel, length=length, seqs=own_seqs),
        (blocks,),
        2,
        [half_spec, half_spec, vec_spec, vec_spec],
        [row_spec(width), row_spec(width), row_spec(128), row_spec(width)],
        [kept((rows, width), BF16), kept((rows, width), F32), kept((rows, 128), F32), kept((rows, width), BF16)],
        [],
        3,
        8,
    )(where, lengths, far(after(tok_rows, pack_a)), far(cot_rows), far(gain_row), far(bias_row))

    packs_a = gather_tensor(pack_a, low)
    pack_b, pack_g = call(
        weight_pack_kernel,
        (1,),
        0,
        [whole((per_s, width))] * 2 + [whole((width, per_f))] * 2 + [whole((per_f, width))],
        [whole(b_shape), whole((width, 2 * per_f))],
        [shape(b_shape, BF16), shape((width, 2 * per_f), BF16)],
        [],
        2,
        10,
    )(*map(far, (after(out_real, packs_a[2]), out_imag, up_weight, gate_weight, down_weight)))
    near_a = tuple(map(near, packs_a))
    drive, ends, powers = call(
        functools.partial(drive_kernel, length=length),
        (blocks,),
        1,
        [row_spec(width)] + a_spec,
        [row_spec(lanes), whole((own_seqs, lanes)), whole((TILE, lanes))],
        [kept((rows, lanes), F32), shape((own_seqs, lanes), F32), shape((TILE, lanes), F32)],
        [
            pltpu.VMEM((lanes, width), BF16),
            pltpu.VMEM((2, length, states), F32),
            pltpu.VMEM((1, lanes), F32),
        ],
        4,
        8,
    )(where, near(low), *near_a)

    local = call(
        functools.partial(scan_kernel, length=length),
        (blocks,),
        0,
        [row_spec(lanes)] + a_spec,
        row_spec(lanes),
        kept((rows, lanes), F32),
        [pltpu.VMEM((4, 2, TILE, states), F32)],
        4,
        8,
    )(near(drive), *near_a)
    ways = groups // 2
    levels = (ways - 1).bit_length()
    end_spec = whole((own_seqs, lanes))
    power_spec = whole((TILE, lanes))

    def small(kernel, prefetch, inputs):
        return call(
            kernel,
            (1,),
            prefetch,
            [end_spec, end_spec, power_spec],
            end_spec,
            shape((own_seqs, lanes), F32),
            [],
            1,
            2,
        )(*inputs)

    def exchange(mine, backwards, beside_work):
        beside = after(flip_dp(mine, 1, groups), beside_work)
        both = small(functools.partial(pair_kernel, backwards=backwards), 1, (where, mine, beside, powers))
        found = [both]
        from_far = []
        for k in range(levels):
            step = 2 << k
            from_far.append(shift_dp(found[-1], -step if backwards else step, groups))
            if k + 1 < levels:
                found.append(small(functools.partial(join_kernel, row=1 + k), 0, (found[-1], from_far[-1], powers)))
        return from_far, beside, found

    far_ends, beside_ends, found_ends = exchange(ends, False, local)
    near_b = tuple(map(near, gather_tensor(pack_b, far_ends[0])))
    hid_grad = call(
        functools.partial(hidden_kernel, per_s=per_s),
        (blocks,),
        1,
        [row_spec(width)] + b_spec,
        row_spec(units),
        kept((rows, units), BF16),
        [],
        3,
        10,
    )(where, near(after(cot_m, found_ends[-1])), *near_b)
    packs_g = gather_tensor(pack_g, hid_grad, *far_ends)
    pack_rows = -(-(2 * per_s + per_f + width) // (16 * groups)) * 16 * groups
    state, back, back_ends, y_low, hid, own_b, sent_b = call(
        functools.partial(middle_kernel, length=length, levels=levels),
        (blocks,),
        1,
        [end_spec] * (levels + 1)
        + [power_spec, row_spec(lanes), row_spec(width), row_spec(units), row_spec(width)]
        + a_spec
        + [vec_spec] * 3
        + any_spec
        + any_spec,
        [
            row_spec(lanes),
            row_spec(lanes),
            end_spec,
            row_spec(width),
            row_spec(units),
            whole((pack_rows, width)),
            whole((pack_rows, width)),
        ],
        [
            kept((rows, lanes), BF16),
            kept((rows, lanes), F32),
            shape((own_seqs, lanes), F32),
            kept((rows, width), BF16),
            kept((rows, units), BF16),
            shape((pack_rows, width), F32),
            shape((pack_rows, width), BF16),
        ],
        [
            pltpu.VMEM((lanes, width), BF16),
            pltpu.VMEM((width, 2 * units), BF16),
            pltpu.VMEM((4, 2, TILE, states), F32),
            pltpu.VMEM((2, length, states), F32),
            pltpu.VMEM((own_seqs, lanes), F32),
            pltpu.VMEM((BLOCK, width), BF16),
            pltpu.VMEM((BLOCK, 2 * units), BF16),
            pltpu.VMEM((BLOCK, lanes), F32),
            pltpu.VMEM((states, width), F32),
            pltpu.VMEM((2 * per_f, width), F32),
            pltpu.VMEM((width, 4 * per_f), F32),
            pltpu.SemaphoreType.DMA((TENSOR, 3)),
        ],
        21,
        20,
    )(
        where,
        *far_ends,
        beside_ends,
        powers,
        *map(near, (local, normed, hid_grad, cot_m)),
        *near_a,
        gain_row,
        bias_row,
        skip_row,
        *near_b,
        *packs_g,
    )

    half, part = pack_rows // 2, pack_rows // groups
    keep_b, send_b = call(
        fold_kernel,
        (1,),
        1,
        [whole((pack_rows, width))] * 2,
        [whole((half, width))] * 2,
        [shape((half, width), F32), shape((half, width), BF16)],
        [],
        2,
        8,
    )(where, own_b, core_swap(sent_b))
    far_back, beside_back, found_back = exchange(back_ends, True, send_b)
    half_b = flip_dp(after(send_b, found_back[0]), 1, groups)

    all_out, out_own = call(
        functools.partial(down_kernel, length=length, per_s=per_s, seqs=own_seqs),
        (blocks,),
        2,
        [half_spec, row_spec(units)] + b_spec,
        [half_spec, row_spec(width)],
        [shape((seqs * length, width), BF16), shape((rows, width), BF16)],
        [pltpu.VMEM((units, width), BF16)],
        5,
        8,
    )(where, lengths, far(tok_rows), near(after(hid, found_back[-1])), *near_b)

    dealt = call(
        deal_kernel,
        (1,),
        1,
        [whole((half, width))] * 2,
        [whole((part, width))] * ways,
        [shape((part, width), F32)] + [shape((part, width), BF16)] * (ways - 1),
        [],
        2,
        8,
    )(where, after(keep_b, out_own, *far_back), half_b)

    all_grad, grad_own, own_a, sent_a = call(
        functools.partial(last_kernel, length=length, levels=levels),
        (blocks,),
        1,
        [end_spec] * (levels + 1)
        + [
            power_spec,
            row_spec(width),
            row_spec(width),
            row_spec(128),
            row_spec(width),
            row_spec(lanes),
            row_spec(lanes),
            row_spec(width),
        ]
        + a_spec
        + [vec_spec] * 3,
        [half_spec, row_spec(width), whole(a_shape), whole(a_shape)],
        [
            shape((seqs * length, width), F32),
            shape((rows, width), BF16),
            shape(a_shape, BF16),
            shape(a_shape, BF16),
        ],
        [
            pltpu.VMEM((lanes, width), BF16),
            pltpu.VMEM((2, length, states), F32),
            pltpu.VMEM((own_seqs, lanes), F32),
            pltpu.VMEM((1, lanes), F32),
            pltpu.VMEM((BLOCK, lanes), BF16),
            pltpu.VMEM((states, width), F32),
            pltpu.VMEM((1, lanes), F32),
            pltpu.VMEM((TILE, width), F32),
        ],
        8,
        14,
    )(
        where,
        *far_back,
        after(beside_back, dealt[0], out_own),
        powers,
        *map(near, (low, normed, inv, cot_m, back, state, y_low)),
        *near_a,
        gain_row,
        bias_row,
        skip_row,
    )

    mine_b = dealt[0]
    for k in range(1, ways):
        mine_b = mine_b + flip_dp(dealt[k], 2 * k, groups).astype(F32)
    mine_b = mine_b.astype(BF16)

    gathered = [mine_b] + [flip_dp(mine_b, 2 * k, groups) for k in range(1, ways)]
    beside = [flip_dp(piece, 1, groups) for piece in gathered]

    grads_a = own_a.astype(F32) + core_swap(after(sent_a, mine_b)).astype(F32)
    low_a = grads_a.astype(BF16)
    other_a = flip_dp(low_a, 1, groups)

    def complete(partly, other):
        steps = blocks // 2
        spec = pl.BlockSpec((rows // steps, width), lambda b, w, *_: ((1 - w[1]) * steps + b, 0))
        return call(
            place_kernel,
            (steps,),
            1,
            [pl.BlockSpec(memory_space=pl.ANY), pl.BlockSpec((rows // steps, width), lambda b, *_: (b, 0))],
            spec,
            shape(partly.shape, partly.dtype),
            [],
            2,
            8,
            {1: 0},
        )(where, partly, other).reshape(seqs, length, width)

    block_out = complete(all_out, core_swap(out_own))
    input_grad = complete(all_grad, core_swap(after(grad_own, low_a)))
    bit = 2
    while bit < groups:
        low_a = (low_a.astype(F32) + other_a.astype(F32)).astype(BF16)
        if bit == 2:
            low_a = after(low_a, block_out, input_grad, *gathered)
        elif bit == 4:
            low_a = after(low_a, *beside[:2])
        other_a = flip_dp(low_a, bit, groups)
        bit *= 2

    state_shape = shape((per_s, width), F32)
    finished = call(
        functools.partial(finish_kernel, ways=ways),
        (1,),
        1,
        [whole((part, width))] * groups
        + [whole(a_shape)] * 2
        + [whole((per_s, width))] * 2
        + [whole((1, per_s))] * 2,
        [vec_spec] * 3
        + [whole((per_s, width))] * 2
        + [whole((1, per_s))] * 3
        + [whole((per_s, width))] * 2
        + [whole((width, per_f))] * 2
        + [whole((per_f, width))],
        [shape((1, width), F32)] * 3
        + [state_shape] * 2
        + [shape((1, per_s), F32)] * 3
        + [state_shape] * 2
        + [shape((width, per_f), F32)] * 2
        + [shape((per_f, width), F32)],
        [pltpu.VMEM((pack_rows, width), F32)],
        3,
        12,
    )(
        where,
        *gathered,
        *beside,
        low_a,
        other_a,
        *map(far, (in_real.T, in_imag.T, line(nu_log), line(theta_log))),
    )
    vectors, in_grads, logs = finished[:3], finished[3:5], finished[5:8]
    return (
        block_out,
        input_grad,
        *[v.reshape(width) for v in vectors],
        *[v.T for v in in_grads],
        *finished[8:10],
        *[v.reshape(per_s) for v in logs],
        *finished[10:],
    )


def solution(mesh):
    rows = P(None, "dp", None)
    columns = P(None, "tensor")
    lines = P("tensor", None)
    vector = P("tensor")
    in_specs = (rows, rows, P(), P(), P(), columns, columns, lines, lines, vector, vector, vector, columns, columns, lines, P())
    out_specs = (rows, rows, P(), P(), P(), columns, columns, lines, lines, vector, vector, vector, columns, columns, lines)
    return jax.shard_map(
        functools.partial(shards, groups=mesh.shape["dp"]),
        mesh=mesh,
        in_specs=in_specs,
        out_specs=out_specs,
        check_vma=False,
    )
```

```python
import functools
import math

import jax
import jax.numpy as jnp
from jax import lax
from jax.experimental import pallas as pl
from jax.experimental.pallas import tpu as pltpu
from jax.sharding import PartitionSpec as P

EPSILON = 1e-05
TENSOR = 4
TILE = 8
BLOCK = 256
PARAM_ROWS = 16
F32 = jnp.float32
BF16 = jnp.bfloat16
GELU_K = math.sqrt(2.0 / math.pi)
MIB = 1024 * 1024


def dot(left, right):
    return jnp.dot(left, right, preferred_element_type=F32)


def dot_nt(left, right):
    return lax.dot_general(left, right, (((1,), (1,)), ((), ())), preferred_element_type=F32)


def dot_tn(left, right):
    return lax.dot_general(left, right, (((0,), (0,)), ((), ())), preferred_element_type=F32)


def layer_norm(rows):
    centre = jnp.mean(rows, axis=-1, keepdims=True)
    shifted = rows - centre
    variance = jnp.mean(shifted * shifted, axis=-1, keepdims=True)
    inv_scale = lax.rsqrt(variance + EPSILON)
    return shifted * inv_scale, inv_scale


def cmul(ar, ai, br, bi):
    return ar * br - ai * bi, ar * bi + ai * br


def read_params(packs, row):
    total = None
    for pack in packs:
        rows = pack[row : row + PARAM_ROWS, :].astype(F32)
        total = rows if total is None else total + rows
    states = total.shape[1] // 2
    at = lambda k: total[k : k + 1, :states] + total[k + 3 : k + 4, :states] + total[k + 6 : k + 7, :states]
    return at(0), at(1), at(2)


def powers_of(decay_real, decay_imag, exponent):
    out_r = jnp.ones(exponent.shape, F32)
    out_i = jnp.zeros(exponent.shape, F32)
    br, bi = decay_real, decay_imag
    for bit in range(4):
        mr, mi = cmul(out_r, out_i, br, bi)
        on = ((exponent >> bit) & 1) == 1
        out_r = jnp.where(on, mr, out_r)
        out_i = jnp.where(on, mi, out_i)
        br, bi = cmul(br, bi, br, bi)
    return out_r, out_i


def fill_steps(decay_real, decay_imag, backwards, step_ref):
    states = decay_real.shape[1]
    row = lax.broadcasted_iota(jnp.int32, (TILE, states), 0)
    if backwards:
        row = TILE - 1 - row
    zero = jnp.zeros((TILE, states), F32)
    for k, shift in enumerate((1, 2, 4)):
        pr, pi = powers_of(decay_real, decay_imag, jnp.full((TILE, states), shift, jnp.int32))
        step_ref[k, 0] = jnp.where(row >= shift, pr, zero)
        step_ref[k, 1] = jnp.where(row >= shift, pi, zero)
    step_ref[3, 0], step_ref[3, 1] = powers_of(decay_real, decay_imag, row + 1)


def fill_powers(decay_real, decay_imag, backwards, first, full_ref):
    states = decay_real.shape[1]
    row = lax.broadcasted_iota(jnp.int32, (TILE, states), 0)
    if backwards:
        row = TILE - 1 - row
    pr, pi = powers_of(decay_real, decay_imag, row + first)
    er, ei = powers_of(decay_real, decay_imag, jnp.full((TILE, states), TILE, jnp.int32))
    tiles = full_ref.shape[1] // TILE
    for n in range(tiles):
        at = (tiles - 1 - n if backwards else n) * TILE
        full_ref[0, at : at + TILE, :] = pr
        full_ref[1, at : at + TILE, :] = pi
        pr, pi = cmul(pr, pi, er, ei)


def scan_block(drive_ref, out_ref, step_ref, length, backwards):
    rows, lanes = drive_ref.shape
    states = lanes // 2
    tiles = length // TILE
    table = [(step_ref[k, 0], step_ref[k, 1]) for k in range(4)]
    edge = 0 if backwards else TILE - 1
    for s in range(rows // length):
        cr = ci = None
        for n in range(tiles):
            at = s * length + (tiles - 1 - n if backwards else n) * TILE
            hr = drive_ref[at : at + TILE, :states]
            hi = drive_ref[at : at + TILE, states:]
            for k, shift in enumerate((1, 2, 4)):
                turn = TILE - shift if backwards else shift
                sr = pltpu.roll(hr, turn, 0)
                si = pltpu.roll(hi, turn, 0)
                mr, mi = cmul(table[k][0], table[k][1], sr, si)
                hr, hi = hr + mr, hi + mi
            if cr is not None:
                mr, mi = cmul(table[3][0], table[3][1], cr, ci)
                hr, hi = hr + mr, hi + mi
            out_ref[at : at + TILE, :states] = hr
            out_ref[at : at + TILE, states:] = hi
            cr, ci = hr[edge : edge + 1], hi[edge : edge + 1]


def each_block(rows, body):
    def step(block, carry):
        at = pl.multiple_of(block * BLOCK, BLOCK)
        body(block, lambda ref: ref.at[pl.ds(at, BLOCK), :])
        return carry

    lax.fori_loop(0, rows // BLOCK, step, 0)


def fetch(pairs, sems):
    copies = [pltpu.make_async_copy(src, dst, sems.at[n]) for n, (src, dst) in enumerate(pairs)]
    for copy in copies:
        copy.start()
    for copy in copies:
        copy.wait()


def half_copies(where_ref, src, dst, sems):
    rows = dst.shape[0]
    first = where_ref[1] * rows
    return [
        pltpu.make_async_copy(
            src.at[pl.ds(pl.multiple_of(first + n * BLOCK, BLOCK), BLOCK), :],
            dst.at[pl.ds(n * BLOCK, BLOCK), :],
            sems.at[n],
        )
        for n in range(rows // BLOCK)
    ]


def incoming(far_refs, beside_ref, odd, powers_ref, backwards, out_ref):
    states = out_ref.shape[1] // 2
    early, late = slice(0, states), slice(states, None)
    sr, si = far_refs[0][:, early], far_refs[0][:, late]
    for k in range(1, len(far_refs)):
        row = slice(4 + k, 5 + k)
        mr, mi = cmul(powers_ref[row, early], powers_ref[row, late], far_refs[k][:, early], far_refs[k][:, late])
        sr, si = sr + mr, si + mi
    mr, mi = cmul(powers_ref[0:1, early], powers_ref[0:1, late], sr, si)
    second = odd == (0 if backwards else 1)
    out_ref[:, early] = jnp.where(second, mr + beside_ref[:, early], sr)
    out_ref[:, late] = jnp.where(second, mi + beside_ref[:, late], si)


def join_kernel(mine_ref, other_ref, powers_ref, out_ref, *, row):
    states = out_ref.shape[1] // 2
    early, late = slice(0, states), slice(states, None)
    row = slice(row, row + 1)
    mr, mi = cmul(powers_ref[row, early], powers_ref[row, late], other_ref[:, early], other_ref[:, late])
    out_ref[:, early] = mine_ref[:, early] + mr
    out_ref[:, late] = mine_ref[:, late] + mi


def pair_kernel(where_ref, mine_ref, other_ref, powers_ref, out_ref, *, backwards):
    states = out_ref.shape[1] // 2
    second = where_ref[0] % 2 == (0 if backwards else 1)
    lr, li = powers_ref[0:1, :states], powers_ref[0:1, states:]
    pick = lambda first, part: jnp.where(second == first, other_ref[:, part], mine_ref[:, part])
    early, late = slice(0, states), slice(states, None)
    mr, mi = cmul(lr, li, pick(True, early), pick(True, late))
    out_ref[:, :states] = mr + pick(False, early)
    out_ref[:, states:] = mi + pick(False, late)


def assemble_input(packs, shard, out_ref):
    per = packs[0].shape[0] - PARAM_ROWS
    half = per // 2
    states = out_ref.shape[0] // 2
    for k, pack in enumerate(packs):
        at = pl.multiple_of((shard ^ k) * half, half)
        out_ref[pl.ds(at, half), :] = pack[:half, :]
        out_ref[pl.ds(states + at, half), :] = pack[half:per, :]


def input_pack_kernel(where_ref, in_real, in_imag, nu, theta, gamma, a_ref, logs, sems):
    per_s, width = in_real.shape
    fetch(
        [(in_real, a_ref.at[pl.ds(0, per_s), :]), (in_imag, a_ref.at[pl.ds(per_s, per_s), :])]
        + [(ref, logs.at[n]) for n, ref in enumerate((nu, theta, gamma))],
        sems,
    )
    modulus = jnp.exp(-jnp.exp(logs[0]))
    angle = jnp.exp(logs[1])
    rest = [modulus * jnp.cos(angle), modulus * jnp.sin(angle), jnp.exp(logs[2])]
    rows = []
    for _ in range(3):
        for n in range(3):
            high = rest[n].astype(BF16).astype(F32)
            rows.append(high)
            rest[n] = rest[n] - high
    table = jnp.concatenate(rows + [jnp.zeros((PARAM_ROWS - 9, per_s), F32)], axis=0)
    table = jnp.concatenate([table] * (width // per_s), axis=1)
    here = lax.broadcasted_iota(jnp.int32, (PARAM_ROWS, width), 1) // per_s == where_ref[2]
    a_ref[2 * per_s :, :] = jnp.where(here, table, 0.0).astype(BF16)


def weight_pack_kernel(out_real, out_imag, up, gate, down, b_ref, g_ref, sems):
    per_s, per_f = out_real.shape[0], down.shape[0]
    fetch(
        [
            (out_real, b_ref.at[pl.ds(0, per_s), :]),
            (out_imag, b_ref.at[pl.ds(per_s, per_s), :]),
            (down, b_ref.at[pl.ds(2 * per_s, per_f), :]),
            (up, g_ref.at[:, pl.ds(0, per_f)]),
            (gate, g_ref.at[:, pl.ds(per_f, per_f)]),
        ],
        sems,
    )


def mask_rows(lens_ref, where_ref, seq, seqs, length, width):
    left = lens_ref[where_ref[1] * seqs + seq] - where_ref[0] * length
    return lax.broadcasted_iota(jnp.int32, (length, width), 0) < left


def norm_kernel(
    where_ref, tok_all, cot_all, gain_all, bias_all, lens_all, low_ref, normed_ref, inv_ref, cotm_ref,
    tok, cot, gain_ref, bias_ref, lens_ref, sems, small_sems, *, length
):
    rows, width = low_ref.shape
    per_block = BLOCK // length
    halves = [half_copies(where_ref, src, dst, sems.at[n]) for n, (src, dst) in enumerate(((tok_all, tok), (cot_all, cot)))]
    for copies in zip(*halves):
        for copy in copies:
            copy.start()
    fetch([(gain_all, gain_ref), (bias_all, bias_ref), (lens_all, lens_ref)], small_sems)
    for block, copies in enumerate(zip(*halves)):
        for copy in copies:
            copy.wait()
        span = slice(block * BLOCK, (block + 1) * BLOCK)
        normed, inv_scale = layer_norm(tok[span, :].astype(F32))
        normed_ref[span, :] = normed
        inv_ref[span, :] = jnp.broadcast_to(inv_scale, (BLOCK, inv_ref.shape[1]))
        low_ref[span, :] = (normed * gain_ref[...] + bias_ref[...]).astype(BF16)
        for s in range(per_block):
            seq = block * per_block + s
            span = slice(seq * length, (seq + 1) * length)
            live = mask_rows(lens_ref, where_ref, seq, rows // length, length, width)
            cotm_ref[span, :] = jnp.where(live, cot[span, :].astype(F32), 0.0).astype(BF16)


def weighted_ends(drive_ref, weigh, length, first, ends_ref):
    rows, lanes = drive_ref.shape
    states = lanes // 2
    for s in range(rows // length):
        er = ei = jnp.zeros((TILE, states), F32)
        for n in range(length // TILE):
            at = s * length + n * TILE
            mr, mi = cmul(
                weigh[0, n * TILE : (n + 1) * TILE, :],
                weigh[1, n * TILE : (n + 1) * TILE, :],
                drive_ref[at : at + TILE, :states],
                drive_ref[at : at + TILE, states:],
            )
            er, ei = er + mr, ei + mi
        ends_ref[pl.ds(first + s, 1), :states] = jnp.sum(er, axis=0, keepdims=True)
        ends_ref[pl.ds(first + s, 1), states:] = jnp.sum(ei, axis=0, keepdims=True)


def drive_kernel(where_ref, low_all, a0, a1, a2, a3, drive_all, ends_ref, powers_ref, in_t, weigh, *, length):
    packs = (a0, a1, a2, a3)
    states = in_t.shape[0] // 2
    assemble_input(packs, where_ref[2], in_t)
    dr, di, gain = read_params(packs, a0.shape[0] - PARAM_ROWS)
    fill_powers(dr, di, True, 0, weigh)
    gam = jnp.concatenate([gain, gain], axis=1)
    lr, li = cmul(weigh[0, :1, :], weigh[1, :1, :], dr, di)
    rows = [(lr, li)] + [cmul(lr, li, lr, li)]
    for _ in range(2):
        rows.append(cmul(*rows[-1], *rows[-1]))
    rows.append((jnp.ones_like(lr), jnp.zeros_like(lr)))
    for _ in range(3):
        rows.append(cmul(*cmul(*rows[-1], *rows[-1]), *rows[1]))
    for k, (lr, li) in enumerate(rows):
        powers_ref[k : k + 1, :] = jnp.concatenate([lr, li], axis=1)
    per_block = BLOCK // length

    def body(block, view):
        low_ref, drive_ref = view(low_all), view(drive_all)
        drive_ref[...] = dot_nt(low_ref[...], in_t[...]) * gam
        weighted_ends(drive_ref, weigh, length, block * per_block, ends_ref)

    each_block(low_all.shape[0], body)


def scan_kernel(drive_all, a0, a1, a2, a3, local_all, step, *, length, backwards):
    dr, di, _ = read_params((a0, a1, a2, a3), a0.shape[0] - PARAM_ROWS)
    fill_steps(dr, di, backwards, step)
    each_block(
        drive_all.shape[0],
        lambda block, view: scan_block(view(drive_all), view(local_all), step, length, backwards),
    )


def hidden_kernel(where_ref, cotm_all, b0, b1, b2, b3, hg_all, *, per_s):
    shard = where_ref[2]
    per_f = hg_all.shape[1] // TENSOR

    def body(block, view):
        hg_ref, cotm = view(hg_all), view(cotm_all)[...]
        for k, pack in enumerate((b0, b1, b2, b3)):
            at = pl.multiple_of((shard ^ k) * per_f, per_f)
            hg_ref[:, pl.ds(at, per_f)] = dot_nt(cotm, pack[2 * per_s :, :]).astype(BF16)

    each_block(cotm_all.shape[0], body)


def middle_kernel(where_ref, *refs, length, levels):
    far_refs, refs = refs[:levels], refs[levels:]
    beside_ref, powers_ref, local_all, normed_all, hg_all, cotm_all, a0, a1, a2, a3 = refs[:10]
    gain_ref, bias_ref, skip_ref, b0, b1, b2, b3, g0, g1, g2, g3 = refs[10:21]
    state_all, back_all, backends_ref, ylow_all, hid_all, act_all, ul_half_all = refs[21:28]
    c_all, ug_all, weigh, full, carry, ul, sems = refs[28:]
    place, core, shard = where_ref[0], where_ref[1], where_ref[2]
    states = c_all.shape[0] // 2
    rows, width = normed_all.shape
    per_block = BLOCK // length
    per_s = states // TENSOR
    per_f = hid_all.shape[1] // TENSOR
    side = shard // 2

    copies = []
    for k, (pack, gates) in enumerate(((b0, g0), (b1, g1), (b2, g2), (b3, g3))):
        t = shard ^ k
        moves = (
            (pack.at[pl.ds(0, per_s), :], c_all.at[pl.ds(pl.multiple_of(t * per_s, per_s), per_s), :]),
            (pack.at[pl.ds(per_s, per_s), :], c_all.at[pl.ds(pl.multiple_of(states + t * per_s, per_s), per_s), :]),
            (gates, ug_all.at[:, pl.ds(pl.multiple_of(t * 2 * per_f, 2 * per_f), 2 * per_f)]),
        )
        for n, (src, dst) in enumerate(moves):
            copies.append(pltpu.make_async_copy(src, dst, sems.at[k, n]))
    for copy in copies:
        copy.start()
    dr, di, _ = read_params((a0, a1, a2, a3), a0.shape[0] - PARAM_ROWS)
    fill_powers(dr, di, False, 1, full)
    incoming(far_refs, beside_ref, place % 2, powers_ref, False, carry)
    fill_powers(dr, di, False, 0, weigh)
    for copy in copies:
        copy.wait()
    skip = skip_ref[...]
    skip_gain, skip_bias = gain_ref[...] * skip, bias_ref[...] * skip

    def body(block, view):
        local_ref, state_ref, hid_ref, ylow_ref = view(local_all), view(state_all), view(hid_all), view(ylow_all)
        hg_ref, act_ref, back_ref = view(hg_all), view(act_all), view(back_all)
        for s in range(per_block):
            seq = block * per_block + s
            span = slice(s * length, (s + 1) * length)
            sr = carry[pl.ds(seq, 1), :states]
            si = carry[pl.ds(seq, 1), states:]
            mr, mi = cmul(full[0], full[1], sr, si)
            state_ref[span, :states] = (local_ref[span, :states] + mr).astype(BF16)
            state_ref[span, states:] = (-(local_ref[span, states:] + mi)).astype(BF16)
        y = dot(state_ref[...], c_all[...]) + (view(normed_all)[...] * skip_gain + skip_bias)
        square = y * y
        th = jnp.tanh(y * (GELU_K + (GELU_K * 0.044715) * square))
        half_y = 0.5 * y
        act_ref[...] = (half_y + half_y * th).astype(BF16)
        slope = (0.5 + 0.5 * th) + half_y * (1.0 - th * th) * (GELU_K + (GELU_K * 3 * 0.044715) * square)
        act = act_ref[...]
        for t in range(TENSOR):
            both = dot(act, ug_all[:, 2 * per_f * t : 2 * per_f * (t + 1)])
            up = both[:, :per_f]
            th = 0.5 * jnp.tanh(0.5 * both[:, per_f:])
            sig = 0.5 + th
            hid_ref[:, per_f * t : per_f * (t + 1)] = (up * sig).astype(BF16)
            up_grad = hg_ref[:, per_f * t : per_f * (t + 1)].astype(F32) * sig
            ul[:, 2 * per_f * t : 2 * per_f * t + per_f] = up_grad.astype(BF16)
            ul[:, 2 * per_f * t + per_f : 2 * per_f * (t + 1)] = (up_grad * up * (0.5 - th)).astype(BF16)
        y_grad = dot_nt(ul[...], ug_all[...]) * slope
        ylow_ref[...] = y_grad.astype(BF16)
        back_ref[...] = dot_nt(ylow_ref[...], c_all[...])
        weighted_ends(back_ref, weigh, length, block * per_block, backends_ref)
        view(ul_half_all)[...] = ul[:, pl.ds(pl.multiple_of(side * 4 * per_f, 4 * per_f), 4 * per_f)]

    each_block(rows, body)


def weight_kernel(where_ref, hid_ref, cotm_ref, act_ref, ul_ref, state_ref, ylow_ref, own_ref, sent_ref):
    core, side = where_ref[1], where_ref[2] // 2
    states = state_ref.shape[1] // 2
    per_s = states // TENSOR
    per_f = hid_ref.shape[1] // TENSOR
    width = act_ref.shape[1]
    cols = [
        state_ref[:, pl.ds(pl.multiple_of(k * states + side * 2 * per_s, 2 * per_s), 2 * per_s)] for k in range(2)
    ]
    out_grad = dot_tn(jnp.concatenate(cols, axis=1), ylow_ref[...])
    act, cotm = act_ref[...], cotm_ref[...]
    for n, ref in ((1 - core, sent_ref), (core, own_ref)):
        ul = ul_ref[:, pl.ds(pl.multiple_of(n * 2 * per_f, 2 * per_f), 2 * per_f)]
        ref[2 * per_s + per_f : 2 * per_s + per_f + width, :] = dot_tn(act, ul).astype(ref.dtype)
        hid = hid_ref[:, pl.ds(pl.multiple_of((2 * side + n) * per_f, per_f), per_f)]
        ref[2 * per_s : 2 * per_s + per_f, :] = dot_tn(hid, cotm).astype(ref.dtype)
        for k in range(2):
            at = 2 * per_s * k
            part = jnp.where(n == 0, out_grad[at : at + per_s, :], out_grad[at + per_s : at + 2 * per_s, :])
            ref[k * per_s : (k + 1) * per_s, :] = part.astype(ref.dtype)


def down_kernel(where_ref, lens_ref, tok_all, hid_all, b0, b1, b2, b3, out_all, down_all, tok, sems, *, length, per_s):
    shard = where_ref[2]
    rows, width = out_all.shape
    per_block = BLOCK // length
    per_f = down_all.shape[0] // TENSOR
    copies = half_copies(where_ref, tok_all, tok, sems)
    for copy in copies:
        copy.start()
    for k, pack in enumerate((b0, b1, b2, b3)):
        down_all[pl.ds(pl.multiple_of((shard ^ k) * per_f, per_f), per_f), :] = pack[2 * per_s :, :]
    for copy in copies:
        copy.wait()

    def body(block, view):
        added = dot(view(hid_all)[...], down_all[...])
        out_ref, tok_ref = view(out_all), view(tok)
        for s in range(per_block):
            span = slice(s * length, (s + 1) * length)
            live = mask_rows(lens_ref, where_ref, block * per_block + s, rows // length, length, width)
            out_ref[span, :] = jnp.where(live, tok_ref[span, :].astype(F32) + added[span, :], 0.0).astype(BF16)

    each_block(rows, body)


def last_kernel(where_ref, *refs, length, levels):
    far_refs, refs = refs[:levels], refs[levels:]
    beside_ref, powers_ref, low_all, normed_all, inv_all, cotm_all, back_all, state_all, ylow_all = refs[:9]
    a0, a1, a2, a3, gain_ref, bias_ref, skip_ref, grad_all, own_ref, sent_ref = refs[9:19]
    in_t, full, carry, dlow, in_grad, lam_grad, vec_grad = refs[19:]
    place, core, shard = where_ref[0], where_ref[1], where_ref[2]
    states = in_t.shape[0] // 2
    rows, width = low_all.shape
    per_block = BLOCK // length
    per_s = states // TENSOR
    packs = (a0, a1, a2, a3)

    assemble_input(packs, shard, in_t)
    dr, di, gain = read_params(packs, a0.shape[0] - PARAM_ROWS)
    fill_powers(dr, di, True, 1, full)
    incoming(far_refs, beside_ref, place % 2, powers_ref, True, carry)
    in_grad[...] = jnp.zeros(in_grad.shape, F32)
    lam_grad[...] = jnp.zeros(lam_grad.shape, F32)
    vec_grad[...] = jnp.zeros(vec_grad.shape, F32)
    at = pl.multiple_of((shard // 2) * 2 * per_s, 2 * per_s)

    def body(block, view):
        back_ref, state_ref = view(back_all), view(state_all)
        for s in range(per_block):
            seq = block * per_block + s
            span = slice(s * length, (s + 1) * length)
            sr = carry[pl.ds(seq, 1), :states]
            si = carry[pl.ds(seq, 1), states:]
            mr, mi = cmul(full[0], full[1], sr, si)
            gr = back_ref[span, :states] + mr
            gi = back_ref[span, states:] + mi
            dlow[span, :states] = (gr * gain).astype(BF16)
            dlow[span, states:] = (gi * -gain).astype(BF16)
            nr = jnp.concatenate([gr[1:], sr], axis=0)
            ni = jnp.concatenate([gi[1:], si], axis=0)
            hr = state_ref[span, :states].astype(F32)
            hi = state_ref[span, states:].astype(F32)
            lam_grad[:, :states] += jnp.sum(nr * hr + ni * hi, axis=0, keepdims=True)
            lam_grad[:, states:] += jnp.sum(nr * hi - ni * hr, axis=0, keepdims=True)
        normed = view(normed_all)[...]
        ylow = view(ylow_all)[...].astype(F32)
        low = view(low_all)[...]
        u_grad = dot(dlow[...], in_t[...]) + ylow * skip_ref[...]
        vec_grad[0:1, :] += jnp.sum(u_grad * normed, axis=0, keepdims=True)
        vec_grad[1:2, :] += jnp.sum(u_grad, axis=0, keepdims=True)
        vec_grad[2:3, :] += jnp.sum(ylow * (normed * gain_ref[...] + bias_ref[...]), axis=0, keepdims=True)
        scaled = u_grad * gain_ref[...]
        grad = (
            scaled
            - jnp.mean(scaled, axis=-1, keepdims=True)
            - normed * jnp.mean(scaled * normed, axis=-1, keepdims=True)
        )
        view(grad_all)[...] = (view(cotm_all)[...].astype(F32) + view(inv_all)[:, :1] * grad).astype(BF16)
        for k in range(2):
            cols = dlow[:, pl.ds(k * states + at, 2 * per_s)]
            in_grad[2 * per_s * k : 2 * per_s * (k + 1), :] += dot_tn(cols, low)

    each_block(rows, body)
    small = jnp.concatenate(
        [vec_grad[:3, :], lam_grad[...], jnp.zeros((PARAM_ROWS - 4, width), F32)], axis=0
    ).astype(BF16)
    for n, ref in ((core, own_ref), (1 - core, sent_ref)):
        for k in range(2):
            part = in_grad[pl.ds(pl.multiple_of(2 * per_s * k + n * per_s, per_s), per_s), :]
            ref[k * per_s : (k + 1) * per_s, :] = part.astype(BF16)
        ref[2 * per_s :, :] = small


def join_halves_kernel(where_ref, own_ref, other_ref, out_ref, sems):
    rows = own_ref.shape[0]
    copies = [
        pltpu.make_async_copy(ref, out_ref.at[pl.ds(pl.multiple_of(n * rows, BLOCK), rows), :], sems.at[k])
        for k, (n, ref) in enumerate(((where_ref[1], own_ref), (1 - where_ref[1], other_ref)))
    ]
    for copy in copies:
        copy.start()
    for copy in copies:
        copy.wait()


def widen_halves_kernel(where_ref, own_ref, other_ref, out_ref, wide, sems):
    rows = own_ref.shape[0]
    slots = wide.shape[0]
    flying = []
    for n in range(2 * rows // BLOCK):
        slot = n % slots
        if n >= slots:
            flying[n - slots].wait()
        at = (n // 2) * BLOCK
        half, ref = ((where_ref[1], own_ref), (1 - where_ref[1], other_ref))[n % 2]
        wide[slot] = ref[at : at + BLOCK, :].astype(F32)
        copy = pltpu.make_async_copy(
            wide.at[slot], out_ref.at[pl.ds(pl.multiple_of(half * rows + at, BLOCK), BLOCK), :], sems.at[slot]
        )
        copy.start()
        flying.append(copy)
    for copy in flying[-slots:]:
        copy.wait()


def fold_kernel(where_ref, own_ref, other_ref, keep_ref, send_ref):
    half = keep_ref.shape[0]
    odd = where_ref[0] % 2
    at = pl.multiple_of(odd * half, 16)
    keep_ref[...] = own_ref[pl.ds(at, half), :] + other_ref[pl.ds(at, half), :].astype(F32)
    at = pl.multiple_of((1 - odd) * half, 16)
    send_ref[...] = (own_ref[pl.ds(at, half), :] + other_ref[pl.ds(at, half), :].astype(F32)).astype(BF16)


def deal_kernel(where_ref, own_ref, other_ref, keep_ref, *send_refs):
    rows = keep_ref.shape[0]
    for k, ref in enumerate((keep_ref,) + send_refs):
        at = pl.multiple_of(((where_ref[0] // 2) ^ k) * rows, 16)
        ref[...] = (own_ref[pl.ds(at, rows), :] + other_ref[pl.ds(at, rows), :].astype(F32)).astype(ref.dtype)


def finish_kernel(where_ref, *refs, ways):
    parts, refs = refs[: 2 * ways], refs[2 * ways :]
    mine_ref, other_ref, in_real, in_imag, nu, theta = refs[:6]
    vec_outs, (in_real_out, in_imag_out), log_outs = refs[6:9], refs[9:11], refs[11:14]
    real_ref, imag_ref, up_ref, gate_ref, down_ref, total, grads_ref, logs, fetched, sems, fetch_sems = refs[14:]
    fetch([(ref, fetched.at[n]) for n, ref in enumerate((nu, theta))], fetch_sems)
    nu, theta = fetched.at[0], fetched.at[1]
    place = where_ref[0]
    rows = parts[0].shape[0]
    for n, part in enumerate(parts):
        half = place % 2 if n < ways else 1 - place % 2
        at = (half * ways + ((place // 2) ^ (n % ways))) * rows
        total[pl.ds(pl.multiple_of(at, 16), rows), :] = part[...].astype(F32)
    per_s = real_ref.shape[0]
    per_f = down_ref.shape[0]
    moves = [
        (total.at[pl.ds(0, per_s), :], real_ref),
        (total.at[pl.ds(per_s, per_s), :], imag_ref),
        (total.at[pl.ds(2 * per_s, per_f), :], down_ref),
        (total.at[pl.ds(2 * per_s + per_f, up_ref.shape[0]), pl.ds(0, per_f)], up_ref),
        (total.at[pl.ds(2 * per_s + per_f, up_ref.shape[0]), pl.ds(per_f, per_f)], gate_ref),
    ]
    copies = [pltpu.make_async_copy(src, dst, sems.at[n]) for n, (src, dst) in enumerate(moves)]
    for copy in copies:
        copy.start()

    grads = mine_ref[...].astype(F32) + other_ref[...].astype(F32)
    grads_ref[...] = grads
    moves = [
        (grads_ref.at[pl.ds(0, per_s), :], in_real_out),
        (grads_ref.at[pl.ds(per_s, per_s), :], in_imag_out),
    ]
    moves += [(grads_ref.at[pl.ds(2 * per_s + n, 1), :], vec_outs[n]) for n in range(3)]
    more = [pltpu.make_async_copy(src, dst, sems.at[5 + n]) for n, (src, dst) in enumerate(moves)]
    for copy in more:
        copy.start()
    lam = [jnp.zeros((1, per_s), F32), jnp.zeros((1, per_s), F32)]
    for t in range(TENSOR):
        for n in range(2):
            at = (n * TENSOR + t) * per_s
            part = grads[2 * per_s + 3 : 2 * per_s + 4, at : at + per_s]
            lam[n] = jnp.where(where_ref[2] == t, part, lam[n])
    decay = jnp.exp(nu[...])
    modulus = jnp.exp(-decay)
    angle = jnp.exp(theta[...])
    cos, sin = jnp.cos(angle), jnp.sin(angle)
    logs[0] = -decay * modulus * (lam[0] * cos + lam[1] * sin)
    logs[1] = angle * modulus * (lam[1] * cos - lam[0] * sin)
    terms = in_real[...].astype(F32) * grads[:per_s, :] + in_imag[...].astype(F32) * grads[per_s : 2 * per_s, :]
    logs[2] = jnp.sum(terms.T, axis=0, keepdims=True)
    rest = [pltpu.make_async_copy(logs.at[n], log_outs[n], sems.at[10 + n]) for n in range(3)]
    for copy in rest:
        copy.start()
    for copy in copies + more + rest:
        copy.wait()


def near(value):
    return pltpu.with_memory_space_constraint(value, pltpu.VMEM)


def call(kernel, scalars, inputs, outs, scratch, vmem, far_inputs=(), far_outs=()):
    here, anywhere = pl.BlockSpec(memory_space=pltpu.VMEM), pl.BlockSpec(memory_space=pl.ANY)
    single = not isinstance(outs, list)
    listed = [outs] if single else outs
    shapes = [
        jax.ShapeDtypeStruct(*out) if n in far_outs else pltpu.VMEM(*out) for n, out in enumerate(listed)
    ]
    out_specs = [anywhere if n in far_outs else here for n in range(len(listed))]
    return pl.pallas_call(
        kernel,
        in_specs=[pl.BlockSpec(memory_space=pltpu.SMEM)] * len(scalars)
        + [anywhere if n in far_inputs else here for n in range(len(inputs))],
        out_specs=out_specs[0] if single else out_specs,
        out_shape=shapes[0] if single else shapes,
        scratch_shapes=scratch,
        compiler_params=pltpu.CompilerParams(vmem_limit_bytes=vmem * MIB),
    )(
        *scalars,
        *[
            pltpu.with_memory_space_constraint(v, pltpu.HBM) if n in far_inputs else near(v)
            for n, v in enumerate(inputs)
        ],
    )


def core_swap(value):
    return lax.ppermute(value, "tensor", [(t, t ^ 1) for t in range(TENSOR)])


def side_swap(value):
    return lax.ppermute(value, "tensor", [(t, t ^ 2) for t in range(TENSOR)])


def gather_tensor(own, *first):
    across = after(side_swap(own), *first)
    return own, core_swap(own), across, core_swap(across)


def after(value, *first):
    return lax.optimization_barrier((value,) + first)[0]


def flip_dp(value, bits, groups):
    return lax.ppermute(value, "dp", [(i, i ^ bits) for i in range(groups)])


def shift_dp(value, by, groups):
    return lax.ppermute(value, "dp", [(i, i + by) for i in range(groups) if 0 <= i + by < groups])


def shards(
    tokens,
    cotangent,
    ln_gain,
    ln_bias,
    skip_gain,
    in_real,
    in_imag,
    out_real,
    out_imag,
    nu_log,
    theta_log,
    gamma_log,
    up_weight,
    gate_weight,
    down_weight,
    lengths,
    *,
    groups,
):
    seqs, length, width = tokens.shape
    per_s = in_real.shape[1]
    per_f = up_weight.shape[1]
    states = per_s * TENSOR
    own_seqs = seqs // 2
    rows = own_seqs * length
    blocks = rows // BLOCK
    place = lax.axis_index("dp").astype(jnp.int32)
    shard = lax.axis_index("tensor").astype(jnp.int32)
    core = shard % 2
    where = jnp.stack([place, core, shard])

    tok_rows = tokens.reshape(seqs * length, width)
    cot_rows = cotangent.reshape(seqs * length, width)
    row = lambda v: v.reshape(1, width)
    gain_row, bias_row, skip_row = row(ln_gain), row(ln_bias), row(skip_gain)
    a_shape = (2 * per_s + PARAM_ROWS, width)
    b_shape = (2 * per_s + per_f, width)
    lanes = 2 * states
    units = TENSOR * per_f
    ends_shape = ((own_seqs, lanes), F32)
    dma = pltpu.SemaphoreType.DMA
    line = lambda v: v.reshape(1, per_s)

    pack_a = call(
        input_pack_kernel,
        [where],
        [in_real.T, in_imag.T, line(nu_log), line(theta_log), line(gamma_log)],
        (a_shape, BF16),
        [pltpu.VMEM((3, 1, per_s), F32), dma((5,))],
        4,
        far_inputs=range(5),
    )
    low, normed, inv, cot_m = call(
        functools.partial(norm_kernel, length=length),
        [where],
        [after(tok_rows, pack_a), cot_rows, gain_row, bias_row, lengths],
        [((rows, width), BF16), ((rows, width), F32), ((rows, 128), F32), ((rows, width), BF16)],
        [
            pltpu.VMEM((rows, width), BF16),
            pltpu.VMEM((rows, width), BF16),
            pltpu.VMEM((1, width), F32),
            pltpu.VMEM((1, width), F32),
            pltpu.SMEM((seqs,), jnp.int32),
            dma((2, blocks)),
            dma((3,)),
        ],
        8,
        far_inputs=range(5),
    )
    packs_a = gather_tensor(pack_a, low)
    pack_b, pack_g = call(
        weight_pack_kernel,
        [],
        [after(out_real, packs_a[2]), out_imag, up_weight, gate_weight, down_weight],
        [(b_shape, BF16), ((width, 2 * per_f), BF16)],
        [dma((5,))],
        4,
        far_inputs=range(5),
    )
    drive, ends, powers = call(
        functools.partial(drive_kernel, length=length),
        [where],
        [low, *packs_a],
        [((rows, lanes), F32), ends_shape, ((TILE, lanes), F32)],
        [pltpu.VMEM((lanes, width), BF16), pltpu.VMEM((2, length, states), F32)],
        8,
    )
    local = call(
        functools.partial(scan_kernel, length=length, backwards=False),
        [],
        [drive, *packs_a],
        ((rows, lanes), F32),
        [pltpu.VMEM((4, 2, TILE, states), F32)],
        8,
    )

    ways = groups // 2
    levels = (ways - 1).bit_length()

    def exchange(mine, backwards, beside_work, first_work=None):
        beside = after(flip_dp(mine, 1, groups), beside_work)
        both = call(
            functools.partial(pair_kernel, backwards=backwards), [where], [mine, beside, powers], ends_shape, [], 2
        )
        found = [both]
        from_far = []
        for k in range(levels):
            step = 2 << k
            from_far.append(shift_dp(found[-1], -step if backwards else step, groups))
            if k == 0 and first_work is not None:
                from_far[0] = after(from_far[0], first_work(both))
            if k + 1 < levels:
                found.append(
                    call(functools.partial(join_kernel, row=1 + k), [], [found[-1], from_far[-1], powers], ends_shape, [], 2)
                )
        return from_far, beside, found

    far_ends, beside_ends, found_ends = exchange(ends, False, local)
    packs_b = gather_tensor(pack_b, far_ends[0])
    hid_grad = call(
        functools.partial(hidden_kernel, per_s=per_s),
        [where],
        [after(cot_m, found_ends[-1]), *packs_b],
        ((rows, units), BF16),
        [],
        8,
    )
    packs_g = gather_tensor(pack_g, hid_grad, *far_ends)

    pack_rows = -(-(2 * per_s + per_f + width) // (16 * groups)) * 16 * groups
    state, back_drive, back_ends, y_low, hid, act, ul_half = call(
        functools.partial(middle_kernel, length=length, levels=levels),
        [where],
        [
            *far_ends,
            beside_ends,
            powers,
            local,
            normed,
            hid_grad,
            cot_m,
            *packs_a,
            gain_row,
            bias_row,
            skip_row,
            *packs_b,
            *packs_g,
        ],
        [
            ((rows, lanes), BF16),
            ((rows, lanes), F32),
            ends_shape,
            ((rows, width), BF16),
            ((rows, units), BF16),
            ((rows, width), BF16),
            ((rows, units), BF16),
        ],
        [
            pltpu.VMEM((lanes, width), BF16),
            pltpu.VMEM((width, 2 * units), BF16),
            pltpu.VMEM((2, length, states), F32),
            pltpu.VMEM((2, length, states), F32),
            pltpu.VMEM((own_seqs, lanes), F32),
            pltpu.VMEM((BLOCK, 2 * units), BF16),
            dma((TENSOR, 3)),
        ],
        14,
    )
    own_b, sent_b = call(
        weight_kernel,
        [where],
        [hid, cot_m, act, ul_half, state, y_low],
        [((pack_rows, width), F32), ((pack_rows, width), BF16)],
        [],
        10,
    )

    half, part = pack_rows // 2, pack_rows // groups
    keep_b, send_b = call(
        fold_kernel,
        [where],
        [own_b, core_swap(sent_b)],
        [((half, width), F32), ((half, width), BF16)],
        [],
        4,
    )
    made = []

    def scan_work(pair_back):
        made.append(
            call(
                functools.partial(scan_kernel, length=length, backwards=True),
                [],
                [after(back_drive, pair_back), *packs_a],
                ((rows, lanes), F32),
                [pltpu.VMEM((4, 2, TILE, states), F32)],
                8,
            )
        )
        return made[0]

    far_back, beside_back, found_back = exchange(back_ends, True, send_b, scan_work)
    back = made[0]
    half_b = flip_dp(after(send_b, found_back[0]), 1, groups)
    out_own = call(
        functools.partial(down_kernel, length=length, per_s=per_s),
        [where, lengths],
        [tok_rows, after(hid, found_back[-1]), *packs_b],
        ((rows, width), BF16),
        [pltpu.VMEM((units, width), BF16), pltpu.VMEM((rows, width), BF16), dma((blocks,))],
        8,
        far_inputs=(0,),
    )
    dealt = call(
        deal_kernel,
        [where],
        [after(keep_b, out_own, *far_back), half_b],
        [((part, width), F32)] + [((part, width), BF16)] * (ways - 1),
        [],
        4,
    )

    grad_own, own_a, sent_a = call(
        functools.partial(last_kernel, length=length, levels=levels),
        [where],
        [
            *far_back,
            after(beside_back, dealt[0]),
            powers,
            low,
            normed,
            inv,
            cot_m,
            back,
            state,
            y_low,
            *packs_a,
            gain_row,
            bias_row,
            skip_row,
        ],
        [((rows, width), BF16), (a_shape, BF16), (a_shape, BF16)],
        [
            pltpu.VMEM((lanes, width), BF16),
            pltpu.VMEM((2, length, states), F32),
            pltpu.VMEM((own_seqs, lanes), F32),
            pltpu.VMEM((BLOCK, lanes), BF16),
            pltpu.VMEM((states, width), F32),
            pltpu.VMEM((1, lanes), F32),
            pltpu.VMEM((TILE, width), F32),
        ],
        12,
    )

    mine_b = dealt[0]
    for k in range(1, ways):
        mine_b = mine_b + flip_dp(dealt[k], 2 * k, groups).astype(F32)
    mine_b = mine_b.astype(BF16)
    gathered = [mine_b] + [flip_dp(mine_b, 2 * k, groups) for k in range(1, ways)]
    beside = [flip_dp(piece, 1, groups) for piece in gathered]

    grads_a = own_a.astype(F32) + core_swap(after(sent_a, mine_b)).astype(F32)
    low_a = grads_a.astype(BF16)
    other_a = flip_dp(low_a, 1, groups)

    block_out = call(
        join_halves_kernel,
        [where],
        [out_own, core_swap(out_own)],
        [((seqs * length, width), BF16)],
        [dma((2,))],
        2,
        far_outs=(0,),
    )[0].reshape(seqs, length, width)
    input_grad = call(
        widen_halves_kernel,
        [where],
        [grad_own, core_swap(after(grad_own, low_a))],
        [((seqs * length, width), F32)],
        [pltpu.VMEM((4, BLOCK, width), F32), dma((4,))],
        4,
        far_outs=(0,),
    )[0].reshape(seqs, length, width)

    works = {1: [beside[0], block_out, input_grad], 2: [beside[1]]}
    other_a = after(other_a, *works[1])
    bit = 2
    while bit < groups:
        low_a = (low_a.astype(F32) + other_a.astype(F32)).astype(BF16)
        if bit == 2:
            low_a = after(low_a, *gathered)
        other_a = flip_dp(low_a, bit, groups)
        if bit in works:
            other_a = after(other_a, *works[bit])
        bit *= 2

    state_shape = ((per_s, width), F32)
    finished = call(
        functools.partial(finish_kernel, ways=ways),
        [where],
        [*gathered, *beside, low_a, other_a, in_real.T, in_imag.T, line(nu_log), line(theta_log)],
        [((1, width), F32)] * 3
        + [state_shape] * 2
        + [((1, per_s), F32)] * 3
        + [state_shape] * 2
        + [((width, per_f), F32)] * 2
        + [((per_f, width), F32)],
        [
            pltpu.VMEM((pack_rows, width), F32),
            pltpu.VMEM(a_shape, F32),
            pltpu.VMEM((3, 1, per_s), F32),
            pltpu.VMEM((2, 1, per_s), F32),
            dma((13,)),
            dma((2,)),
        ],
        8,
        far_inputs=(groups + 4, groups + 5),
        far_outs=range(13),
    )
    vectors, in_grads, logs = finished[:3], finished[3:5], finished[5:8]
    return (
        block_out,
        input_grad,
        *[v.reshape(width) for v in vectors],
        *[v.T for v in in_grads],
        *finished[8:10],
        *[v.reshape(per_s) for v in logs],
        *finished[10:],
    )


def solution(mesh):
    rows = P(None, "dp", None)
    columns = P(None, "tensor")
    lines = P("tensor", None)
    vector = P("tensor")
    in_specs = (rows, rows, P(), P(), P(), columns, columns, lines, lines, vector, vector, vector, columns, columns, lines, P())
    out_specs = (rows, rows, P(), P(), P(), columns, columns, lines, lines, vector, vector, vector, columns, columns, lines)
    return jax.shard_map(
        functools.partial(shards, groups=mesh.shape["dp"]),
        mesh=mesh,
        in_specs=in_specs,
        out_specs=out_specs,
        check_vma=False,
    )
```

```python
import functools
import math

import jax
import jax.numpy as jnp
from jax import lax
from jax.experimental import pallas as pl
from jax.experimental.pallas import tpu as pltpu
from jax.sharding import PartitionSpec as P

EPSILON = 1e-05
TENSOR = 4
TILE = 8
BLOCK = 256
LARGE = 512
PARAM_ROWS = 16
F32 = jnp.float32
BF16 = jnp.bfloat16
GELU_K = math.sqrt(2.0 / math.pi)
MIB = 1024 * 1024


def dot(left, right):
    return jnp.dot(left, right, preferred_element_type=F32)


def dot_nt(left, right):
    return lax.dot_general(left, right, (((1,), (1,)), ((), ())), preferred_element_type=F32)


def dot_tn(left, right):
    return lax.dot_general(left, right, (((0,), (0,)), ((), ())), preferred_element_type=F32)


def layer_norm(rows):
    centre = jnp.mean(rows, axis=-1, keepdims=True)
    shifted = rows - centre
    variance = jnp.mean(shifted * shifted, axis=-1, keepdims=True)
    inv_scale = lax.rsqrt(variance + EPSILON)
    return shifted * inv_scale, inv_scale


def cmul(ar, ai, br, bi):
    return ar * br - ai * bi, ar * bi + ai * br


def read_params(packs, row):
    total = None
    for pack in packs:
        rows = pack[row : row + PARAM_ROWS, :].astype(F32)
        total = rows if total is None else total + rows
    states = total.shape[1] // 2
    at = lambda k: total[k : k + 1, :states] + total[k + 3 : k + 4, :states] + total[k + 6 : k + 7, :states]
    return at(0), at(1), at(2)


def powers_of(decay_real, decay_imag, exponent):
    out_r = jnp.ones(exponent.shape, F32)
    out_i = jnp.zeros(exponent.shape, F32)
    br, bi = decay_real, decay_imag
    for bit in range(4):
        mr, mi = cmul(out_r, out_i, br, bi)
        on = ((exponent >> bit) & 1) == 1
        out_r = jnp.where(on, mr, out_r)
        out_i = jnp.where(on, mi, out_i)
        br, bi = cmul(br, bi, br, bi)
    return out_r, out_i


def fill_steps(decay_real, decay_imag, backwards, step_ref):
    states = decay_real.shape[1]
    row = lax.broadcasted_iota(jnp.int32, (TILE, states), 0)
    if backwards:
        row = TILE - 1 - row
    zero = jnp.zeros((TILE, states), F32)
    for k, shift in enumerate((1, 2, 4)):
        pr, pi = powers_of(decay_real, decay_imag, jnp.full((TILE, states), shift, jnp.int32))
        step_ref[k, 0] = jnp.where(row >= shift, pr, zero)
        step_ref[k, 1] = jnp.where(row >= shift, pi, zero)
    step_ref[3, 0], step_ref[3, 1] = powers_of(decay_real, decay_imag, row + 1)


def fill_powers(decay_real, decay_imag, backwards, first, full_ref):
    states = decay_real.shape[1]
    row = lax.broadcasted_iota(jnp.int32, (TILE, states), 0)
    if backwards:
        row = TILE - 1 - row
    pr, pi = powers_of(decay_real, decay_imag, row + first)
    er, ei = powers_of(decay_real, decay_imag, jnp.full((TILE, states), TILE, jnp.int32))
    tiles = full_ref.shape[1] // TILE
    for n in range(tiles):
        at = (tiles - 1 - n if backwards else n) * TILE
        full_ref[0, at : at + TILE, :] = pr
        full_ref[1, at : at + TILE, :] = pi
        pr, pi = cmul(pr, pi, er, ei)


def scan_block(drive_ref, out_ref, step_ref, length, backwards):
    rows, lanes = drive_ref.shape
    states = lanes // 2
    tiles = length // TILE
    table = [(step_ref[k, 0], step_ref[k, 1]) for k in range(4)]
    edge = 0 if backwards else TILE - 1
    for s in range(rows // length):
        cr = ci = None
        for n in range(tiles):
            at = s * length + (tiles - 1 - n if backwards else n) * TILE
            hr = drive_ref[at : at + TILE, :states]
            hi = drive_ref[at : at + TILE, states:]
            for k, shift in enumerate((1, 2, 4)):
                turn = TILE - shift if backwards else shift
                sr = pltpu.roll(hr, turn, 0)
                si = pltpu.roll(hi, turn, 0)
                mr, mi = cmul(table[k][0], table[k][1], sr, si)
                hr, hi = hr + mr, hi + mi
            if cr is not None:
                mr, mi = cmul(table[3][0], table[3][1], cr, ci)
                hr, hi = hr + mr, hi + mi
            out_ref[at : at + TILE, :states] = hr
            out_ref[at : at + TILE, states:] = hi
            cr, ci = hr[edge : edge + 1], hi[edge : edge + 1]


def each_block(rows, size, body):
    def step(block, carry):
        at = pl.multiple_of(block * size, size)
        body(block, lambda ref: ref.at[pl.ds(at, size), :])
        return carry

    lax.fori_loop(0, rows // size, step, 0)


def fetch(pairs, sems):
    copies = [pltpu.make_async_copy(src, dst, sems.at[n]) for n, (src, dst) in enumerate(pairs)]
    for copy in copies:
        copy.start()
    for copy in copies:
        copy.wait()


def half_copies(where_ref, src, dst, sems):
    rows = dst.shape[0]
    first = where_ref[1] * rows
    return [
        pltpu.make_async_copy(
            src.at[pl.ds(pl.multiple_of(first + n * BLOCK, BLOCK), BLOCK), :],
            dst.at[pl.ds(n * BLOCK, BLOCK), :],
            sems.at[n],
        )
        for n in range(rows // BLOCK)
    ]


def incoming(far_refs, beside_ref, odd, powers_ref, backwards, out_ref):
    states = out_ref.shape[1] // 2
    early, late = slice(0, states), slice(states, None)
    sr, si = far_refs[0][:, early], far_refs[0][:, late]
    for k in range(1, len(far_refs)):
        row = slice(4 + k, 5 + k)
        mr, mi = cmul(powers_ref[row, early], powers_ref[row, late], far_refs[k][:, early], far_refs[k][:, late])
        sr, si = sr + mr, si + mi
    mr, mi = cmul(powers_ref[0:1, early], powers_ref[0:1, late], sr, si)
    second = odd == (0 if backwards else 1)
    out_ref[:, early] = jnp.where(second, mr + beside_ref[:, early], sr)
    out_ref[:, late] = jnp.where(second, mi + beside_ref[:, late], si)


def join_kernel(mine_ref, other_ref, powers_ref, out_ref, *, row):
    states = out_ref.shape[1] // 2
    early, late = slice(0, states), slice(states, None)
    row = slice(row, row + 1)
    mr, mi = cmul(powers_ref[row, early], powers_ref[row, late], other_ref[:, early], other_ref[:, late])
    out_ref[:, early] = mine_ref[:, early] + mr
    out_ref[:, late] = mine_ref[:, late] + mi


def pair_kernel(where_ref, mine_ref, other_ref, powers_ref, out_ref, *, backwards):
    states = out_ref.shape[1] // 2
    second = where_ref[0] % 2 == (0 if backwards else 1)
    lr, li = powers_ref[0:1, :states], powers_ref[0:1, states:]
    pick = lambda first, part: jnp.where(second == first, other_ref[:, part], mine_ref[:, part])
    early, late = slice(0, states), slice(states, None)
    mr, mi = cmul(lr, li, pick(True, early), pick(True, late))
    out_ref[:, :states] = mr + pick(False, early)
    out_ref[:, states:] = mi + pick(False, late)


def assemble_input(packs, shard, out_ref):
    per = packs[0].shape[0] - PARAM_ROWS
    half = per // 2
    states = out_ref.shape[0] // 2
    for k, pack in enumerate(packs):
        at = pl.multiple_of((shard ^ k) * half, half)
        out_ref[pl.ds(at, half), :] = pack[:half, :]
        out_ref[pl.ds(states + at, half), :] = pack[half:per, :]


def input_pack_kernel(where_ref, in_real, in_imag, nu, theta, gamma, a_ref, logs, sems):
    per_s, width = in_real.shape
    fetch(
        [(in_real, a_ref.at[pl.ds(0, per_s), :]), (in_imag, a_ref.at[pl.ds(per_s, per_s), :])]
        + [(ref, logs.at[n]) for n, ref in enumerate((nu, theta, gamma))],
        sems,
    )
    modulus = jnp.exp(-jnp.exp(logs[0]))
    angle = jnp.exp(logs[1])
    rest = [modulus * jnp.cos(angle), modulus * jnp.sin(angle), jnp.exp(logs[2])]
    rows = []
    for _ in range(3):
        for n in range(3):
            high = rest[n].astype(BF16).astype(F32)
            rows.append(high)
            rest[n] = rest[n] - high
    table = jnp.concatenate(rows + [jnp.zeros((PARAM_ROWS - 9, per_s), F32)], axis=0)
    table = jnp.concatenate([table] * (width // per_s), axis=1)
    here = lax.broadcasted_iota(jnp.int32, (PARAM_ROWS, width), 1) // per_s == where_ref[2]
    a_ref[2 * per_s :, :] = jnp.where(here, table, 0.0).astype(BF16)


def weight_pack_kernel(out_real, out_imag, up, gate, down, b_ref, g_ref, sems):
    per_s, per_f = out_real.shape[0], down.shape[0]
    fetch(
        [
            (out_real, b_ref.at[pl.ds(0, per_s), :]),
            (out_imag, b_ref.at[pl.ds(per_s, per_s), :]),
            (down, b_ref.at[pl.ds(2 * per_s, per_f), :]),
            (up, g_ref.at[:, pl.ds(0, per_f)]),
            (gate, g_ref.at[:, pl.ds(per_f, per_f)]),
        ],
        sems,
    )


def mask_rows(lens_ref, where_ref, seq, seqs, length, width):
    left = lens_ref[where_ref[1] * seqs + seq] - where_ref[0] * length
    return lax.broadcasted_iota(jnp.int32, (length, width), 0) < left


def norm_kernel(
    where_ref, tok_all, cot_all, gain_all, bias_all, lens_all, low_ref, normed_ref, inv_ref, cotm_ref,
    tok, cot, gain_ref, bias_ref, lens_ref, sems, small_sems, *, length
):
    rows, width = low_ref.shape
    per_block = BLOCK // length
    halves = [half_copies(where_ref, src, dst, sems.at[n]) for n, (src, dst) in enumerate(((tok_all, tok), (cot_all, cot)))]
    for copies in zip(*halves):
        for copy in copies:
            copy.start()
    fetch([(gain_all, gain_ref), (bias_all, bias_ref), (lens_all, lens_ref)], small_sems)
    for block, copies in enumerate(zip(*halves)):
        for copy in copies:
            copy.wait()
        span = slice(block * BLOCK, (block + 1) * BLOCK)
        normed, inv_scale = layer_norm(tok[span, :].astype(F32))
        normed_ref[span, :] = normed
        inv_ref[span, :] = jnp.broadcast_to(inv_scale, (BLOCK, inv_ref.shape[1]))
        low_ref[span, :] = (normed * gain_ref[...] + bias_ref[...]).astype(BF16)
        for s in range(per_block):
            seq = block * per_block + s
            span = slice(seq * length, (seq + 1) * length)
            live = mask_rows(lens_ref, where_ref, seq, rows // length, length, width)
            cotm_ref[span, :] = jnp.where(live, cot[span, :].astype(F32), 0.0).astype(BF16)


def weighted_ends(drive_ref, weigh, length, first, ends_ref):
    rows, lanes = drive_ref.shape
    states = lanes // 2
    for s in range(rows // length):
        er = ei = jnp.zeros((TILE, states), F32)
        for n in range(length // TILE):
            at = s * length + n * TILE
            mr, mi = cmul(
                weigh[0, n * TILE : (n + 1) * TILE, :],
                weigh[1, n * TILE : (n + 1) * TILE, :],
                drive_ref[at : at + TILE, :states],
                drive_ref[at : at + TILE, states:],
            )
            er, ei = er + mr, ei + mi
        ends_ref[pl.ds(first + s, 1), :states] = jnp.sum(er, axis=0, keepdims=True)
        ends_ref[pl.ds(first + s, 1), states:] = jnp.sum(ei, axis=0, keepdims=True)


def drive_kernel(where_ref, low_all, a0, a1, a2, a3, drive_all, ends_ref, powers_ref, in_t, weigh, *, length):
    packs = (a0, a1, a2, a3)
    states = in_t.shape[0] // 2
    assemble_input(packs, where_ref[2], in_t)
    dr, di, gain = read_params(packs, a0.shape[0] - PARAM_ROWS)
    fill_powers(dr, di, True, 0, weigh)
    gam = jnp.concatenate([gain, gain], axis=1)
    lr, li = cmul(weigh[0, :1, :], weigh[1, :1, :], dr, di)
    rows = [(lr, li)] + [cmul(lr, li, lr, li)]
    for _ in range(2):
        rows.append(cmul(*rows[-1], *rows[-1]))
    rows.append((jnp.ones_like(lr), jnp.zeros_like(lr)))
    for _ in range(3):
        rows.append(cmul(*cmul(*rows[-1], *rows[-1]), *rows[1]))
    for k, (lr, li) in enumerate(rows):
        powers_ref[k : k + 1, :] = jnp.concatenate([lr, li], axis=1)
    per_block = LARGE // length

    def body(block, view):
        low_ref, drive_ref = view(low_all), view(drive_all)
        drive_ref[...] = dot_nt(low_ref[...], in_t[...]) * gam
        weighted_ends(drive_ref, weigh, length, block * per_block, ends_ref)

    each_block(low_all.shape[0], LARGE, body)


def scan_kernel(drive_all, a0, a1, a2, a3, local_all, step, *, length, backwards):
    dr, di, _ = read_params((a0, a1, a2, a3), a0.shape[0] - PARAM_ROWS)
    fill_steps(dr, di, backwards, step)
    each_block(
        drive_all.shape[0],
        BLOCK,
        lambda block, view: scan_block(view(drive_all), view(local_all), step, length, backwards),
    )


def hidden_kernel(where_ref, cotm_all, b0, b1, b2, b3, hg_all, *, per_s):
    shard = where_ref[2]
    per_f = hg_all.shape[1] // TENSOR

    def body(block, view):
        hg_ref, cotm = view(hg_all), view(cotm_all)[...]
        for k, pack in enumerate((b0, b1, b2, b3)):
            at = pl.multiple_of((shard ^ k) * per_f, per_f)
            hg_ref[:, pl.ds(at, per_f)] = dot_nt(cotm, pack[2 * per_s :, :]).astype(BF16)

    each_block(cotm_all.shape[0], LARGE, body)


def middle_kernel(where_ref, *refs, length, levels):
    far_refs, refs = refs[:levels], refs[levels:]
    beside_ref, powers_ref, local_all, normed_all, hg_all, cotm_all, a0, a1, a2, a3 = refs[:10]
    gain_ref, bias_ref, skip_ref, b0, b1, b2, b3, g0, g1, g2, g3 = refs[10:21]
    state_all, back_all, backends_ref, ylow_all, hid_all, act_all, ul_all = refs[21:28]
    c_all, ug_all, weigh, full, carry, sems = refs[28:]
    place, core, shard = where_ref[0], where_ref[1], where_ref[2]
    states = c_all.shape[0] // 2
    rows, width = normed_all.shape
    per_block = LARGE // length
    per_s = states // TENSOR
    per_f = hid_all.shape[1] // TENSOR

    copies = []
    for k, (pack, gates) in enumerate(((b0, g0), (b1, g1), (b2, g2), (b3, g3))):
        t = shard ^ k
        moves = (
            (pack.at[pl.ds(0, per_s), :], c_all.at[pl.ds(pl.multiple_of(t * per_s, per_s), per_s), :]),
            (pack.at[pl.ds(per_s, per_s), :], c_all.at[pl.ds(pl.multiple_of(states + t * per_s, per_s), per_s), :]),
            (gates, ug_all.at[:, pl.ds(pl.multiple_of(t * 2 * per_f, 2 * per_f), 2 * per_f)]),
        )
        for n, (src, dst) in enumerate(moves):
            copies.append(pltpu.make_async_copy(src, dst, sems.at[k, n]))
    for copy in copies:
        copy.start()
    dr, di, _ = read_params((a0, a1, a2, a3), a0.shape[0] - PARAM_ROWS)
    fill_powers(dr, di, False, 1, full)
    incoming(far_refs, beside_ref, place % 2, powers_ref, False, carry)
    fill_powers(dr, di, False, 0, weigh)
    for copy in copies:
        copy.wait()
    skip = skip_ref[...]
    skip_gain, skip_bias = gain_ref[...] * skip, bias_ref[...] * skip

    def body(block, view):
        local_ref, state_ref, hid_ref, ylow_ref = view(local_all), view(state_all), view(hid_all), view(ylow_all)
        hg_ref, act_ref, back_ref, ul = view(hg_all), view(act_all), view(back_all), view(ul_all)
        for s in range(per_block):
            seq = block * per_block + s
            span = slice(s * length, (s + 1) * length)
            sr = carry[pl.ds(seq, 1), :states]
            si = carry[pl.ds(seq, 1), states:]
            mr, mi = cmul(full[0], full[1], sr, si)
            state_ref[span, :states] = (local_ref[span, :states] + mr).astype(BF16)
            state_ref[span, states:] = (-(local_ref[span, states:] + mi)).astype(BF16)
        y = dot(state_ref[...], c_all[...]) + (view(normed_all)[...] * skip_gain + skip_bias)
        square = y * y
        th = jnp.tanh(y * (GELU_K + (GELU_K * 0.044715) * square))
        half_y = 0.5 * y
        act_ref[...] = (half_y + half_y * th).astype(BF16)
        slope = (0.5 + 0.5 * th) + half_y * (1.0 - th * th) * (GELU_K + (GELU_K * 3 * 0.044715) * square)
        act = act_ref[...]
        for t in range(TENSOR):
            both = dot(act, ug_all[:, 2 * per_f * t : 2 * per_f * (t + 1)])
            up = both[:, :per_f]
            th = 0.5 * jnp.tanh(0.5 * both[:, per_f:])
            sig = 0.5 + th
            hid_ref[:, per_f * t : per_f * (t + 1)] = (up * sig).astype(BF16)
            up_grad = hg_ref[:, per_f * t : per_f * (t + 1)].astype(F32) * sig
            ul[:, 2 * per_f * t : 2 * per_f * t + per_f] = up_grad.astype(BF16)
            ul[:, 2 * per_f * t + per_f : 2 * per_f * (t + 1)] = (up_grad * up * (0.5 - th)).astype(BF16)
        y_grad = dot_nt(ul[...], ug_all[...]) * slope
        ylow_ref[...] = y_grad.astype(BF16)
        back_ref[...] = dot_nt(ylow_ref[...], c_all[...])
        weighted_ends(back_ref, weigh, length, block * per_block, backends_ref)

    each_block(rows, LARGE, body)


def weight_kernel(where_ref, hid_ref, cotm_ref, act_ref, ul_ref, state_ref, ylow_ref, own_ref, sent_ref):
    core, side = where_ref[1], where_ref[2] // 2
    states = state_ref.shape[1] // 2
    per_s = states // TENSOR
    per_f = hid_ref.shape[1] // TENSOR
    width = act_ref.shape[1]
    cols = [
        state_ref[:, pl.ds(pl.multiple_of(k * states + side * 2 * per_s, 2 * per_s), 2 * per_s)] for k in range(2)
    ]
    out_grad = dot_tn(jnp.concatenate(cols, axis=1), ylow_ref[...])
    act, cotm = act_ref[...], cotm_ref[...]
    for n, ref in ((1 - core, sent_ref), (core, own_ref)):
        ul = ul_ref[:, pl.ds(pl.multiple_of((2 * side + n) * 2 * per_f, 2 * per_f), 2 * per_f)]
        ref[2 * per_s + per_f : 2 * per_s + per_f + width, :] = dot_tn(act, ul).astype(ref.dtype)
        hid = hid_ref[:, pl.ds(pl.multiple_of((2 * side + n) * per_f, per_f), per_f)]
        ref[2 * per_s : 2 * per_s + per_f, :] = dot_tn(hid, cotm).astype(ref.dtype)
        for k in range(2):
            at = 2 * per_s * k
            part = jnp.where(n == 0, out_grad[at : at + per_s, :], out_grad[at + per_s : at + 2 * per_s, :])
            ref[k * per_s : (k + 1) * per_s, :] = part.astype(ref.dtype)


def down_kernel(where_ref, lens_ref, tok_all, hid_all, b0, b1, b2, b3, out_all, down_all, tok, sems, *, length, per_s):
    shard = where_ref[2]
    rows, width = out_all.shape
    per_block = LARGE // length
    per_f = down_all.shape[0] // TENSOR
    copies = half_copies(where_ref, tok_all, tok, sems)
    for copy in copies:
        copy.start()
    for k, pack in enumerate((b0, b1, b2, b3)):
        down_all[pl.ds(pl.multiple_of((shard ^ k) * per_f, per_f), per_f), :] = pack[2 * per_s :, :]
    for copy in copies:
        copy.wait()

    def body(block, view):
        added = dot(view(hid_all)[...], down_all[...])
        out_ref, tok_ref = view(out_all), view(tok)
        for s in range(per_block):
            span = slice(s * length, (s + 1) * length)
            live = mask_rows(lens_ref, where_ref, block * per_block + s, rows // length, length, width)
            out_ref[span, :] = jnp.where(live, tok_ref[span, :].astype(F32) + added[span, :], 0.0).astype(BF16)

    each_block(rows, LARGE, body)


def last_kernel(where_ref, *refs, length, levels):
    far_refs, refs = refs[:levels], refs[levels:]
    beside_ref, powers_ref, low_all, normed_all, inv_all, cotm_all, back_all, state_all, ylow_all = refs[:9]
    a0, a1, a2, a3, gain_ref, bias_ref, skip_ref, grad_all, own_ref, sent_ref = refs[9:19]
    in_t, full, carry, dlow, in_grad, lam_grad, vec_grad = refs[19:]
    place, core, shard = where_ref[0], where_ref[1], where_ref[2]
    states = in_t.shape[0] // 2
    rows, width = low_all.shape
    per_block = BLOCK // length
    per_s = states // TENSOR
    packs = (a0, a1, a2, a3)

    assemble_input(packs, shard, in_t)
    dr, di, gain = read_params(packs, a0.shape[0] - PARAM_ROWS)
    fill_powers(dr, di, True, 1, full)
    incoming(far_refs, beside_ref, place % 2, powers_ref, True, carry)
    in_grad[...] = jnp.zeros(in_grad.shape, F32)
    lam_grad[...] = jnp.zeros(lam_grad.shape, F32)
    vec_grad[...] = jnp.zeros(vec_grad.shape, F32)
    at = pl.multiple_of((shard // 2) * 2 * per_s, 2 * per_s)

    def body(block, view):
        back_ref, state_ref = view(back_all), view(state_all)
        for s in range(per_block):
            seq = block * per_block + s
            span = slice(s * length, (s + 1) * length)
            sr = carry[pl.ds(seq, 1), :states]
            si = carry[pl.ds(seq, 1), states:]
            mr, mi = cmul(full[0], full[1], sr, si)
            gr = back_ref[span, :states] + mr
            gi = back_ref[span, states:] + mi
            dlow[span, :states] = (gr * gain).astype(BF16)
            dlow[span, states:] = (gi * -gain).astype(BF16)
            nr = jnp.concatenate([gr[1:], sr], axis=0)
            ni = jnp.concatenate([gi[1:], si], axis=0)
            hr = state_ref[span, :states].astype(F32)
            hi = state_ref[span, states:].astype(F32)
            lam_grad[:, :states] += jnp.sum(nr * hr + ni * hi, axis=0, keepdims=True)
            lam_grad[:, states:] += jnp.sum(nr * hi - ni * hr, axis=0, keepdims=True)
        normed = view(normed_all)[...]
        ylow = view(ylow_all)[...].astype(F32)
        low = view(low_all)[...]
        u_grad = dot(dlow[...], in_t[...]) + ylow * skip_ref[...]
        vec_grad[0:1, :] += jnp.sum(u_grad * normed, axis=0, keepdims=True)
        vec_grad[1:2, :] += jnp.sum(u_grad, axis=0, keepdims=True)
        vec_grad[2:3, :] += jnp.sum(ylow * (normed * gain_ref[...] + bias_ref[...]), axis=0, keepdims=True)
        scaled = u_grad * gain_ref[...]
        grad = (
            scaled
            - jnp.mean(scaled, axis=-1, keepdims=True)
            - normed * jnp.mean(scaled * normed, axis=-1, keepdims=True)
        )
        view(grad_all)[...] = (view(cotm_all)[...].astype(F32) + view(inv_all)[:, :1] * grad).astype(BF16)
        for k in range(2):
            cols = dlow[:, pl.ds(k * states + at, 2 * per_s)]
            in_grad[2 * per_s * k : 2 * per_s * (k + 1), :] += dot_tn(cols, low)

    each_block(rows, BLOCK, body)
    small = jnp.concatenate(
        [vec_grad[:3, :], lam_grad[...], jnp.zeros((PARAM_ROWS - 4, width), F32)], axis=0
    ).astype(BF16)
    for n, ref in ((core, own_ref), (1 - core, sent_ref)):
        for k in range(2):
            part = in_grad[pl.ds(pl.multiple_of(2 * per_s * k + n * per_s, per_s), per_s), :]
            ref[k * per_s : (k + 1) * per_s, :] = part.astype(BF16)
        ref[2 * per_s :, :] = small


def join_halves_kernel(where_ref, own_ref, other_ref, out_ref, sems):
    rows = own_ref.shape[0]
    copies = [
        pltpu.make_async_copy(ref, out_ref.at[pl.ds(pl.multiple_of(n * rows, BLOCK), rows), :], sems.at[k])
        for k, (n, ref) in enumerate(((where_ref[1], own_ref), (1 - where_ref[1], other_ref)))
    ]
    for copy in copies:
        copy.start()
    for copy in copies:
        copy.wait()


def widen_halves_kernel(where_ref, own_ref, other_ref, out_ref, wide, sems):
    rows = own_ref.shape[0]
    slots = wide.shape[0]
    flying = []
    for n in range(2 * rows // BLOCK):
        slot = n % slots
        if n >= slots:
            flying[n - slots].wait()
        at = (n // 2) * BLOCK
        half, ref = ((where_ref[1], own_ref), (1 - where_ref[1], other_ref))[n % 2]
        wide[slot] = ref[at : at + BLOCK, :].astype(F32)
        copy = pltpu.make_async_copy(
            wide.at[slot], out_ref.at[pl.ds(pl.multiple_of(half * rows + at, BLOCK), BLOCK), :], sems.at[slot]
        )
        copy.start()
        flying.append(copy)
    for copy in flying[-slots:]:
        copy.wait()


def fold_kernel(where_ref, own_ref, other_ref, keep_ref, send_ref):
    half = keep_ref.shape[0]
    odd = where_ref[0] % 2
    at = pl.multiple_of(odd * half, 16)
    keep_ref[...] = own_ref[pl.ds(at, half), :] + other_ref[pl.ds(at, half), :].astype(F32)
    at = pl.multiple_of((1 - odd) * half, 16)
    send_ref[...] = (own_ref[pl.ds(at, half), :] + other_ref[pl.ds(at, half), :].astype(F32)).astype(BF16)


def deal_kernel(where_ref, own_ref, other_ref, keep_ref, *send_refs):
    rows = keep_ref.shape[0]
    for k, ref in enumerate((keep_ref,) + send_refs):
        at = pl.multiple_of(((where_ref[0] // 2) ^ k) * rows, 16)
        ref[...] = (own_ref[pl.ds(at, rows), :] + other_ref[pl.ds(at, rows), :].astype(F32)).astype(ref.dtype)


def unpack_kernel(where_ref, *refs, ways):
    parts, (real_ref, imag_ref, up_ref, gate_ref, down_ref, total, sems) = refs[: ways + 2], refs[ways + 2 :]
    place = where_ref[0]
    rows = parts[0].shape[0]
    for n in range(2 * ways):
        k = n % ways
        half = place % 2 if n < ways else 1 - place % 2
        at = (half * ways + ((place // 2) ^ k)) * rows
        if n <= ways:
            part = parts[n][...]
        else:
            part = parts[-1][(k - 1) * rows : k * rows, :]
        total[pl.ds(pl.multiple_of(at, 16), rows), :] = part.astype(F32)
    per_s, per_f, width = real_ref.shape[0], down_ref.shape[0], up_ref.shape[0]
    first = 2 * per_s + per_f
    moves = [
        (total.at[pl.ds(first, width), pl.ds(0, per_f)], up_ref),
        (total.at[pl.ds(first, width), pl.ds(per_f, per_f)], gate_ref),
        (total.at[pl.ds(2 * per_s, per_f), :], down_ref),
        (total.at[pl.ds(0, per_s), :], real_ref),
        (total.at[pl.ds(per_s, per_s), :], imag_ref),
    ]
    fetch(moves, sems)


def finish_kernel(where_ref, mine_ref, other_ref, a_ref, logs_ref, *refs):
    outs, (grads_ref, logs, sems) = refs[:8], refs[8:]
    width = grads_ref.shape[1]
    per_s = logs_ref.shape[2]
    grads = mine_ref[...].astype(F32) + other_ref[...].astype(F32)
    grads_ref[...] = grads
    lam = [jnp.zeros((1, per_s), F32), jnp.zeros((1, per_s), F32)]
    for t in range(TENSOR):
        for n in range(2):
            at = (n * TENSOR + t) * per_s
            part = grads[2 * per_s + 3 : 2 * per_s + 4, at : at + per_s]
            lam[n] = jnp.where(where_ref[2] == t, part, lam[n])
    decay = jnp.exp(logs_ref[0])
    modulus = jnp.exp(-decay)
    angle = jnp.exp(logs_ref[1])
    cos, sin = jnp.cos(angle), jnp.sin(angle)
    logs[0] = -decay * modulus * (lam[0] * cos + lam[1] * sin)
    logs[1] = angle * modulus * (lam[1] * cos - lam[0] * sin)
    terms = a_ref[:per_s, :].astype(F32) * grads[:per_s, :] + a_ref[per_s : 2 * per_s, :].astype(F32) * grads[per_s : 2 * per_s, :]
    logs[2] = jnp.sum(terms.T, axis=0, keepdims=True)
    moves = [(grads_ref.at[pl.ds(2 * per_s + n, 1), :], outs[n]) for n in range(3)]
    moves += [(grads_ref.at[pl.ds(n * per_s, per_s), :], outs[3 + n]) for n in range(2)]
    moves += [(logs.at[n], outs[5 + n]) for n in range(3)]
    fetch(moves, sems)


def near(value):
    return pltpu.with_memory_space_constraint(value, pltpu.VMEM)


def call(kernel, scalars, inputs, outs, scratch, vmem, far_inputs=(), far_outs=()):
    here, anywhere = pl.BlockSpec(memory_space=pltpu.VMEM), pl.BlockSpec(memory_space=pl.ANY)
    single = not isinstance(outs, list)
    listed = [outs] if single else outs
    shapes = [
        jax.ShapeDtypeStruct(*out) if n in far_outs else pltpu.VMEM(*out) for n, out in enumerate(listed)
    ]
    out_specs = [anywhere if n in far_outs else here for n in range(len(listed))]
    return pl.pallas_call(
        kernel,
        in_specs=[pl.BlockSpec(memory_space=pltpu.SMEM)] * len(scalars)
        + [anywhere if n in far_inputs else here for n in range(len(inputs))],
        out_specs=out_specs[0] if single else out_specs,
        out_shape=shapes[0] if single else shapes,
        scratch_shapes=scratch,
        compiler_params=pltpu.CompilerParams(vmem_limit_bytes=vmem * MIB),
    )(
        *scalars,
        *[
            pltpu.with_memory_space_constraint(v, pltpu.HBM) if n in far_inputs else near(v)
            for n, v in enumerate(inputs)
        ],
    )


def core_swap(value):
    return lax.ppermute(value, "tensor", [(t, t ^ 1) for t in range(TENSOR)])


def side_swap(value):
    return lax.ppermute(value, "tensor", [(t, t ^ 2) for t in range(TENSOR)])


def gather_tensor(own, *first):
    across = after(side_swap(own), *first)
    return own, core_swap(own), across, core_swap(across)


def after(value, *first):
    return lax.optimization_barrier((value,) + first)[0]


def flip_dp(value, bits, groups):
    return lax.ppermute(value, "dp", [(i, i ^ bits) for i in range(groups)])


def shift_dp(value, by, groups):
    return lax.ppermute(value, "dp", [(i, i + by) for i in range(groups) if 0 <= i + by < groups])


def shards(
    tokens,
    cotangent,
    ln_gain,
    ln_bias,
    skip_gain,
    in_real,
    in_imag,
    out_real,
    out_imag,
    nu_log,
    theta_log,
    gamma_log,
    up_weight,
    gate_weight,
    down_weight,
    lengths,
    *,
    groups,
):
    seqs, length, width = tokens.shape
    per_s = in_real.shape[1]
    per_f = up_weight.shape[1]
    states = per_s * TENSOR
    own_seqs = seqs // 2
    rows = own_seqs * length
    blocks = rows // BLOCK
    place = lax.axis_index("dp").astype(jnp.int32)
    shard = lax.axis_index("tensor").astype(jnp.int32)
    core = shard % 2
    where = jnp.stack([place, core, shard])

    tok_rows = tokens.reshape(seqs * length, width)
    cot_rows = cotangent.reshape(seqs * length, width)
    row = lambda v: v.reshape(1, width)
    gain_row, bias_row, skip_row = row(ln_gain), row(ln_bias), row(skip_gain)
    a_shape = (2 * per_s + PARAM_ROWS, width)
    b_shape = (2 * per_s + per_f, width)
    lanes = 2 * states
    units = TENSOR * per_f
    ends_shape = ((own_seqs, lanes), F32)
    dma = pltpu.SemaphoreType.DMA
    line = lambda v: v.reshape(1, per_s)

    pack_a, logs = call(
        input_pack_kernel,
        [where],
        [in_real.T, in_imag.T, line(nu_log), line(theta_log), line(gamma_log)],
        [(a_shape, BF16), ((3, 1, per_s), F32)],
        [dma((5,))],
        4,
        far_inputs=range(5),
    )
    low, normed, inv, cot_m = call(
        functools.partial(norm_kernel, length=length),
        [where],
        [after(tok_rows, pack_a), cot_rows, gain_row, bias_row, lengths],
        [((rows, width), BF16), ((rows, width), F32), ((rows, 128), F32), ((rows, width), BF16)],
        [
            pltpu.VMEM((rows, width), BF16),
            pltpu.VMEM((rows, width), BF16),
            pltpu.VMEM((1, width), F32),
            pltpu.VMEM((1, width), F32),
            pltpu.SMEM((seqs,), jnp.int32),
            dma((2, blocks)),
            dma((3,)),
        ],
        8,
        far_inputs=range(5),
    )
    packs_a = gather_tensor(pack_a, low)
    pack_b, pack_g = call(
        weight_pack_kernel,
        [],
        [after(out_real, packs_a[2]), out_imag, up_weight, gate_weight, down_weight],
        [(b_shape, BF16), ((width, 2 * per_f), BF16)],
        [dma((5,))],
        4,
        far_inputs=range(5),
    )
    drive, ends, powers = call(
        functools.partial(drive_kernel, length=length),
        [where],
        [low, *packs_a],
        [((rows, lanes), F32), ends_shape, ((TILE, lanes), F32)],
        [pltpu.VMEM((lanes, width), BF16), pltpu.VMEM((2, length, states), F32)],
        8,
    )
    local = call(
        functools.partial(scan_kernel, length=length, backwards=False),
        [],
        [drive, *packs_a],
        ((rows, lanes), F32),
        [pltpu.VMEM((4, 2, TILE, states), F32)],
        8,
    )

    ways = groups // 2
    levels = (ways - 1).bit_length()

    def exchange(mine, backwards, beside_work, first_work=None):
        beside = after(flip_dp(mine, 1, groups), beside_work)
        both = call(
            functools.partial(pair_kernel, backwards=backwards), [where], [mine, beside, powers], ends_shape, [], 2
        )
        found = [both]
        from_far = []
        for k in range(levels):
            step = 2 << k
            from_far.append(shift_dp(found[-1], -step if backwards else step, groups))
            if k == 0 and first_work is not None:
                from_far[0] = after(from_far[0], first_work(both))
            if k + 1 < levels:
                found.append(
                    call(functools.partial(join_kernel, row=1 + k), [], [found[-1], from_far[-1], powers], ends_shape, [], 2)
                )
        return from_far, beside, found

    far_ends, beside_ends, found_ends = exchange(ends, False, local)
    packs_b = gather_tensor(pack_b, far_ends[0])
    hid_grad = call(
        functools.partial(hidden_kernel, per_s=per_s),
        [where],
        [after(cot_m, found_ends[-1]), *packs_b],
        ((rows, units), BF16),
        [],
        8,
    )
    packs_g = gather_tensor(pack_g, hid_grad, *far_ends)

    pack_rows = -(-(2 * per_s + per_f + width) // (16 * groups)) * 16 * groups
    state, back_drive, back_ends, y_low, hid, act, ul = call(
        functools.partial(middle_kernel, length=length, levels=levels),
        [where],
        [
            *far_ends,
            beside_ends,
            powers,
            local,
            normed,
            hid_grad,
            cot_m,
            *packs_a,
            gain_row,
            bias_row,
            skip_row,
            *packs_b,
            *packs_g,
        ],
        [
            ((rows, lanes), BF16),
            ((rows, lanes), F32),
            ends_shape,
            ((rows, width), BF16),
            ((rows, units), BF16),
            ((rows, width), BF16),
            ((rows, 2 * units), BF16),
        ],
        [
            pltpu.VMEM((lanes, width), BF16),
            pltpu.VMEM((width, 2 * units), BF16),
            pltpu.VMEM((2, length, states), F32),
            pltpu.VMEM((2, length, states), F32),
            pltpu.VMEM((own_seqs, lanes), F32),
            dma((TENSOR, 3)),
        ],
        16,
    )
    own_b, sent_b = call(
        weight_kernel,
        [where],
        [hid, cot_m, act, ul, state, y_low],
        [((pack_rows, width), F32), ((pack_rows, width), BF16)],
        [],
        10,
    )

    half, part = pack_rows // 2, pack_rows // groups
    made = []

    def scan_work(pair_back):
        made.append(
            call(
                functools.partial(scan_kernel, length=length, backwards=True),
                [],
                [after(back_drive, pair_back), *packs_a],
                ((rows, lanes), F32),
                [pltpu.VMEM((4, 2, TILE, states), F32)],
                8,
            )
        )
        return made[0]

    far_back, beside_back, found_back = exchange(back_ends, True, own_b, scan_work)
    back = made[0]
    keep_b, send_b = call(
        fold_kernel,
        [where],
        [own_b, core_swap(after(sent_b, beside_back))],
        [((half, width), F32), ((half, width), BF16)],
        [],
        4,
    )
    half_b = flip_dp(after(send_b, found_back[0]), 1, groups)
    out_own = call(
        functools.partial(down_kernel, length=length, per_s=per_s),
        [where, lengths],
        [tok_rows, after(hid, found_back[-1]), *packs_b],
        ((rows, width), BF16),
        [pltpu.VMEM((units, width), BF16), pltpu.VMEM((rows, width), BF16), dma((blocks,))],
        8,
        far_inputs=(0,),
    )
    dealt = call(
        deal_kernel,
        [where],
        [after(keep_b, out_own, *far_back), half_b],
        [((part, width), F32)] + [((part, width), BF16)] * (ways - 1),
        [],
        4,
    )

    grad_own, own_a, sent_a = call(
        functools.partial(last_kernel, length=length, levels=levels),
        [where],
        [
            *far_back,
            after(beside_back, dealt[0]),
            powers,
            low,
            normed,
            inv,
            cot_m,
            back,
            state,
            y_low,
            *packs_a,
            gain_row,
            bias_row,
            skip_row,
        ],
        [((rows, width), BF16), (a_shape, BF16), (a_shape, BF16)],
        [
            pltpu.VMEM((lanes, width), BF16),
            pltpu.VMEM((2, length, states), F32),
            pltpu.VMEM((own_seqs, lanes), F32),
            pltpu.VMEM((BLOCK, lanes), BF16),
            pltpu.VMEM((states, width), F32),
            pltpu.VMEM((1, lanes), F32),
            pltpu.VMEM((TILE, width), F32),
        ],
        12,
    )

    mine_b = dealt[0]
    for k in range(1, ways):
        mine_b = mine_b + flip_dp(dealt[k], 2 * k, groups).astype(F32)
    mine_b = mine_b.astype(BF16)
    gathered = [mine_b] + [flip_dp(mine_b, 2 * k, groups) for k in range(1, ways)]
    beside = [flip_dp(mine_b, 1, groups), flip_dp(jnp.concatenate(gathered[1:], axis=0), 1, groups)]

    grads_a = own_a.astype(F32) + core_swap(after(sent_a, mine_b)).astype(F32)
    low_a = grads_a.astype(BF16)

    block_out = call(
        join_halves_kernel,
        [where],
        [out_own, core_swap(out_own)],
        [((seqs * length, width), BF16)],
        [dma((2,))],
        2,
        far_outs=(0,),
    )[0].reshape(seqs, length, width)
    input_grad = call(
        widen_halves_kernel,
        [where],
        [grad_own, core_swap(after(grad_own, low_a))],
        [((seqs * length, width), F32)],
        [pltpu.VMEM((4, BLOCK, width), F32), dma((4,))],
        4,
        far_outs=(0,),
    )[0].reshape(seqs, length, width)

    state_shape = ((per_s, width), F32)
    unpacked = call(
        functools.partial(unpack_kernel, ways=ways),
        [where],
        [*gathered, *beside],
        [state_shape] * 2 + [((width, per_f), F32)] * 2 + [((per_f, width), F32)],
        [pltpu.VMEM((pack_rows, width), F32), dma((5,))],
        8,
        far_outs=range(5),
    )
    works = {1: [block_out], 2: [input_grad, beside[0]], 4: unpacked}
    bit = 1
    while bit < groups:
        other_a = after(flip_dp(low_a, bit, groups), *works.get(bit, []))
        bit *= 2
        if bit < groups:
            low_a = (low_a.astype(F32) + other_a.astype(F32)).astype(BF16)
        if bit == 4:
            low_a = after(low_a, *gathered)

    finished = call(
        finish_kernel,
        [where],
        [low_a, other_a, pack_a, logs],
        [((1, width), F32)] * 3 + [state_shape] * 2 + [((1, per_s), F32)] * 3,
        [pltpu.VMEM(a_shape, F32), pltpu.VMEM((3, 1, per_s), F32), dma((8,))],
        4,
        far_outs=range(8),
    )
    return (
        block_out,
        input_grad,
        *[v.reshape(width) for v in finished[:3]],
        *[v.T for v in finished[3:5]],
        *unpacked[:2],
        *[v.reshape(per_s) for v in finished[5:]],
        *unpacked[2:],
    )


def solution(mesh):
    rows = P(None, "dp", None)
    columns = P(None, "tensor")
    lines = P("tensor", None)
    vector = P("tensor")
    in_specs = (rows, rows, P(), P(), P(), columns, columns, lines, lines, vector, vector, vector, columns, columns, lines, P())
    out_specs = (rows, rows, P(), P(), P(), columns, columns, lines, lines, vector, vector, vector, columns, columns, lines)
    return jax.shard_map(
        functools.partial(shards, groups=mesh.shape["dp"]),
        mesh=mesh,
        in_specs=in_specs,
        out_specs=out_specs,
        check_vma=False,
    )
```

```python
import functools
import math

import jax
import jax.numpy as jnp
from jax import lax
from jax.experimental import pallas as pl
from jax.experimental.pallas import tpu as pltpu
from jax.sharding import PartitionSpec as P

EPSILON = 1e-05
TENSOR = 4
TILE = 8
BLOCK = 256
LARGE = 512
PARAM_ROWS = 16
F32 = jnp.float32
BF16 = jnp.bfloat16
GELU_K = math.sqrt(2.0 / math.pi)
MIB = 1024 * 1024


def dot(left, right):
    return jnp.dot(left, right, preferred_element_type=F32)


def dot_nt(left, right):
    return lax.dot_general(left, right, (((1,), (1,)), ((), ())), preferred_element_type=F32)


def dot_tn(left, right):
    return lax.dot_general(left, right, (((0,), (0,)), ((), ())), preferred_element_type=F32)


def layer_norm(rows):
    centre = jnp.mean(rows, axis=-1, keepdims=True)
    shifted = rows - centre
    variance = jnp.mean(shifted * shifted, axis=-1, keepdims=True)
    inv_scale = lax.rsqrt(variance + EPSILON)
    return shifted * inv_scale, inv_scale


def cmul(ar, ai, br, bi):
    return ar * br - ai * bi, ar * bi + ai * br


def read_params(packs, row):
    total = None
    for pack in packs:
        rows = pack[row : row + PARAM_ROWS, :].astype(F32)
        total = rows if total is None else total + rows
    states = total.shape[1] // 2
    at = lambda k: total[k : k + 1, :states] + total[k + 3 : k + 4, :states] + total[k + 6 : k + 7, :states]
    return at(0), at(1), at(2)


def powers_of(decay_real, decay_imag, exponent):
    out_r = jnp.ones(exponent.shape, F32)
    out_i = jnp.zeros(exponent.shape, F32)
    br, bi = decay_real, decay_imag
    for bit in range(4):
        mr, mi = cmul(out_r, out_i, br, bi)
        on = ((exponent >> bit) & 1) == 1
        out_r = jnp.where(on, mr, out_r)
        out_i = jnp.where(on, mi, out_i)
        br, bi = cmul(br, bi, br, bi)
    return out_r, out_i


def fill_steps(decay_real, decay_imag, backwards, step_ref):
    states = decay_real.shape[1]
    row = lax.broadcasted_iota(jnp.int32, (TILE, states), 0)
    if backwards:
        row = TILE - 1 - row
    zero = jnp.zeros((TILE, states), F32)
    for k, shift in enumerate((1, 2, 4)):
        pr, pi = powers_of(decay_real, decay_imag, jnp.full((TILE, states), shift, jnp.int32))
        step_ref[k, 0] = jnp.where(row >= shift, pr, zero)
        step_ref[k, 1] = jnp.where(row >= shift, pi, zero)
    step_ref[3, 0], step_ref[3, 1] = powers_of(decay_real, decay_imag, row + 1)


def fill_powers(decay_real, decay_imag, backwards, first, full_ref):
    states = decay_real.shape[1]
    row = lax.broadcasted_iota(jnp.int32, (TILE, states), 0)
    if backwards:
        row = TILE - 1 - row
    pr, pi = powers_of(decay_real, decay_imag, row + first)
    er, ei = powers_of(decay_real, decay_imag, jnp.full((TILE, states), TILE, jnp.int32))
    tiles = full_ref.shape[1] // TILE
    for n in range(tiles):
        at = (tiles - 1 - n if backwards else n) * TILE
        full_ref[0, at : at + TILE, :] = pr
        full_ref[1, at : at + TILE, :] = pi
        pr, pi = cmul(pr, pi, er, ei)


def scan_block(drive_ref, out_ref, step_ref, length, backwards):
    rows, lanes = drive_ref.shape
    states = lanes // 2
    tiles = length // TILE
    table = [(step_ref[k, 0], step_ref[k, 1]) for k in range(4)]
    edge = 0 if backwards else TILE - 1
    for s in range(rows // length):
        cr = ci = None
        for n in range(tiles):
            at = s * length + (tiles - 1 - n if backwards else n) * TILE
            hr = drive_ref[at : at + TILE, :states]
            hi = drive_ref[at : at + TILE, states:]
            for k, shift in enumerate((1, 2, 4)):
                turn = TILE - shift if backwards else shift
                sr = pltpu.roll(hr, turn, 0)
                si = pltpu.roll(hi, turn, 0)
                mr, mi = cmul(table[k][0], table[k][1], sr, si)
                hr, hi = hr + mr, hi + mi
            if cr is not None:
                mr, mi = cmul(table[3][0], table[3][1], cr, ci)
                hr, hi = hr + mr, hi + mi
            out_ref[at : at + TILE, :states] = hr
            out_ref[at : at + TILE, states:] = hi
            cr, ci = hr[edge : edge + 1], hi[edge : edge + 1]


def each_block(rows, size, body):
    def step(block, carry):
        at = pl.multiple_of(block * size, size)
        body(block, lambda ref: ref.at[pl.ds(at, size), :])
        return carry

    lax.fori_loop(0, rows // size, step, 0)


def fetch(pairs, sems, behind=()):
    copies = [pltpu.make_async_copy(src, dst, sems.at[n]) for n, (src, dst) in enumerate(pairs)]
    for copy in copies + list(behind):
        copy.start()
    for copy in copies:
        copy.wait()


def incoming(far_refs, beside_ref, odd, powers_ref, backwards, out_ref):
    states = out_ref.shape[1] // 2
    early, late = slice(0, states), slice(states, None)
    sr, si = far_refs[0][:, early], far_refs[0][:, late]
    for k in range(1, len(far_refs)):
        row = slice(4 + k, 5 + k)
        mr, mi = cmul(powers_ref[row, early], powers_ref[row, late], far_refs[k][:, early], far_refs[k][:, late])
        sr, si = sr + mr, si + mi
    mr, mi = cmul(powers_ref[0:1, early], powers_ref[0:1, late], sr, si)
    second = odd == (0 if backwards else 1)
    out_ref[:, early] = jnp.where(second, mr + beside_ref[:, early], sr)
    out_ref[:, late] = jnp.where(second, mi + beside_ref[:, late], si)


def join_kernel(mine_ref, other_ref, powers_ref, out_ref, *, row):
    states = out_ref.shape[1] // 2
    early, late = slice(0, states), slice(states, None)
    row = slice(row, row + 1)
    mr, mi = cmul(powers_ref[row, early], powers_ref[row, late], other_ref[:, early], other_ref[:, late])
    out_ref[:, early] = mine_ref[:, early] + mr
    out_ref[:, late] = mine_ref[:, late] + mi


def pair_kernel(where_ref, mine_ref, other_ref, powers_ref, out_ref, *, backwards):
    states = out_ref.shape[1] // 2
    second = where_ref[0] % 2 == (0 if backwards else 1)
    lr, li = powers_ref[0:1, :states], powers_ref[0:1, states:]
    pick = lambda first, part: jnp.where(second == first, other_ref[:, part], mine_ref[:, part])
    early, late = slice(0, states), slice(states, None)
    mr, mi = cmul(lr, li, pick(True, early), pick(True, late))
    out_ref[:, :states] = mr + pick(False, early)
    out_ref[:, states:] = mi + pick(False, late)


def assemble_input(packs, shard, out_ref):
    per = packs[0].shape[0] - PARAM_ROWS
    half = per // 2
    states = out_ref.shape[0] // 2
    for k, pack in enumerate(packs):
        at = pl.multiple_of((shard ^ k) * half, half)
        out_ref[pl.ds(at, half), :] = pack[:half, :]
        out_ref[pl.ds(states + at, half), :] = pack[half:per, :]


def input_pack_kernel(
    where_ref, in_real, in_imag, nu, theta, gamma, tok_all, cot_all, a_ref, logs, tok, cot, sems, row_sems
):
    per_s, width = in_real.shape
    rows = tok.shape[0]
    mine = pl.ds(pl.multiple_of(where_ref[1] * rows, BLOCK), rows)
    halves = [
        pltpu.make_async_copy(src.at[mine, :], dst, row_sems.at[n]) for n, (src, dst) in enumerate(((tok_all, tok), (cot_all, cot)))
    ]
    fetch(
        [(in_real, a_ref.at[pl.ds(0, per_s), :]), (in_imag, a_ref.at[pl.ds(per_s, per_s), :])]
        + [(ref, logs.at[n]) for n, ref in enumerate((nu, theta, gamma))],
        sems,
        halves,
    )
    modulus = jnp.exp(-jnp.exp(logs[0]))
    angle = jnp.exp(logs[1])
    rest = [modulus * jnp.cos(angle), modulus * jnp.sin(angle), jnp.exp(logs[2])]
    rows = []
    for _ in range(3):
        for n in range(3):
            high = rest[n].astype(BF16).astype(F32)
            rows.append(high)
            rest[n] = rest[n] - high
    table = jnp.concatenate(rows + [jnp.zeros((PARAM_ROWS - 9, per_s), F32)], axis=0)
    table = jnp.concatenate([table] * (width // per_s), axis=1)
    here = lax.broadcasted_iota(jnp.int32, (PARAM_ROWS, width), 1) // per_s == where_ref[2]
    a_ref[2 * per_s :, :] = jnp.where(here, table, 0.0).astype(BF16)
    for copy in halves:
        copy.wait()


def weight_pack_kernel(out_real, out_imag, up, gate, down, b_ref, g_ref, sems):
    per_s, per_f = out_real.shape[0], down.shape[0]
    fetch(
        [
            (out_real, b_ref.at[pl.ds(0, per_s), :]),
            (out_imag, b_ref.at[pl.ds(per_s, per_s), :]),
            (down, b_ref.at[pl.ds(2 * per_s, per_f), :]),
            (up, g_ref.at[:, pl.ds(0, per_f)]),
            (gate, g_ref.at[:, pl.ds(per_f, per_f)]),
        ],
        sems,
    )


def mask_rows(lens_ref, where_ref, seq, seqs, length, width):
    left = lens_ref[where_ref[1] * seqs + seq] - where_ref[0] * length
    return lax.broadcasted_iota(jnp.int32, (length, width), 0) < left


def norm_kernel(
    where_ref, tok, cot, gain_all, bias_all, lens_all, low_ref, normed_ref, inv_ref, cotm_ref,
    gain_ref, bias_ref, lens_ref, sems, *, length
):
    rows, width = low_ref.shape
    fetch([(gain_all, gain_ref), (bias_all, bias_ref), (lens_all, lens_ref)], sems)
    for block in range(rows // BLOCK):
        span = slice(block * BLOCK, (block + 1) * BLOCK)
        normed, inv_scale = layer_norm(tok[span, :].astype(F32))
        normed_ref[span, :] = normed
        inv_ref[span, :] = jnp.broadcast_to(inv_scale, (BLOCK, inv_ref.shape[1]))
        low_ref[span, :] = (normed * gain_ref[...] + bias_ref[...]).astype(BF16)
        for seq in range(block * BLOCK // length, (block + 1) * BLOCK // length):
            span = slice(seq * length, (seq + 1) * length)
            live = mask_rows(lens_ref, where_ref, seq, rows // length, length, width)
            cotm_ref[span, :] = jnp.where(live, cot[span, :].astype(F32), 0.0).astype(BF16)


def weighted_ends(drive_ref, weigh, length, first, ends_ref):
    rows, lanes = drive_ref.shape
    states = lanes // 2
    for s in range(rows // length):
        er = ei = jnp.zeros((TILE, states), F32)
        for n in range(length // TILE):
            at = s * length + n * TILE
            mr, mi = cmul(
                weigh[0, n * TILE : (n + 1) * TILE, :],
                weigh[1, n * TILE : (n + 1) * TILE, :],
                drive_ref[at : at + TILE, :states],
                drive_ref[at : at + TILE, states:],
            )
            er, ei = er + mr, ei + mi
        ends_ref[pl.ds(first + s, 1), :states] = jnp.sum(er, axis=0, keepdims=True)
        ends_ref[pl.ds(first + s, 1), states:] = jnp.sum(ei, axis=0, keepdims=True)


def drive_kernel(where_ref, low_all, a0, a1, a2, a3, drive_all, ends_ref, powers_ref, in_t, weigh, *, length):
    packs = (a0, a1, a2, a3)
    states = in_t.shape[0] // 2
    assemble_input(packs, where_ref[2], in_t)
    dr, di, gain = read_params(packs, a0.shape[0] - PARAM_ROWS)
    fill_powers(dr, di, True, 0, weigh)
    gam = jnp.concatenate([gain, gain], axis=1)
    lr, li = cmul(weigh[0, :1, :], weigh[1, :1, :], dr, di)
    rows = [(lr, li)] + [cmul(lr, li, lr, li)]
    for _ in range(2):
        rows.append(cmul(*rows[-1], *rows[-1]))
    rows.append((jnp.ones_like(lr), jnp.zeros_like(lr)))
    for _ in range(3):
        rows.append(cmul(*cmul(*rows[-1], *rows[-1]), *rows[1]))
    for k, (lr, li) in enumerate(rows):
        powers_ref[k : k + 1, :] = jnp.concatenate([lr, li], axis=1)
    per_block = LARGE // length

    def body(block, view):
        low_ref, drive_ref = view(low_all), view(drive_all)
        drive_ref[...] = dot_nt(low_ref[...], in_t[...]) * gam
        weighted_ends(drive_ref, weigh, length, block * per_block, ends_ref)

    each_block(low_all.shape[0], LARGE, body)


def scan_kernel(drive_all, a0, a1, a2, a3, local_all, step, *, length, backwards):
    dr, di, _ = read_params((a0, a1, a2, a3), a0.shape[0] - PARAM_ROWS)
    fill_steps(dr, di, backwards, step)
    each_block(
        drive_all.shape[0],
        BLOCK,
        lambda block, view: scan_block(view(drive_all), view(local_all), step, length, backwards),
    )


def hidden_kernel(where_ref, cotm_all, b0, b1, b2, b3, hg_all, *, per_s):
    shard = where_ref[2]
    per_f = hg_all.shape[1] // TENSOR

    def body(block, view):
        hg_ref, cotm = view(hg_all), view(cotm_all)[...]
        for k, pack in enumerate((b0, b1, b2, b3)):
            at = pl.multiple_of((shard ^ k) * per_f, per_f)
            hg_ref[:, pl.ds(at, per_f)] = dot_nt(cotm, pack[2 * per_s :, :]).astype(BF16)

    each_block(cotm_all.shape[0], LARGE, body)


def middle_kernel(where_ref, *refs, length, levels):
    far_refs, refs = refs[:levels], refs[levels:]
    beside_ref, powers_ref, local_all, normed_all, hg_all, cotm_all, a0, a1, a2, a3 = refs[:10]
    gain_ref, bias_ref, skip_ref, b0, b1, b2, b3, g0, g1, g2, g3 = refs[10:21]
    state_all, back_all, backends_ref, ylow_all, hid_all, act_all, ul_all = refs[21:28]
    c_all, ug_all, weigh, full, carry, sems = refs[28:]
    place, core, shard = where_ref[0], where_ref[1], where_ref[2]
    states = c_all.shape[0] // 2
    rows, width = normed_all.shape
    per_block = LARGE // length
    per_s = states // TENSOR
    per_f = hid_all.shape[1] // TENSOR

    copies = []
    for k, (pack, gates) in enumerate(((b0, g0), (b1, g1), (b2, g2), (b3, g3))):
        t = shard ^ k
        moves = (
            (pack.at[pl.ds(0, per_s), :], c_all.at[pl.ds(pl.multiple_of(t * per_s, per_s), per_s), :]),
            (pack.at[pl.ds(per_s, per_s), :], c_all.at[pl.ds(pl.multiple_of(states + t * per_s, per_s), per_s), :]),
            (gates, ug_all.at[:, pl.ds(pl.multiple_of(t * 2 * per_f, 2 * per_f), 2 * per_f)]),
        )
        for n, (src, dst) in enumerate(moves):
            copies.append(pltpu.make_async_copy(src, dst, sems.at[k, n]))
    for copy in copies:
        copy.start()
    dr, di, _ = read_params((a0, a1, a2, a3), a0.shape[0] - PARAM_ROWS)
    fill_powers(dr, di, False, 1, full)
    incoming(far_refs, beside_ref, place % 2, powers_ref, False, carry)
    fill_powers(dr, di, False, 0, weigh)
    for copy in copies:
        copy.wait()
    skip = skip_ref[...]
    skip_gain, skip_bias = gain_ref[...] * skip, bias_ref[...] * skip

    def body(block, view):
        local_ref, state_ref, hid_ref, ylow_ref = view(local_all), view(state_all), view(hid_all), view(ylow_all)
        hg_ref, act_ref, back_ref, ul = view(hg_all), view(act_all), view(back_all), view(ul_all)
        for s in range(per_block):
            seq = block * per_block + s
            span = slice(s * length, (s + 1) * length)
            sr = carry[pl.ds(seq, 1), :states]
            si = carry[pl.ds(seq, 1), states:]
            mr, mi = cmul(full[0], full[1], sr, si)
            state_ref[span, :states] = (local_ref[span, :states] + mr).astype(BF16)
            state_ref[span, states:] = (-(local_ref[span, states:] + mi)).astype(BF16)
        y = dot(state_ref[...], c_all[...]) + (view(normed_all)[...] * skip_gain + skip_bias)
        square = y * y
        th = jnp.tanh(y * (GELU_K + (GELU_K * 0.044715) * square))
        half_y = 0.5 * y
        act_ref[...] = (half_y + half_y * th).astype(BF16)
        slope = (0.5 + 0.5 * th) + half_y * (1.0 - th * th) * (GELU_K + (GELU_K * 3 * 0.044715) * square)
        act = act_ref[...]
        for t in range(TENSOR):
            both = dot(act, ug_all[:, 2 * per_f * t : 2 * per_f * (t + 1)])
            up = both[:, :per_f]
            th = 0.5 * jnp.tanh(0.5 * both[:, per_f:])
            sig = 0.5 + th
            hid_ref[:, per_f * t : per_f * (t + 1)] = (up * sig).astype(BF16)
            up_grad = hg_ref[:, per_f * t : per_f * (t + 1)].astype(F32) * sig
            ul[:, 2 * per_f * t : 2 * per_f * t + per_f] = up_grad.astype(BF16)
            ul[:, 2 * per_f * t + per_f : 2 * per_f * (t + 1)] = (up_grad * up * (0.5 - th)).astype(BF16)
        y_grad = dot_nt(ul[...], ug_all[...]) * slope
        ylow_ref[...] = y_grad.astype(BF16)
        back_ref[...] = dot_nt(ylow_ref[...], c_all[...])
        weighted_ends(back_ref, weigh, length, block * per_block, backends_ref)

    each_block(rows, LARGE, body)


def weight_kernel(where_ref, hid_ref, cotm_ref, act_ref, ul_ref, state_ref, ylow_ref, own_ref, sent_ref):
    core, side = where_ref[1], where_ref[2] // 2
    states = state_ref.shape[1] // 2
    per_s = states // TENSOR
    per_f = hid_ref.shape[1] // TENSOR
    width = act_ref.shape[1]
    cols = [
        state_ref[:, pl.ds(pl.multiple_of(k * states + side * 2 * per_s, 2 * per_s), 2 * per_s)] for k in range(2)
    ]
    out_grad = dot_tn(jnp.concatenate(cols, axis=1), ylow_ref[...])
    act, cotm = act_ref[...], cotm_ref[...]
    for n, ref in ((1 - core, sent_ref), (core, own_ref)):
        ul = ul_ref[:, pl.ds(pl.multiple_of((2 * side + n) * 2 * per_f, 2 * per_f), 2 * per_f)]
        ref[2 * per_s + per_f : 2 * per_s + per_f + width, :] = dot_tn(act, ul).astype(ref.dtype)
        hid = hid_ref[:, pl.ds(pl.multiple_of((2 * side + n) * per_f, per_f), per_f)]
        ref[2 * per_s : 2 * per_s + per_f, :] = dot_tn(hid, cotm).astype(ref.dtype)
        for k in range(2):
            at = 2 * per_s * k
            part = jnp.where(n == 0, out_grad[at : at + per_s, :], out_grad[at + per_s : at + 2 * per_s, :])
            ref[k * per_s : (k + 1) * per_s, :] = part.astype(ref.dtype)


def down_kernel(where_ref, lens_ref, tok, hid_all, b0, b1, b2, b3, out_all, down_all, *, length, per_s):
    shard = where_ref[2]
    rows, width = out_all.shape
    per_block = LARGE // length
    per_f = down_all.shape[0] // TENSOR
    for k, pack in enumerate((b0, b1, b2, b3)):
        down_all[pl.ds(pl.multiple_of((shard ^ k) * per_f, per_f), per_f), :] = pack[2 * per_s :, :]

    def body(block, view):
        added = dot(view(hid_all)[...], down_all[...])
        out_ref, tok_ref = view(out_all), view(tok)
        for s in range(per_block):
            span = slice(s * length, (s + 1) * length)
            live = mask_rows(lens_ref, where_ref, block * per_block + s, rows // length, length, width)
            out_ref[span, :] = jnp.where(live, tok_ref[span, :].astype(F32) + added[span, :], 0.0).astype(BF16)

    each_block(rows, LARGE, body)


def last_kernel(where_ref, *refs, length, levels):
    far_refs, refs = refs[:levels], refs[levels:]
    beside_ref, powers_ref, low_all, normed_all, inv_all, cotm_all, back_all, state_all, ylow_all = refs[:9]
    a0, a1, a2, a3, gain_ref, bias_ref, skip_ref, grad_all, own_ref, sent_ref = refs[9:19]
    in_t, full, carry, dlow, in_grad, lam_grad, vec_grad = refs[19:]
    place, core, shard = where_ref[0], where_ref[1], where_ref[2]
    states = in_t.shape[0] // 2
    rows, width = low_all.shape
    per_block = LARGE // length
    per_s = states // TENSOR
    packs = (a0, a1, a2, a3)

    assemble_input(packs, shard, in_t)
    dr, di, gain = read_params(packs, a0.shape[0] - PARAM_ROWS)
    fill_powers(dr, di, True, 1, full)
    incoming(far_refs, beside_ref, place % 2, powers_ref, True, carry)
    in_grad[...] = jnp.zeros(in_grad.shape, F32)
    lam_grad[...] = jnp.zeros(lam_grad.shape, F32)
    vec_grad[...] = jnp.zeros(vec_grad.shape, F32)
    at = pl.multiple_of((shard // 2) * 2 * per_s, 2 * per_s)

    def body(block, view):
        back_ref, state_ref = view(back_all), view(state_all)
        for s in range(per_block):
            seq = block * per_block + s
            span = slice(s * length, (s + 1) * length)
            sr = carry[pl.ds(seq, 1), :states]
            si = carry[pl.ds(seq, 1), states:]
            mr, mi = cmul(full[0], full[1], sr, si)
            gr = back_ref[span, :states] + mr
            gi = back_ref[span, states:] + mi
            dlow[span, :states] = (gr * gain).astype(BF16)
            dlow[span, states:] = (gi * -gain).astype(BF16)
            nr = jnp.concatenate([gr[1:], sr], axis=0)
            ni = jnp.concatenate([gi[1:], si], axis=0)
            hr = state_ref[span, :states].astype(F32)
            hi = state_ref[span, states:].astype(F32)
            lam_grad[:, :states] += jnp.sum(nr * hr + ni * hi, axis=0, keepdims=True)
            lam_grad[:, states:] += jnp.sum(nr * hi - ni * hr, axis=0, keepdims=True)
        normed = view(normed_all)[...]
        ylow = view(ylow_all)[...].astype(F32)
        low = view(low_all)[...]
        u_grad = dot(dlow[...], in_t[...]) + ylow * skip_ref[...]
        vec_grad[0:1, :] += jnp.sum(u_grad * normed, axis=0, keepdims=True)
        vec_grad[1:2, :] += jnp.sum(u_grad, axis=0, keepdims=True)
        vec_grad[2:3, :] += jnp.sum(ylow * (normed * gain_ref[...] + bias_ref[...]), axis=0, keepdims=True)
        scaled = u_grad * gain_ref[...]
        grad = (
            scaled
            - jnp.mean(scaled, axis=-1, keepdims=True)
            - normed * jnp.mean(scaled * normed, axis=-1, keepdims=True)
        )
        view(grad_all)[...] = (view(cotm_all)[...].astype(F32) + view(inv_all)[:, :1] * grad).astype(BF16)
        for k in range(2):
            cols = dlow[:, pl.ds(k * states + at, 2 * per_s)]
            in_grad[2 * per_s * k : 2 * per_s * (k + 1), :] += dot_tn(cols, low)

    each_block(rows, LARGE, body)
    small = jnp.concatenate(
        [vec_grad[:3, :], lam_grad[...], jnp.zeros((PARAM_ROWS - 4, width), F32)], axis=0
    ).astype(BF16)
    for n, ref in ((core, own_ref), (1 - core, sent_ref)):
        for k in range(2):
            part = in_grad[pl.ds(pl.multiple_of(2 * per_s * k + n * per_s, per_s), per_s), :]
            ref[k * per_s : (k + 1) * per_s, :] = part.astype(BF16)
        ref[2 * per_s :, :] = small


def join_halves_kernel(where_ref, own_ref, other_ref, out_ref, sems):
    rows = own_ref.shape[0]
    copies = [
        pltpu.make_async_copy(ref, out_ref.at[pl.ds(pl.multiple_of(n * rows, BLOCK), rows), :], sems.at[k])
        for k, (n, ref) in enumerate(((where_ref[1], own_ref), (1 - where_ref[1], other_ref)))
    ]
    for copy in copies:
        copy.start()
    for copy in copies:
        copy.wait()


def widen_halves_kernel(where_ref, own_ref, other_ref, out_ref, wide, sems):
    rows = own_ref.shape[0]
    slots = wide.shape[0]
    flying = []
    for n in range(2 * rows // BLOCK):
        slot = n % slots
        if n >= slots:
            flying[n - slots].wait()
        at = (n // 2) * BLOCK
        half, ref = ((where_ref[1], own_ref), (1 - where_ref[1], other_ref))[n % 2]
        wide[slot] = ref[at : at + BLOCK, :].astype(F32)
        copy = pltpu.make_async_copy(
            wide.at[slot], out_ref.at[pl.ds(pl.multiple_of(half * rows + at, BLOCK), BLOCK), :], sems.at[slot]
        )
        copy.start()
        flying.append(copy)
    for copy in flying[-slots:]:
        copy.wait()


def fold_kernel(where_ref, own_ref, other_ref, keep_ref, send_ref):
    half = keep_ref.shape[0]
    odd = where_ref[0] % 2
    at = pl.multiple_of(odd * half, 16)
    keep_ref[...] = own_ref[pl.ds(at, half), :] + other_ref[pl.ds(at, half), :].astype(F32)
    at = pl.multiple_of((1 - odd) * half, 16)
    send_ref[...] = (own_ref[pl.ds(at, half), :] + other_ref[pl.ds(at, half), :].astype(F32)).astype(BF16)


def deal_kernel(where_ref, own_ref, other_ref, keep_ref, *send_refs):
    rows = keep_ref.shape[0]
    for k, ref in enumerate((keep_ref,) + send_refs):
        at = pl.multiple_of(((where_ref[0] // 2) ^ k) * rows, 16)
        ref[...] = (own_ref[pl.ds(at, rows), :] + other_ref[pl.ds(at, rows), :].astype(F32)).astype(ref.dtype)


def unpack_kernel(where_ref, *refs, ways):
    parts, (real_ref, imag_ref, up_ref, gate_ref, down_ref, total, sems) = refs[: ways + 2], refs[ways + 2 :]
    place = where_ref[0]
    rows = parts[0].shape[0]
    for n in range(2 * ways):
        k = n % ways
        half = place % 2 if n < ways else 1 - place % 2
        at = (half * ways + ((place // 2) ^ k)) * rows
        if n <= ways:
            part = parts[n][...]
        else:
            part = parts[-1][(k - 1) * rows : k * rows, :]
        total[pl.ds(pl.multiple_of(at, 16), rows), :] = part.astype(F32)
    per_s, per_f, width = real_ref.shape[0], down_ref.shape[0], up_ref.shape[0]
    first = 2 * per_s + per_f
    moves = [
        (total.at[pl.ds(first, width), pl.ds(0, per_f)], up_ref),
        (total.at[pl.ds(first, width), pl.ds(per_f, per_f)], gate_ref),
        (total.at[pl.ds(2 * per_s, per_f), :], down_ref),
        (total.at[pl.ds(0, per_s), :], real_ref),
        (total.at[pl.ds(per_s, per_s), :], imag_ref),
    ]
    fetch(moves, sems)


def finish_kernel(where_ref, mine_ref, other_ref, a_ref, logs_ref, *refs):
    outs, (grads_ref, logs, sems) = refs[:8], refs[8:]
    width = grads_ref.shape[1]
    per_s = logs_ref.shape[2]
    grads = mine_ref[...].astype(F32) + other_ref[...].astype(F32)
    grads_ref[...] = grads
    lam = [jnp.zeros((1, per_s), F32), jnp.zeros((1, per_s), F32)]
    for t in range(TENSOR):
        for n in range(2):
            at = (n * TENSOR + t) * per_s
            part = grads[2 * per_s + 3 : 2 * per_s + 4, at : at + per_s]
            lam[n] = jnp.where(where_ref[2] == t, part, lam[n])
    decay = jnp.exp(logs_ref[0])
    modulus = jnp.exp(-decay)
    angle = jnp.exp(logs_ref[1])
    cos, sin = jnp.cos(angle), jnp.sin(angle)
    logs[0] = -decay * modulus * (lam[0] * cos + lam[1] * sin)
    logs[1] = angle * modulus * (lam[1] * cos - lam[0] * sin)
    terms = a_ref[:per_s, :].astype(F32) * grads[:per_s, :] + a_ref[per_s : 2 * per_s, :].astype(F32) * grads[per_s : 2 * per_s, :]
    logs[2] = jnp.sum(terms.T, axis=0, keepdims=True)
    moves = [(grads_ref.at[pl.ds(2 * per_s + n, 1), :], outs[n]) for n in range(3)]
    moves += [(grads_ref.at[pl.ds(n * per_s, per_s), :], outs[3 + n]) for n in range(2)]
    moves += [(logs.at[n], outs[5 + n]) for n in range(3)]
    fetch(moves, sems)


def near(value):
    return pltpu.with_memory_space_constraint(value, pltpu.VMEM)


def call(kernel, scalars, inputs, outs, scratch, vmem, far_inputs=(), far_outs=()):
    here, anywhere = pl.BlockSpec(memory_space=pltpu.VMEM), pl.BlockSpec(memory_space=pl.ANY)
    single = not isinstance(outs, list)
    listed = [outs] if single else outs
    shapes = [
        jax.ShapeDtypeStruct(*out) if n in far_outs else pltpu.VMEM(*out) for n, out in enumerate(listed)
    ]
    out_specs = [anywhere if n in far_outs else here for n in range(len(listed))]
    return pl.pallas_call(
        kernel,
        in_specs=[pl.BlockSpec(memory_space=pltpu.SMEM)] * len(scalars)
        + [anywhere if n in far_inputs else here for n in range(len(inputs))],
        out_specs=out_specs[0] if single else out_specs,
        out_shape=shapes[0] if single else shapes,
        scratch_shapes=scratch,
        compiler_params=pltpu.CompilerParams(vmem_limit_bytes=vmem * MIB),
    )(
        *scalars,
        *[
            pltpu.with_memory_space_constraint(v, pltpu.HBM) if n in far_inputs else near(v)
            for n, v in enumerate(inputs)
        ],
    )


def core_swap(value):
    return lax.ppermute(value, "tensor", [(t, t ^ 1) for t in range(TENSOR)])


def side_swap(value):
    return lax.ppermute(value, "tensor", [(t, t ^ 2) for t in range(TENSOR)])


def gather_tensor(own, *first):
    across = after(side_swap(own), *first)
    return own, core_swap(own), across, core_swap(across)


def after(value, *first):
    return lax.optimization_barrier((value,) + first)[0]


def flip_dp(value, bits, groups):
    return lax.ppermute(value, "dp", [(i, i ^ bits) for i in range(groups)])


def shift_dp(value, by, groups):
    return lax.ppermute(value, "dp", [(i, i + by) for i in range(groups) if 0 <= i + by < groups])


def shards(
    tokens,
    cotangent,
    ln_gain,
    ln_bias,
    skip_gain,
    in_real,
    in_imag,
    out_real,
    out_imag,
    nu_log,
    theta_log,
    gamma_log,
    up_weight,
    gate_weight,
    down_weight,
    lengths,
    *,
    groups,
):
    seqs, length, width = tokens.shape
    per_s = in_real.shape[1]
    per_f = up_weight.shape[1]
    states = per_s * TENSOR
    own_seqs = seqs // 2
    rows = own_seqs * length
    blocks = rows // BLOCK
    place = lax.axis_index("dp").astype(jnp.int32)
    shard = lax.axis_index("tensor").astype(jnp.int32)
    core = shard % 2
    where = jnp.stack([place, core, shard])

    tok_rows = tokens.reshape(seqs * length, width)
    cot_rows = cotangent.reshape(seqs * length, width)
    row = lambda v: v.reshape(1, width)
    gain_row, bias_row, skip_row = row(ln_gain), row(ln_bias), row(skip_gain)
    a_shape = (2 * per_s + PARAM_ROWS, width)
    b_shape = (2 * per_s + per_f, width)
    lanes = 2 * states
    units = TENSOR * per_f
    ends_shape = ((own_seqs, lanes), F32)
    dma = pltpu.SemaphoreType.DMA
    line = lambda v: v.reshape(1, per_s)

    pack_a, logs, own_tok, own_cot = call(
        input_pack_kernel,
        [where],
        [in_real.T, in_imag.T, line(nu_log), line(theta_log), line(gamma_log), tok_rows, cot_rows],
        [(a_shape, BF16), ((3, 1, per_s), F32), ((rows, width), BF16), ((rows, width), BF16)],
        [dma((5,)), dma((2,))],
        4,
        far_inputs=range(7),
    )
    pack_b, pack_g = call(
        weight_pack_kernel,
        [],
        [after(out_real, pack_a), out_imag, up_weight, gate_weight, down_weight],
        [(b_shape, BF16), ((width, 2 * per_f), BF16)],
        [dma((5,))],
        4,
        far_inputs=range(5),
    )
    low, normed, inv, cot_m = call(
        functools.partial(norm_kernel, length=length),
        [where],
        [own_tok, after(own_cot, pack_b), gain_row, bias_row, lengths],
        [((rows, width), BF16), ((rows, width), F32), ((rows, 128), F32), ((rows, width), BF16)],
        [
            pltpu.VMEM((1, width), F32),
            pltpu.VMEM((1, width), F32),
            pltpu.SMEM((seqs,), jnp.int32),
            dma((3,)),
        ],
        8,
        far_inputs=(2, 3, 4),
    )
    packs_a = gather_tensor(pack_a, low)
    pack_b, pack_g = after((pack_b, pack_g), packs_a[2])
    drive, ends, powers = call(
        functools.partial(drive_kernel, length=length),
        [where],
        [low, *packs_a],
        [((rows, lanes), F32), ends_shape, ((TILE, lanes), F32)],
        [pltpu.VMEM((lanes, width), BF16), pltpu.VMEM((2, length, states), F32)],
        8,
    )
    local = call(
        functools.partial(scan_kernel, length=length, backwards=False),
        [],
        [drive, *packs_a],
        ((rows, lanes), F32),
        [pltpu.VMEM((4, 2, TILE, states), F32)],
        8,
    )

    ways = groups // 2
    levels = (ways - 1).bit_length()

    def exchange(mine, backwards, beside_work, first_work=None):
        beside = after(flip_dp(mine, 1, groups), beside_work)
        both = call(
            functools.partial(pair_kernel, backwards=backwards), [where], [mine, beside, powers], ends_shape, [], 2
        )
        found = [both]
        from_far = []
        for k in range(levels):
            step = 2 << k
            from_far.append(shift_dp(found[-1], -step if backwards else step, groups))
            if k == 0 and first_work is not None:
                from_far[0] = after(from_far[0], first_work(both))
            if k + 1 < levels:
                found.append(
                    call(functools.partial(join_kernel, row=1 + k), [], [found[-1], from_far[-1], powers], ends_shape, [], 2)
                )
        return from_far, beside, found

    far_ends, beside_ends, found_ends = exchange(ends, False, local)
    packs_b = gather_tensor(pack_b, far_ends[0])
    hid_grad = call(
        functools.partial(hidden_kernel, per_s=per_s),
        [where],
        [after(cot_m, found_ends[-1]), *packs_b],
        ((rows, units), BF16),
        [],
        8,
    )
    packs_g = gather_tensor(pack_g, hid_grad, *far_ends)

    pack_rows = -(-(2 * per_s + per_f + width) // (16 * groups)) * 16 * groups
    state, back_drive, back_ends, y_low, hid, act, ul = call(
        functools.partial(middle_kernel, length=length, levels=levels),
        [where],
        [
            *far_ends,
            beside_ends,
            powers,
            local,
            normed,
            hid_grad,
            cot_m,
            *packs_a,
            gain_row,
            bias_row,
            skip_row,
            *packs_b,
            *packs_g,
        ],
        [
            ((rows, lanes), BF16),
            ((rows, lanes), F32),
            ends_shape,
            ((rows, width), BF16),
            ((rows, units), BF16),
            ((rows, width), BF16),
            ((rows, 2 * units), BF16),
        ],
        [
            pltpu.VMEM((lanes, width), BF16),
            pltpu.VMEM((width, 2 * units), BF16),
            pltpu.VMEM((2, length, states), F32),
            pltpu.VMEM((2, length, states), F32),
            pltpu.VMEM((own_seqs, lanes), F32),
            dma((TENSOR, 3)),
        ],
        16,
    )
    own_b, sent_b = call(
        weight_kernel,
        [where],
        [hid, cot_m, act, ul, state, y_low],
        [((pack_rows, width), F32), ((pack_rows, width), BF16)],
        [],
        10,
    )

    half, part = pack_rows // 2, pack_rows // groups
    made = []

    def scan_work(pair_back):
        made.append(
            call(
                functools.partial(scan_kernel, length=length, backwards=True),
                [],
                [after(back_drive, pair_back), *packs_a],
                ((rows, lanes), F32),
                [pltpu.VMEM((4, 2, TILE, states), F32)],
                8,
            )
        )
        return made[0]

    far_back, beside_back, found_back = exchange(back_ends, True, own_b, scan_work)
    back = made[0]
    keep_b, send_b = call(
        fold_kernel,
        [where],
        [own_b, core_swap(after(sent_b, beside_back))],
        [((half, width), F32), ((half, width), BF16)],
        [],
        4,
    )
    half_b = flip_dp(after(send_b, found_back[0]), 1, groups)
    out_own = call(
        functools.partial(down_kernel, length=length, per_s=per_s),
        [where, lengths],
        [own_tok, after(hid, found_back[-1]), *packs_b],
        ((rows, width), BF16),
        [pltpu.VMEM((units, width), BF16)],
        8,
    )
    dealt = call(
        deal_kernel,
        [where],
        [after(keep_b, out_own, *far_back), half_b],
        [((part, width), F32)] + [((part, width), BF16)] * (ways - 1),
        [],
        4,
    )

    grad_own, own_a, sent_a = call(
        functools.partial(last_kernel, length=length, levels=levels),
        [where],
        [
            *far_back,
            after(beside_back, dealt[0]),
            powers,
            low,
            normed,
            inv,
            cot_m,
            back,
            state,
            y_low,
            *packs_a,
            gain_row,
            bias_row,
            skip_row,
        ],
        [((rows, width), BF16), (a_shape, BF16), (a_shape, BF16)],
        [
            pltpu.VMEM((lanes, width), BF16),
            pltpu.VMEM((2, length, states), F32),
            pltpu.VMEM((own_seqs, lanes), F32),
            pltpu.VMEM((LARGE, lanes), BF16),
            pltpu.VMEM((states, width), F32),
            pltpu.VMEM((1, lanes), F32),
            pltpu.VMEM((TILE, width), F32),
        ],
        12,
    )

    mine_b = dealt[0]
    for k in range(1, ways):
        mine_b = mine_b + flip_dp(dealt[k], 2 * k, groups).astype(F32)
    mine_b = mine_b.astype(BF16)
    gathered = [mine_b] + [flip_dp(mine_b, 2 * k, groups) for k in range(1, ways)]
    beside = [flip_dp(mine_b, 1, groups), flip_dp(jnp.concatenate(gathered[1:], axis=0), 1, groups)]

    grads_a = own_a.astype(F32) + after(core_swap(sent_a), mine_b).astype(F32)
    low_a = grads_a.astype(BF16)

    block_out = call(
        join_halves_kernel,
        [where],
        [out_own, core_swap(after(out_own, low_a))],
        [((seqs * length, width), BF16)],
        [dma((2,))],
        2,
        far_outs=(0,),
    )[0].reshape(seqs, length, width)
    input_grad = call(
        widen_halves_kernel,
        [where],
        [grad_own, core_swap(after(grad_own, low_a))],
        [((seqs * length, width), F32)],
        [pltpu.VMEM((4, BLOCK, width), F32), dma((4,))],
        4,
        far_outs=(0,),
    )[0].reshape(seqs, length, width)

    state_shape = ((per_s, width), F32)
    unpacked = call(
        functools.partial(unpack_kernel, ways=ways),
        [where],
        [*gathered, beside[0], after(beside[1], input_grad)],
        [state_shape] * 2 + [((width, per_f), F32)] * 2 + [((per_f, width), F32)],
        [pltpu.VMEM((pack_rows, width), F32), dma((5,))],
        8,
        far_outs=range(5),
    )
    works = {1: [block_out], 2: [beside[0]], 4: unpacked}
    bit = 1
    while bit < groups:
        other_a = after(flip_dp(low_a, bit, groups), *works.get(bit, []))
        bit *= 2
        if bit < groups:
            low_a = (low_a.astype(F32) + other_a.astype(F32)).astype(BF16)
        if bit == 4:
            low_a = after(low_a, *gathered)

    finished = call(
        finish_kernel,
        [where],
        [low_a, other_a, pack_a, logs],
        [((1, width), F32)] * 3 + [state_shape] * 2 + [((1, per_s), F32)] * 3,
        [pltpu.VMEM(a_shape, F32), pltpu.VMEM((3, 1, per_s), F32), dma((8,))],
        4,
        far_outs=range(8),
    )
    return (
        block_out,
        input_grad,
        *[v.reshape(width) for v in finished[:3]],
        *[v.T for v in finished[3:5]],
        *unpacked[:2],
        *[v.reshape(per_s) for v in finished[5:]],
        *unpacked[2:],
    )


def solution(mesh):
    rows = P(None, "dp", None)
    columns = P(None, "tensor")
    lines = P("tensor", None)
    vector = P("tensor")
    in_specs = (rows, rows, P(), P(), P(), columns, columns, lines, lines, vector, vector, vector, columns, columns, lines, P())
    out_specs = (rows, rows, P(), P(), P(), columns, columns, lines, lines, vector, vector, vector, columns, columns, lines)
    return jax.shard_map(
        functools.partial(shards, groups=mesh.shape["dp"]),
        mesh=mesh,
        in_specs=in_specs,
        out_specs=out_specs,
        check_vma=False,
    )
```

```python
import functools
import math

import jax
import jax.numpy as jnp
from jax import lax
from jax.experimental import pallas as pl
from jax.experimental.pallas import tpu as pltpu
from jax.sharding import PartitionSpec as P

EPSILON = 1e-05
TENSOR = 4
TILE = 8
BLOCK = 256
LARGE = 512
PARAM_ROWS = 16
F32 = jnp.float32
BF16 = jnp.bfloat16
GELU_K = math.sqrt(2.0 / math.pi)
MIB = 1024 * 1024


def dot(left, right):
    return jnp.dot(left, right, preferred_element_type=F32)


def dot_nt(left, right):
    return lax.dot_general(left, right, (((1,), (1,)), ((), ())), preferred_element_type=F32)


def dot_tn(left, right):
    return lax.dot_general(left, right, (((0,), (0,)), ((), ())), preferred_element_type=F32)


def layer_norm(rows):
    centre = jnp.mean(rows, axis=-1, keepdims=True)
    shifted = rows - centre
    variance = jnp.mean(shifted * shifted, axis=-1, keepdims=True)
    inv_scale = lax.rsqrt(variance + EPSILON)
    return shifted * inv_scale, inv_scale


def cmul(ar, ai, br, bi):
    return ar * br - ai * bi, ar * bi + ai * br


def read_params(packs, row):
    total = None
    for pack in packs:
        rows = pack[row : row + PARAM_ROWS, :].astype(F32)
        total = rows if total is None else total + rows
    states = total.shape[1] // 2
    at = lambda k: total[k : k + 1, :states] + total[k + 3 : k + 4, :states] + total[k + 6 : k + 7, :states]
    return at(0), at(1), at(2)


def powers_of(decay_real, decay_imag, exponent):
    out_r = jnp.ones(exponent.shape, F32)
    out_i = jnp.zeros(exponent.shape, F32)
    br, bi = decay_real, decay_imag
    for bit in range(4):
        mr, mi = cmul(out_r, out_i, br, bi)
        on = ((exponent >> bit) & 1) == 1
        out_r = jnp.where(on, mr, out_r)
        out_i = jnp.where(on, mi, out_i)
        br, bi = cmul(br, bi, br, bi)
    return out_r, out_i


def fill_steps(decay_real, decay_imag, backwards, step_ref):
    states = decay_real.shape[1]
    row = lax.broadcasted_iota(jnp.int32, (TILE, states), 0)
    if backwards:
        row = TILE - 1 - row
    zero = jnp.zeros((TILE, states), F32)
    for k, shift in enumerate((1, 2, 4)):
        pr, pi = powers_of(decay_real, decay_imag, jnp.full((TILE, states), shift, jnp.int32))
        step_ref[k, 0] = jnp.where(row >= shift, pr, zero)
        step_ref[k, 1] = jnp.where(row >= shift, pi, zero)
    step_ref[3, 0], step_ref[3, 1] = powers_of(decay_real, decay_imag, row + 1)


def fill_powers(decay_real, decay_imag, backwards, first, full_ref):
    states = decay_real.shape[1]
    row = lax.broadcasted_iota(jnp.int32, (TILE, states), 0)
    if backwards:
        row = TILE - 1 - row
    pr, pi = powers_of(decay_real, decay_imag, row + first)
    er, ei = powers_of(decay_real, decay_imag, jnp.full((TILE, states), TILE, jnp.int32))
    tiles = full_ref.shape[1] // TILE
    for n in range(tiles):
        at = (tiles - 1 - n if backwards else n) * TILE
        full_ref[0, at : at + TILE, :] = pr
        full_ref[1, at : at + TILE, :] = pi
        pr, pi = cmul(pr, pi, er, ei)


def scan_block(drive_ref, out_ref, step_ref, length, backwards):
    rows, lanes = drive_ref.shape
    states = lanes // 2
    tiles = length // TILE
    table = [(step_ref[k, 0], step_ref[k, 1]) for k in range(4)]
    edge = 0 if backwards else TILE - 1
    for s in range(rows // length):
        cr = ci = None
        for n in range(tiles):
            at = s * length + (tiles - 1 - n if backwards else n) * TILE
            hr = drive_ref[at : at + TILE, :states]
            hi = drive_ref[at : at + TILE, states:]
            for k, shift in enumerate((1, 2, 4)):
                turn = TILE - shift if backwards else shift
                sr = pltpu.roll(hr, turn, 0)
                si = pltpu.roll(hi, turn, 0)
                mr, mi = cmul(table[k][0], table[k][1], sr, si)
                hr, hi = hr + mr, hi + mi
            if cr is not None:
                mr, mi = cmul(table[3][0], table[3][1], cr, ci)
                hr, hi = hr + mr, hi + mi
            out_ref[at : at + TILE, :states] = hr
            out_ref[at : at + TILE, states:] = hi
            cr, ci = hr[edge : edge + 1], hi[edge : edge + 1]


def each_block(rows, size, body):
    def step(block, carry):
        at = pl.multiple_of(block * size, size)
        body(block, lambda ref: ref.at[pl.ds(at, size), :])
        return carry

    lax.fori_loop(0, rows // size, step, 0)


def fetch(pairs, sems, behind=()):
    copies = [pltpu.make_async_copy(src, dst, sems.at[n]) for n, (src, dst) in enumerate(pairs)]
    for copy in copies + list(behind):
        copy.start()
    for copy in copies:
        copy.wait()


def incoming(far_refs, beside_ref, odd, powers_ref, backwards, out_ref):
    states = out_ref.shape[1] // 2
    early, late = slice(0, states), slice(states, None)
    sr, si = far_refs[0][:, early], far_refs[0][:, late]
    for k in range(1, len(far_refs)):
        row = slice(4 + k, 5 + k)
        mr, mi = cmul(powers_ref[row, early], powers_ref[row, late], far_refs[k][:, early], far_refs[k][:, late])
        sr, si = sr + mr, si + mi
    mr, mi = cmul(powers_ref[0:1, early], powers_ref[0:1, late], sr, si)
    second = odd == (0 if backwards else 1)
    out_ref[:, early] = jnp.where(second, mr + beside_ref[:, early], sr)
    out_ref[:, late] = jnp.where(second, mi + beside_ref[:, late], si)


def join_kernel(mine_ref, other_ref, powers_ref, out_ref, *, row):
    states = out_ref.shape[1] // 2
    early, late = slice(0, states), slice(states, None)
    row = slice(row, row + 1)
    mr, mi = cmul(powers_ref[row, early], powers_ref[row, late], other_ref[:, early], other_ref[:, late])
    out_ref[:, early] = mine_ref[:, early] + mr
    out_ref[:, late] = mine_ref[:, late] + mi


def pair_kernel(where_ref, mine_ref, other_ref, powers_ref, out_ref, *, backwards):
    states = out_ref.shape[1] // 2
    second = where_ref[0] % 2 == (0 if backwards else 1)
    lr, li = powers_ref[0:1, :states], powers_ref[0:1, states:]
    pick = lambda first, part: jnp.where(second == first, other_ref[:, part], mine_ref[:, part])
    early, late = slice(0, states), slice(states, None)
    mr, mi = cmul(lr, li, pick(True, early), pick(True, late))
    out_ref[:, :states] = mr + pick(False, early)
    out_ref[:, states:] = mi + pick(False, late)


def assemble_input(packs, shard, out_ref):
    per = packs[0].shape[0] - PARAM_ROWS
    half = per // 2
    states = out_ref.shape[0] // 2
    for k, pack in enumerate(packs):
        at = pl.multiple_of((shard ^ k) * half, half)
        out_ref[pl.ds(at, half), :] = pack[:half, :]
        out_ref[pl.ds(states + at, half), :] = pack[half:per, :]


def input_pack_kernel(
    where_ref, in_real, in_imag, nu, theta, gamma, tok_all, cot_all, a_ref, logs, tok, cot, sems, row_sems
):
    per_s, width = in_real.shape
    rows = tok.shape[0]
    mine = pl.ds(pl.multiple_of(where_ref[1] * rows, BLOCK), rows)
    halves = [
        pltpu.make_async_copy(src.at[mine, :], dst, row_sems.at[n]) for n, (src, dst) in enumerate(((tok_all, tok), (cot_all, cot)))
    ]
    fetch(
        [(in_real, a_ref.at[pl.ds(0, per_s), :]), (in_imag, a_ref.at[pl.ds(per_s, per_s), :])]
        + [(ref, logs.at[n]) for n, ref in enumerate((nu, theta, gamma))],
        sems,
        halves,
    )
    modulus = jnp.exp(-jnp.exp(logs[0]))
    angle = jnp.exp(logs[1])
    rest = [modulus * jnp.cos(angle), modulus * jnp.sin(angle), jnp.exp(logs[2])]
    rows = []
    for _ in range(3):
        for n in range(3):
            high = rest[n].astype(BF16).astype(F32)
            rows.append(high)
            rest[n] = rest[n] - high
    table = jnp.concatenate(rows + [jnp.zeros((PARAM_ROWS - 9, per_s), F32)], axis=0)
    table = jnp.concatenate([table] * (width // per_s), axis=1)
    here = lax.broadcasted_iota(jnp.int32, (PARAM_ROWS, width), 1) // per_s == where_ref[2]
    a_ref[2 * per_s :, :] = jnp.where(here, table, 0.0).astype(BF16)
    for copy in halves:
        copy.wait()


def weight_pack_kernel(out_real, out_imag, up, gate, down, b_ref, g_ref, sems):
    per_s, per_f = out_real.shape[0], down.shape[0]
    fetch(
        [
            (out_real, b_ref.at[pl.ds(0, per_s), :]),
            (out_imag, b_ref.at[pl.ds(per_s, per_s), :]),
            (down, b_ref.at[pl.ds(2 * per_s, per_f), :]),
            (up, g_ref.at[:, pl.ds(0, per_f)]),
            (gate, g_ref.at[:, pl.ds(per_f, per_f)]),
        ],
        sems,
    )


def mask_rows(lens_ref, where_ref, seq, seqs, length, width):
    left = lens_ref[where_ref[1] * seqs + seq] - where_ref[0] * length
    return lax.broadcasted_iota(jnp.int32, (length, width), 0) < left


def norm_kernel(
    where_ref, tok, cot, gain_all, bias_all, lens_all, low_ref, normed_ref, inv_ref, cotm_ref,
    gain_ref, bias_ref, lens_ref, sems, *, length
):
    rows, width = low_ref.shape
    fetch([(gain_all, gain_ref), (bias_all, bias_ref), (lens_all, lens_ref)], sems)
    for block in range(rows // BLOCK):
        span = slice(block * BLOCK, (block + 1) * BLOCK)
        normed, inv_scale = layer_norm(tok[span, :].astype(F32))
        normed_ref[span, :] = normed
        inv_ref[span, :] = jnp.broadcast_to(inv_scale, (BLOCK, inv_ref.shape[1]))
        low_ref[span, :] = (normed * gain_ref[...] + bias_ref[...]).astype(BF16)
        for seq in range(block * BLOCK // length, (block + 1) * BLOCK // length):
            span = slice(seq * length, (seq + 1) * length)
            live = mask_rows(lens_ref, where_ref, seq, rows // length, length, width)
            cotm_ref[span, :] = jnp.where(live, cot[span, :].astype(F32), 0.0).astype(BF16)


def weighted_ends(drive_ref, weigh, length, first, ends_ref):
    rows, lanes = drive_ref.shape
    states = lanes // 2
    for s in range(rows // length):
        er = ei = jnp.zeros((TILE, states), F32)
        for n in range(length // TILE):
            at = s * length + n * TILE
            mr, mi = cmul(
                weigh[0, n * TILE : (n + 1) * TILE, :],
                weigh[1, n * TILE : (n + 1) * TILE, :],
                drive_ref[at : at + TILE, :states],
                drive_ref[at : at + TILE, states:],
            )
            er, ei = er + mr, ei + mi
        ends_ref[pl.ds(first + s, 1), :states] = jnp.sum(er, axis=0, keepdims=True)
        ends_ref[pl.ds(first + s, 1), states:] = jnp.sum(ei, axis=0, keepdims=True)


def drive_kernel(where_ref, low_all, a0, a1, a2, a3, drive_all, ends_ref, powers_ref, in_t, weigh, *, length):
    packs = (a0, a1, a2, a3)
    states = in_t.shape[0] // 2
    assemble_input(packs, where_ref[2], in_t)
    dr, di, gain = read_params(packs, a0.shape[0] - PARAM_ROWS)
    fill_powers(dr, di, True, 0, weigh)
    gam = jnp.concatenate([gain, gain], axis=1)
    lr, li = cmul(weigh[0, :1, :], weigh[1, :1, :], dr, di)
    rows = [(lr, li)] + [cmul(lr, li, lr, li)]
    for _ in range(2):
        rows.append(cmul(*rows[-1], *rows[-1]))
    rows.append((jnp.ones_like(lr), jnp.zeros_like(lr)))
    for _ in range(3):
        rows.append(cmul(*cmul(*rows[-1], *rows[-1]), *rows[1]))
    for k, (lr, li) in enumerate(rows):
        powers_ref[k : k + 1, :] = jnp.concatenate([lr, li], axis=1)
    per_block = LARGE // length

    def body(block, view):
        low_ref, drive_ref = view(low_all), view(drive_all)
        drive_ref[...] = dot_nt(low_ref[...], in_t[...]) * gam
        weighted_ends(drive_ref, weigh, length, block * per_block, ends_ref)

    each_block(low_all.shape[0], LARGE, body)


def scan_kernel(drive_all, a0, a1, a2, a3, local_all, step, *, length, backwards):
    dr, di, _ = read_params((a0, a1, a2, a3), a0.shape[0] - PARAM_ROWS)
    fill_steps(dr, di, backwards, step)
    each_block(
        drive_all.shape[0],
        BLOCK,
        lambda block, view: scan_block(view(drive_all), view(local_all), step, length, backwards),
    )


def hidden_kernel(where_ref, cotm_all, b0, b1, b2, b3, hg_all, *, per_s):
    shard = where_ref[2]
    per_f = hg_all.shape[1] // TENSOR

    def body(block, view):
        hg_ref, cotm = view(hg_all), view(cotm_all)[...]
        for k, pack in enumerate((b0, b1, b2, b3)):
            at = pl.multiple_of((shard ^ k) * per_f, per_f)
            hg_ref[:, pl.ds(at, per_f)] = dot_nt(cotm, pack[2 * per_s :, :]).astype(BF16)

    each_block(cotm_all.shape[0], LARGE, body)


def middle_kernel(where_ref, *refs, length, levels):
    far_refs, refs = refs[:levels], refs[levels:]
    beside_ref, powers_ref, local_all, normed_all, hg_all, cotm_all, a0, a1, a2, a3 = refs[:10]
    gain_ref, bias_ref, skip_ref, b0, b1, b2, b3, g0, g1, g2, g3 = refs[10:21]
    state_all, back_all, backends_ref, ylow_all, hid_all, own_ref, sent_ref = refs[21:28]
    c_all, ug_all, weigh, full, carry, act_ref, ul, acc_out, acc_down, acc_ug, sems = refs[28:]
    place, core, shard = where_ref[0], where_ref[1], where_ref[2]
    side = shard // 2
    states = c_all.shape[0] // 2
    rows, width = normed_all.shape
    per_block = LARGE // length
    per_s = states // TENSOR
    per_f = hid_all.shape[1] // TENSOR

    copies = []
    for k, (pack, gates) in enumerate(((b0, g0), (b1, g1), (b2, g2), (b3, g3))):
        t = shard ^ k
        moves = (
            (pack.at[pl.ds(0, per_s), :], c_all.at[pl.ds(pl.multiple_of(t * per_s, per_s), per_s), :]),
            (pack.at[pl.ds(per_s, per_s), :], c_all.at[pl.ds(pl.multiple_of(states + t * per_s, per_s), per_s), :]),
            (gates, ug_all.at[:, pl.ds(pl.multiple_of(t * 2 * per_f, 2 * per_f), 2 * per_f)]),
        )
        for n, (src, dst) in enumerate(moves):
            copies.append(pltpu.make_async_copy(src, dst, sems.at[k, n]))
    for copy in copies:
        copy.start()
    dr, di, _ = read_params((a0, a1, a2, a3), a0.shape[0] - PARAM_ROWS)
    fill_powers(dr, di, False, 1, full)
    incoming(far_refs, beside_ref, place % 2, powers_ref, False, carry)
    fill_powers(dr, di, False, 0, weigh)
    acc_out[...] = jnp.zeros(acc_out.shape, F32)
    acc_down[...] = jnp.zeros(acc_down.shape, F32)
    acc_ug[...] = jnp.zeros(acc_ug.shape, F32)
    for copy in copies:
        copy.wait()
    skip = skip_ref[...]
    skip_gain, skip_bias = gain_ref[...] * skip, bias_ref[...] * skip

    def body(block, view):
        local_ref, state_ref, hid_ref, ylow_ref = view(local_all), view(state_all), view(hid_all), view(ylow_all)
        hg_ref, back_ref = view(hg_all), view(back_all)
        for s in range(per_block):
            seq = block * per_block + s
            span = slice(s * length, (s + 1) * length)
            sr = carry[pl.ds(seq, 1), :states]
            si = carry[pl.ds(seq, 1), states:]
            mr, mi = cmul(full[0], full[1], sr, si)
            state_ref[span, :states] = (local_ref[span, :states] + mr).astype(BF16)
            state_ref[span, states:] = (-(local_ref[span, states:] + mi)).astype(BF16)
        y = dot(state_ref[...], c_all[...]) + (view(normed_all)[...] * skip_gain + skip_bias)
        square = y * y
        th = jnp.tanh(y * (GELU_K + (GELU_K * 0.044715) * square))
        half_y = 0.5 * y
        act_ref[...] = (half_y + half_y * th).astype(BF16)
        slope = (0.5 + 0.5 * th) + half_y * (1.0 - th * th) * (GELU_K + (GELU_K * 3 * 0.044715) * square)
        act = act_ref[...]
        for t in range(TENSOR):
            both = dot(act, ug_all[:, 2 * per_f * t : 2 * per_f * (t + 1)])
            up = both[:, :per_f]
            th = 0.5 * jnp.tanh(0.5 * both[:, per_f:])
            sig = 0.5 + th
            hid_ref[:, per_f * t : per_f * (t + 1)] = (up * sig).astype(BF16)
            up_grad = hg_ref[:, per_f * t : per_f * (t + 1)].astype(F32) * sig
            ul[:, 2 * per_f * t : 2 * per_f * t + per_f] = up_grad.astype(BF16)
            ul[:, 2 * per_f * t + per_f : 2 * per_f * (t + 1)] = (up_grad * up * (0.5 - th)).astype(BF16)
        y_grad = dot_nt(ul[...], ug_all[...]) * slope
        ylow_ref[...] = y_grad.astype(BF16)
        back_ref[...] = dot_nt(ylow_ref[...], c_all[...])
        acc_ug[...] += dot_tn(act, ul[:, pl.ds(pl.multiple_of(side * 4 * per_f, 4 * per_f), 4 * per_f)])
        hid = hid_ref[:, pl.ds(pl.multiple_of(side * 2 * per_f, 2 * per_f), 2 * per_f)]
        acc_down[...] += dot_tn(hid, view(cotm_all)[...])
        for k in range(2):
            cols = state_ref[:, pl.ds(pl.multiple_of(k * states + side * 2 * per_s, 2 * per_s), 2 * per_s)]
            acc_out[k * 2 * per_s : (k + 1) * 2 * per_s, :] += dot_tn(cols, ylow_ref[...])
        weighted_ends(back_ref, weigh, length, block * per_block, backends_ref)

    each_block(rows, LARGE, body)
    for n, ref in ((core, own_ref), (1 - core, sent_ref)):
        for k in range(2):
            part = acc_out[pl.ds(pl.multiple_of(2 * per_s * k + n * per_s, per_s), per_s), :]
            ref[k * per_s : (k + 1) * per_s, :] = part.astype(ref.dtype)
        part = acc_down[pl.ds(pl.multiple_of(n * per_f, per_f), per_f), :]
        ref[2 * per_s : 2 * per_s + per_f, :] = part.astype(ref.dtype)
        part = acc_ug[:, pl.ds(pl.multiple_of(n * 2 * per_f, 2 * per_f), 2 * per_f)]
        ref[2 * per_s + per_f : 2 * per_s + per_f + width, :] = part.astype(ref.dtype)


def down_kernel(where_ref, lens_ref, tok, hid_all, b0, b1, b2, b3, out_all, down_all, *, length, per_s):
    shard = where_ref[2]
    rows, width = out_all.shape
    per_block = LARGE // length
    per_f = down_all.shape[0] // TENSOR
    for k, pack in enumerate((b0, b1, b2, b3)):
        down_all[pl.ds(pl.multiple_of((shard ^ k) * per_f, per_f), per_f), :] = pack[2 * per_s :, :]

    def body(block, view):
        added = dot(view(hid_all)[...], down_all[...])
        out_ref, tok_ref = view(out_all), view(tok)
        for s in range(per_block):
            span = slice(s * length, (s + 1) * length)
            live = mask_rows(lens_ref, where_ref, block * per_block + s, rows // length, length, width)
            out_ref[span, :] = jnp.where(live, tok_ref[span, :].astype(F32) + added[span, :], 0.0).astype(BF16)

    each_block(rows, LARGE, body)


def last_kernel(where_ref, *refs, length, levels):
    far_refs, refs = refs[:levels], refs[levels:]
    beside_ref, powers_ref, low_all, normed_all, inv_all, cotm_all, back_all, state_all, ylow_all = refs[:9]
    a0, a1, a2, a3, gain_ref, bias_ref, skip_ref, grad_all, own_ref, sent_ref = refs[9:19]
    in_t, full, carry, dlow, in_grad, lam_grad, vec_grad = refs[19:]
    place, core, shard = where_ref[0], where_ref[1], where_ref[2]
    states = in_t.shape[0] // 2
    rows, width = low_all.shape
    per_block = LARGE // length
    per_s = states // TENSOR
    packs = (a0, a1, a2, a3)

    assemble_input(packs, shard, in_t)
    dr, di, gain = read_params(packs, a0.shape[0] - PARAM_ROWS)
    fill_powers(dr, di, True, 1, full)
    incoming(far_refs, beside_ref, place % 2, powers_ref, True, carry)
    in_grad[...] = jnp.zeros(in_grad.shape, F32)
    lam_grad[...] = jnp.zeros(lam_grad.shape, F32)
    vec_grad[...] = jnp.zeros(vec_grad.shape, F32)
    at = pl.multiple_of((shard // 2) * 2 * per_s, 2 * per_s)

    def body(block, view):
        back_ref, state_ref = view(back_all), view(state_all)
        for s in range(per_block):
            seq = block * per_block + s
            span = slice(s * length, (s + 1) * length)
            sr = carry[pl.ds(seq, 1), :states]
            si = carry[pl.ds(seq, 1), states:]
            mr, mi = cmul(full[0], full[1], sr, si)
            gr = back_ref[span, :states] + mr
            gi = back_ref[span, states:] + mi
            dlow[span, :states] = (gr * gain).astype(BF16)
            dlow[span, states:] = (gi * -gain).astype(BF16)
            nr = jnp.concatenate([gr[1:], sr], axis=0)
            ni = jnp.concatenate([gi[1:], si], axis=0)
            hr = state_ref[span, :states].astype(F32)
            hi = state_ref[span, states:].astype(F32)
            lam_grad[:, :states] += jnp.sum(nr * hr + ni * hi, axis=0, keepdims=True)
            lam_grad[:, states:] += jnp.sum(nr * hi - ni * hr, axis=0, keepdims=True)
        normed = view(normed_all)[...]
        ylow = view(ylow_all)[...].astype(F32)
        low = view(low_all)[...]
        u_grad = dot(dlow[...], in_t[...]) + ylow * skip_ref[...]
        vec_grad[0:1, :] += jnp.sum(u_grad * normed, axis=0, keepdims=True)
        vec_grad[1:2, :] += jnp.sum(u_grad, axis=0, keepdims=True)
        vec_grad[2:3, :] += jnp.sum(ylow * (normed * gain_ref[...] + bias_ref[...]), axis=0, keepdims=True)
        scaled = u_grad * gain_ref[...]
        grad = (
            scaled
            - jnp.mean(scaled, axis=-1, keepdims=True)
            - normed * jnp.mean(scaled * normed, axis=-1, keepdims=True)
        )
        view(grad_all)[...] = (view(cotm_all)[...].astype(F32) + view(inv_all)[:, :1] * grad).astype(BF16)
        for k in range(2):
            cols = dlow[:, pl.ds(k * states + at, 2 * per_s)]
            in_grad[2 * per_s * k : 2 * per_s * (k + 1), :] += dot_tn(cols, low)

    each_block(rows, LARGE, body)
    small = jnp.concatenate(
        [vec_grad[:3, :], lam_grad[...], jnp.zeros((PARAM_ROWS - 4, width), F32)], axis=0
    ).astype(BF16)
    for n, ref in ((core, own_ref), (1 - core, sent_ref)):
        for k in range(2):
            part = in_grad[pl.ds(pl.multiple_of(2 * per_s * k + n * per_s, per_s), per_s), :]
            ref[k * per_s : (k + 1) * per_s, :] = part.astype(BF16)
        ref[2 * per_s :, :] = small


def join_halves_kernel(where_ref, own_ref, other_ref, out_ref, sems):
    rows = own_ref.shape[0]
    copies = [
        pltpu.make_async_copy(ref, out_ref.at[pl.ds(pl.multiple_of(n * rows, BLOCK), rows), :], sems.at[k])
        for k, (n, ref) in enumerate(((where_ref[1], own_ref), (1 - where_ref[1], other_ref)))
    ]
    for copy in copies:
        copy.start()
    for copy in copies:
        copy.wait()


def widen_halves_kernel(where_ref, own_ref, other_ref, out_ref, wide, sems):
    rows = own_ref.shape[0]
    slots = wide.shape[0]
    flying = []
    for n in range(2 * rows // BLOCK):
        slot = n % slots
        if n >= slots:
            flying[n - slots].wait()
        at = (n // 2) * BLOCK
        half, ref = ((where_ref[1], own_ref), (1 - where_ref[1], other_ref))[n % 2]
        wide[slot] = ref[at : at + BLOCK, :].astype(F32)
        copy = pltpu.make_async_copy(
            wide.at[slot], out_ref.at[pl.ds(pl.multiple_of(half * rows + at, BLOCK), BLOCK), :], sems.at[slot]
        )
        copy.start()
        flying.append(copy)
    for copy in flying[-slots:]:
        copy.wait()


def fold_kernel(where_ref, own_ref, other_ref, keep_ref, send_ref):
    half = keep_ref.shape[0]
    odd = where_ref[0] % 2
    at = pl.multiple_of(odd * half, 16)
    keep_ref[...] = own_ref[pl.ds(at, half), :] + other_ref[pl.ds(at, half), :].astype(F32)
    at = pl.multiple_of((1 - odd) * half, 16)
    send_ref[...] = (own_ref[pl.ds(at, half), :] + other_ref[pl.ds(at, half), :].astype(F32)).astype(BF16)


def deal_kernel(where_ref, own_ref, other_ref, keep_ref, *send_refs):
    rows = keep_ref.shape[0]
    for k, ref in enumerate((keep_ref,) + send_refs):
        at = pl.multiple_of(((where_ref[0] // 2) ^ k) * rows, 16)
        ref[...] = (own_ref[pl.ds(at, rows), :] + other_ref[pl.ds(at, rows), :].astype(F32)).astype(ref.dtype)


def unpack_kernel(where_ref, *refs, ways):
    parts, (real_ref, imag_ref, up_ref, gate_ref, down_ref, total, sems) = refs[: ways + 2], refs[ways + 2 :]
    place = where_ref[0]
    rows = parts[0].shape[0]
    for n in range(2 * ways):
        k = n % ways
        half = place % 2 if n < ways else 1 - place % 2
        at = (half * ways + ((place // 2) ^ k)) * rows
        if n <= ways:
            part = parts[n][...]
        else:
            part = parts[-1][(k - 1) * rows : k * rows, :]
        total[pl.ds(pl.multiple_of(at, 16), rows), :] = part.astype(F32)
    per_s, per_f, width = real_ref.shape[0], down_ref.shape[0], up_ref.shape[0]
    first = 2 * per_s + per_f
    moves = [
        (total.at[pl.ds(first, width), pl.ds(0, per_f)], up_ref),
        (total.at[pl.ds(first, width), pl.ds(per_f, per_f)], gate_ref),
        (total.at[pl.ds(2 * per_s, per_f), :], down_ref),
        (total.at[pl.ds(0, per_s), :], real_ref),
        (total.at[pl.ds(per_s, per_s), :], imag_ref),
    ]
    fetch(moves, sems)


def finish_kernel(where_ref, mine_ref, other_ref, a_ref, logs_ref, *refs):
    outs, (grads_ref, logs, sems) = refs[:8], refs[8:]
    width = grads_ref.shape[1]
    per_s = logs_ref.shape[2]
    grads = mine_ref[...].astype(F32) + other_ref[...].astype(F32)
    grads_ref[...] = grads
    lam = [jnp.zeros((1, per_s), F32), jnp.zeros((1, per_s), F32)]
    for t in range(TENSOR):
        for n in range(2):
            at = (n * TENSOR + t) * per_s
            part = grads[2 * per_s + 3 : 2 * per_s + 4, at : at + per_s]
            lam[n] = jnp.where(where_ref[2] == t, part, lam[n])
    decay = jnp.exp(logs_ref[0])
    modulus = jnp.exp(-decay)
    angle = jnp.exp(logs_ref[1])
    cos, sin = jnp.cos(angle), jnp.sin(angle)
    logs[0] = -decay * modulus * (lam[0] * cos + lam[1] * sin)
    logs[1] = angle * modulus * (lam[1] * cos - lam[0] * sin)
    terms = a_ref[:per_s, :].astype(F32) * grads[:per_s, :] + a_ref[per_s : 2 * per_s, :].astype(F32) * grads[per_s : 2 * per_s, :]
    logs[2] = jnp.sum(terms.T, axis=0, keepdims=True)
    moves = [(grads_ref.at[pl.ds(2 * per_s + n, 1), :], outs[n]) for n in range(3)]
    moves += [(grads_ref.at[pl.ds(n * per_s, per_s), :], outs[3 + n]) for n in range(2)]
    moves += [(logs.at[n], outs[5 + n]) for n in range(3)]
    fetch(moves, sems)


def near(value):
    return pltpu.with_memory_space_constraint(value, pltpu.VMEM)


def call(kernel, scalars, inputs, outs, scratch, vmem, far_inputs=(), far_outs=()):
    here, anywhere = pl.BlockSpec(memory_space=pltpu.VMEM), pl.BlockSpec(memory_space=pl.ANY)
    single = not isinstance(outs, list)
    listed = [outs] if single else outs
    shapes = [
        jax.ShapeDtypeStruct(*out) if n in far_outs else pltpu.VMEM(*out) for n, out in enumerate(listed)
    ]
    out_specs = [anywhere if n in far_outs else here for n in range(len(listed))]
    return pl.pallas_call(
        kernel,
        in_specs=[pl.BlockSpec(memory_space=pltpu.SMEM)] * len(scalars)
        + [anywhere if n in far_inputs else here for n in range(len(inputs))],
        out_specs=out_specs[0] if single else out_specs,
        out_shape=shapes[0] if single else shapes,
        scratch_shapes=scratch,
        compiler_params=pltpu.CompilerParams(vmem_limit_bytes=vmem * MIB),
    )(
        *scalars,
        *[
            pltpu.with_memory_space_constraint(v, pltpu.HBM) if n in far_inputs else near(v)
            for n, v in enumerate(inputs)
        ],
    )


def core_swap(value):
    return lax.ppermute(value, "tensor", [(t, t ^ 1) for t in range(TENSOR)])


def side_swap(value):
    return lax.ppermute(value, "tensor", [(t, t ^ 2) for t in range(TENSOR)])


def gather_tensor(own, *first):
    across = after(side_swap(own), *first)
    return own, core_swap(own), across, core_swap(across)


def after(value, *first):
    return lax.optimization_barrier((value,) + first)[0]


def flip_dp(value, bits, groups):
    return lax.ppermute(value, "dp", [(i, i ^ bits) for i in range(groups)])


def shift_dp(value, by, groups):
    return lax.ppermute(value, "dp", [(i, i + by) for i in range(groups) if 0 <= i + by < groups])


def shards(
    tokens,
    cotangent,
    ln_gain,
    ln_bias,
    skip_gain,
    in_real,
    in_imag,
    out_real,
    out_imag,
    nu_log,
    theta_log,
    gamma_log,
    up_weight,
    gate_weight,
    down_weight,
    lengths,
    *,
    groups,
):
    seqs, length, width = tokens.shape
    per_s = in_real.shape[1]
    per_f = up_weight.shape[1]
    states = per_s * TENSOR
    own_seqs = seqs // 2
    rows = own_seqs * length
    blocks = rows // BLOCK
    place = lax.axis_index("dp").astype(jnp.int32)
    shard = lax.axis_index("tensor").astype(jnp.int32)
    core = shard % 2
    where = jnp.stack([place, core, shard])

    tok_rows = tokens.reshape(seqs * length, width)
    cot_rows = cotangent.reshape(seqs * length, width)
    row = lambda v: v.reshape(1, width)
    gain_row, bias_row, skip_row = row(ln_gain), row(ln_bias), row(skip_gain)
    a_shape = (2 * per_s + PARAM_ROWS, width)
    b_shape = (2 * per_s + per_f, width)
    lanes = 2 * states
    units = TENSOR * per_f
    ends_shape = ((own_seqs, lanes), F32)
    dma = pltpu.SemaphoreType.DMA
    line = lambda v: v.reshape(1, per_s)

    pack_a, logs, own_tok, own_cot = call(
        input_pack_kernel,
        [where],
        [in_real.T, in_imag.T, line(nu_log), line(theta_log), line(gamma_log), tok_rows, cot_rows],
        [(a_shape, BF16), ((3, 1, per_s), F32), ((rows, width), BF16), ((rows, width), BF16)],
        [dma((5,)), dma((2,))],
        4,
        far_inputs=range(7),
    )
    pack_b, pack_g = call(
        weight_pack_kernel,
        [],
        [after(out_real, pack_a), out_imag, up_weight, gate_weight, down_weight],
        [(b_shape, BF16), ((width, 2 * per_f), BF16)],
        [dma((5,))],
        4,
        far_inputs=range(5),
    )
    low, normed, inv, cot_m = call(
        functools.partial(norm_kernel, length=length),
        [where],
        [own_tok, after(own_cot, pack_b), gain_row, bias_row, lengths],
        [((rows, width), BF16), ((rows, width), F32), ((rows, 128), F32), ((rows, width), BF16)],
        [
            pltpu.VMEM((1, width), F32),
            pltpu.VMEM((1, width), F32),
            pltpu.SMEM((seqs,), jnp.int32),
            dma((3,)),
        ],
        8,
        far_inputs=(2, 3, 4),
    )
    packs_a = gather_tensor(pack_a, low)
    pack_b, pack_g = after((pack_b, pack_g), packs_a[2])
    drive, ends, powers = call(
        functools.partial(drive_kernel, length=length),
        [where],
        [low, *packs_a],
        [((rows, lanes), F32), ends_shape, ((TILE, lanes), F32)],
        [pltpu.VMEM((lanes, width), BF16), pltpu.VMEM((2, length, states), F32)],
        8,
    )
    local = call(
        functools.partial(scan_kernel, length=length, backwards=False),
        [],
        [drive, *packs_a],
        ((rows, lanes), F32),
        [pltpu.VMEM((4, 2, TILE, states), F32)],
        8,
    )

    ways = groups // 2
    levels = (ways - 1).bit_length()

    def exchange(mine, backwards, beside_work, first_work=None):
        beside = after(flip_dp(mine, 1, groups), beside_work)
        both = call(
            functools.partial(pair_kernel, backwards=backwards), [where], [mine, beside, powers], ends_shape, [], 2
        )
        found = [both]
        from_far = []
        for k in range(levels):
            step = 2 << k
            from_far.append(shift_dp(found[-1], -step if backwards else step, groups))
            if k == 0 and first_work is not None:
                from_far[0] = after(from_far[0], first_work(both))
            if k + 1 < levels:
                found.append(
                    call(functools.partial(join_kernel, row=1 + k), [], [found[-1], from_far[-1], powers], ends_shape, [], 2)
                )
        return from_far, beside, found

    far_ends, beside_ends, found_ends = exchange(ends, False, local)
    packs_b = gather_tensor(pack_b, far_ends[0])
    hid_grad = call(
        functools.partial(hidden_kernel, per_s=per_s),
        [where],
        [after(cot_m, found_ends[-1]), *packs_b],
        ((rows, units), BF16),
        [],
        8,
    )
    packs_g = gather_tensor(pack_g, hid_grad, *far_ends)

    pack_rows = -(-(2 * per_s + per_f + width) // (16 * groups)) * 16 * groups
    state, back_drive, back_ends, y_low, hid, own_b, sent_b = call(
        functools.partial(middle_kernel, length=length, levels=levels),
        [where],
        [
            *far_ends,
            beside_ends,
            powers,
            local,
            normed,
            hid_grad,
            cot_m,
            *packs_a,
            gain_row,
            bias_row,
            skip_row,
            *packs_b,
            *packs_g,
        ],
        [
            ((rows, lanes), BF16),
            ((rows, lanes), F32),
            ends_shape,
            ((rows, width), BF16),
            ((rows, units), BF16),
            ((pack_rows, width), F32),
            ((pack_rows, width), BF16),
        ],
        [
            pltpu.VMEM((lanes, width), BF16),
            pltpu.VMEM((width, 2 * units), BF16),
            pltpu.VMEM((2, length, states), F32),
            pltpu.VMEM((2, length, states), F32),
            pltpu.VMEM((own_seqs, lanes), F32),
            pltpu.VMEM((LARGE, width), BF16),
            pltpu.VMEM((LARGE, 2 * units), BF16),
            pltpu.VMEM((states, width), F32),
            pltpu.VMEM((2 * per_f, width), F32),
            pltpu.VMEM((width, 4 * per_f), F32),
            dma((TENSOR, 3)),
        ],
        24,
    )
    half, part = pack_rows // 2, pack_rows // groups
    keep_b, send_b = call(
        fold_kernel,
        [where],
        [own_b, core_swap(sent_b)],
        [((half, width), F32), ((half, width), BF16)],
        [],
        4,
    )
    made = []

    def scan_work(pair_back):
        made.append(
            call(
                functools.partial(scan_kernel, length=length, backwards=True),
                [],
                [after(back_drive, pair_back), *packs_a],
                ((rows, lanes), F32),
                [pltpu.VMEM((4, 2, TILE, states), F32)],
                8,
            )
        )
        return made[0]

    far_back, beside_back, found_back = exchange(back_ends, True, send_b, scan_work)
    back = made[0]
    half_b = flip_dp(after(send_b, beside_back), 1, groups)
    out_own = call(
        functools.partial(down_kernel, length=length, per_s=per_s),
        [where, lengths],
        [own_tok, after(hid, found_back[-1]), *packs_b],
        ((rows, width), BF16),
        [pltpu.VMEM((units, width), BF16)],
        8,
    )
    dealt = call(
        deal_kernel,
        [where],
        [after(keep_b, out_own, *far_back), half_b],
        [((part, width), F32)] + [((part, width), BF16)] * (ways - 1),
        [],
        4,
    )

    grad_own, own_a, sent_a = call(
        functools.partial(last_kernel, length=length, levels=levels),
        [where],
        [
            *far_back,
            after(beside_back, dealt[0]),
            powers,
            low,
            normed,
            inv,
            cot_m,
            back,
            state,
            y_low,
            *packs_a,
            gain_row,
            bias_row,
            skip_row,
        ],
        [((rows, width), BF16), (a_shape, BF16), (a_shape, BF16)],
        [
            pltpu.VMEM((lanes, width), BF16),
            pltpu.VMEM((2, length, states), F32),
            pltpu.VMEM((own_seqs, lanes), F32),
            pltpu.VMEM((LARGE, lanes), BF16),
            pltpu.VMEM((states, width), F32),
            pltpu.VMEM((1, lanes), F32),
            pltpu.VMEM((TILE, width), F32),
        ],
        12,
    )

    mine_b = dealt[0]
    for k in range(1, ways):
        mine_b = mine_b + flip_dp(dealt[k], 2 * k, groups).astype(F32)
    mine_b = mine_b.astype(BF16)
    gathered = [mine_b] + [flip_dp(mine_b, 2 * k, groups) for k in range(1, ways)]
    beside = [flip_dp(mine_b, 1, groups), flip_dp(jnp.concatenate(gathered[1:], axis=0), 1, groups)]

    grads_a = own_a.astype(F32) + after(core_swap(sent_a), mine_b).astype(F32)
    low_a = grads_a.astype(BF16)

    block_out = call(
        join_halves_kernel,
        [where],
        [out_own, core_swap(after(out_own, low_a))],
        [((seqs * length, width), BF16)],
        [dma((2,))],
        2,
        far_outs=(0,),
    )[0].reshape(seqs, length, width)
    input_grad = call(
        widen_halves_kernel,
        [where],
        [grad_own, core_swap(after(grad_own, low_a))],
        [((seqs * length, width), F32)],
        [pltpu.VMEM((4, BLOCK, width), F32), dma((4,))],
        4,
        far_outs=(0,),
    )[0].reshape(seqs, length, width)

    state_shape = ((per_s, width), F32)
    unpacked = call(
        functools.partial(unpack_kernel, ways=ways),
        [where],
        [*gathered, beside[0], after(beside[1], input_grad)],
        [state_shape] * 2 + [((width, per_f), F32)] * 2 + [((per_f, width), F32)],
        [pltpu.VMEM((pack_rows, width), F32), dma((5,))],
        8,
        far_outs=range(5),
    )
    works = {1: [block_out], 2: [beside[0]], 4: unpacked}
    bit = 1
    while bit < groups:
        other_a = after(flip_dp(low_a, bit, groups), *works.get(bit, []))
        bit *= 2
        if bit < groups:
            low_a = (low_a.astype(F32) + other_a.astype(F32)).astype(BF16)
        if bit == 4:
            low_a = after(low_a, *gathered)

    finished = call(
        finish_kernel,
        [where],
        [low_a, other_a, pack_a, logs],
        [((1, width), F32)] * 3 + [state_shape] * 2 + [((1, per_s), F32)] * 3,
        [pltpu.VMEM(a_shape, F32), pltpu.VMEM((3, 1, per_s), F32), dma((8,))],
        4,
        far_outs=range(8),
    )
    return (
        block_out,
        input_grad,
        *[v.reshape(width) for v in finished[:3]],
        *[v.T for v in finished[3:5]],
        *unpacked[:2],
        *[v.reshape(per_s) for v in finished[5:]],
        *unpacked[2:],
    )


def solution(mesh):
    rows = P(None, "dp", None)
    columns = P(None, "tensor")
    lines = P("tensor", None)
    vector = P("tensor")
    in_specs = (rows, rows, P(), P(), P(), columns, columns, lines, lines, vector, vector, vector, columns, columns, lines, P())
    out_specs = (rows, rows, P(), P(), P(), columns, columns, lines, lines, vector, vector, vector, columns, columns, lines)
    return jax.shard_map(
        functools.partial(shards, groups=mesh.shape["dp"]),
        mesh=mesh,
        in_specs=in_specs,
        out_specs=out_specs,
        check_vma=False,
    )
```

```python
import functools
import math

import jax
import jax.numpy as jnp
from jax import lax
from jax.experimental import pallas as pl
from jax.experimental.pallas import tpu as pltpu
from jax.sharding import PartitionSpec as P

EPSILON = 1e-05
TENSOR = 4
TILE = 8
BLOCK = 256
LARGE = 512
PARAM_ROWS = 16
F32 = jnp.float32
BF16 = jnp.bfloat16
GELU_K = math.sqrt(2.0 / math.pi)
MIB = 1024 * 1024


def dot(left, right):
    return jnp.dot(left, right, preferred_element_type=F32)


def dot_nt(left, right):
    return lax.dot_general(left, right, (((1,), (1,)), ((), ())), preferred_element_type=F32)


def dot_tn(left, right):
    return lax.dot_general(left, right, (((0,), (0,)), ((), ())), preferred_element_type=F32)


def layer_norm(rows):
    centre = jnp.mean(rows, axis=-1, keepdims=True)
    shifted = rows - centre
    variance = jnp.mean(shifted * shifted, axis=-1, keepdims=True)
    inv_scale = lax.rsqrt(variance + EPSILON)
    return shifted * inv_scale, inv_scale


def cmul(ar, ai, br, bi):
    return ar * br - ai * bi, ar * bi + ai * br


def read_params(packs, row):
    total = None
    for pack in packs:
        rows = pack[row : row + PARAM_ROWS, :].astype(F32)
        total = rows if total is None else total + rows
    states = total.shape[1] // 2
    at = lambda k: total[k : k + 1, :states] + total[k + 3 : k + 4, :states] + total[k + 6 : k + 7, :states]
    return at(0), at(1), at(2)


def powers_of(decay_real, decay_imag, exponent):
    out_r = jnp.ones(exponent.shape, F32)
    out_i = jnp.zeros(exponent.shape, F32)
    br, bi = decay_real, decay_imag
    for bit in range(4):
        mr, mi = cmul(out_r, out_i, br, bi)
        on = ((exponent >> bit) & 1) == 1
        out_r = jnp.where(on, mr, out_r)
        out_i = jnp.where(on, mi, out_i)
        br, bi = cmul(br, bi, br, bi)
    return out_r, out_i


def fill_steps(decay_real, decay_imag, backwards, step_ref):
    states = decay_real.shape[1]
    row = lax.broadcasted_iota(jnp.int32, (TILE, states), 0)
    if backwards:
        row = TILE - 1 - row
    zero = jnp.zeros((TILE, states), F32)
    for k, shift in enumerate((1, 2, 4)):
        pr, pi = powers_of(decay_real, decay_imag, jnp.full((TILE, states), shift, jnp.int32))
        step_ref[k, 0] = jnp.where(row >= shift, pr, zero)
        step_ref[k, 1] = jnp.where(row >= shift, pi, zero)
    step_ref[3, 0], step_ref[3, 1] = powers_of(decay_real, decay_imag, row + 1)


def fill_powers(decay_real, decay_imag, backwards, first, full_ref):
    states = decay_real.shape[1]
    row = lax.broadcasted_iota(jnp.int32, (TILE, states), 0)
    if backwards:
        row = TILE - 1 - row
    pr, pi = powers_of(decay_real, decay_imag, row + first)
    er, ei = powers_of(decay_real, decay_imag, jnp.full((TILE, states), TILE, jnp.int32))
    tiles = full_ref.shape[1] // TILE
    for n in range(tiles):
        at = (tiles - 1 - n if backwards else n) * TILE
        full_ref[0, at : at + TILE, :] = pr
        full_ref[1, at : at + TILE, :] = pi
        pr, pi = cmul(pr, pi, er, ei)


def scan_block(drive_ref, out_ref, step_ref, length, backwards):
    rows, lanes = drive_ref.shape
    states = lanes // 2
    tiles = length // TILE
    table = [(step_ref[k, 0], step_ref[k, 1]) for k in range(4)]
    edge = 0 if backwards else TILE - 1
    for s in range(rows // length):
        cr = ci = None
        for n in range(tiles):
            at = s * length + (tiles - 1 - n if backwards else n) * TILE
            hr = drive_ref[at : at + TILE, :states]
            hi = drive_ref[at : at + TILE, states:]
            for k, shift in enumerate((1, 2, 4)):
                turn = TILE - shift if backwards else shift
                sr = pltpu.roll(hr, turn, 0)
                si = pltpu.roll(hi, turn, 0)
                mr, mi = cmul(table[k][0], table[k][1], sr, si)
                hr, hi = hr + mr, hi + mi
            if cr is not None:
                mr, mi = cmul(table[3][0], table[3][1], cr, ci)
                hr, hi = hr + mr, hi + mi
            out_ref[at : at + TILE, :states] = hr
            out_ref[at : at + TILE, states:] = hi
            cr, ci = hr[edge : edge + 1], hi[edge : edge + 1]


def each_block(rows, size, body):
    def step(block, carry):
        at = pl.multiple_of(block * size, size)
        body(block, lambda ref: ref.at[pl.ds(at, size), :])
        return carry

    lax.fori_loop(0, rows // size, step, 0)


def fetch(pairs, sems, behind=()):
    copies = [pltpu.make_async_copy(src, dst, sems.at[n]) for n, (src, dst) in enumerate(pairs)]
    for copy in copies + list(behind):
        copy.start()
    for copy in copies:
        copy.wait()


def incoming(far_refs, beside_ref, odd, powers_ref, backwards, out_ref):
    states = out_ref.shape[1] // 2
    early, late = slice(0, states), slice(states, None)
    sr, si = far_refs[0][:, early], far_refs[0][:, late]
    for k in range(1, len(far_refs)):
        row = slice(4 + k, 5 + k)
        mr, mi = cmul(powers_ref[row, early], powers_ref[row, late], far_refs[k][:, early], far_refs[k][:, late])
        sr, si = sr + mr, si + mi
    mr, mi = cmul(powers_ref[0:1, early], powers_ref[0:1, late], sr, si)
    second = odd == (0 if backwards else 1)
    out_ref[:, early] = jnp.where(second, mr + beside_ref[:, early], sr)
    out_ref[:, late] = jnp.where(second, mi + beside_ref[:, late], si)


def join_kernel(mine_ref, other_ref, powers_ref, out_ref, *, row):
    states = out_ref.shape[1] // 2
    early, late = slice(0, states), slice(states, None)
    row = slice(row, row + 1)
    mr, mi = cmul(powers_ref[row, early], powers_ref[row, late], other_ref[:, early], other_ref[:, late])
    out_ref[:, early] = mine_ref[:, early] + mr
    out_ref[:, late] = mine_ref[:, late] + mi


def pair_kernel(where_ref, mine_ref, other_ref, powers_ref, out_ref, *, backwards):
    states = out_ref.shape[1] // 2
    second = where_ref[0] % 2 == (0 if backwards else 1)
    lr, li = powers_ref[0:1, :states], powers_ref[0:1, states:]
    pick = lambda first, part: jnp.where(second == first, other_ref[:, part], mine_ref[:, part])
    early, late = slice(0, states), slice(states, None)
    mr, mi = cmul(lr, li, pick(True, early), pick(True, late))
    out_ref[:, :states] = mr + pick(False, early)
    out_ref[:, states:] = mi + pick(False, late)


def assemble_input(packs, shard, out_ref):
    per = packs[0].shape[0] - PARAM_ROWS
    half = per // 2
    states = out_ref.shape[0] // 2
    for k, pack in enumerate(packs):
        at = pl.multiple_of((shard ^ k) * half, half)
        out_ref[pl.ds(at, half), :] = pack[:half, :]
        out_ref[pl.ds(states + at, half), :] = pack[half:per, :]


def input_pack_kernel(
    where_ref, in_real, in_imag, nu, theta, gamma, tok_all, cot_all, a_ref, logs, tok, cot, sems, row_sems
):
    per_s, width = in_real.shape
    rows = tok.shape[0]
    mine = pl.ds(pl.multiple_of(where_ref[1] * rows, BLOCK), rows)
    halves = [
        pltpu.make_async_copy(src.at[mine, :], dst, row_sems.at[n]) for n, (src, dst) in enumerate(((tok_all, tok), (cot_all, cot)))
    ]
    fetch(
        [(in_real, a_ref.at[pl.ds(0, per_s), :]), (in_imag, a_ref.at[pl.ds(per_s, per_s), :])]
        + [(ref, logs.at[n]) for n, ref in enumerate((nu, theta, gamma))],
        sems,
        halves,
    )
    modulus = jnp.exp(-jnp.exp(logs[0]))
    angle = jnp.exp(logs[1])
    rest = [modulus * jnp.cos(angle), modulus * jnp.sin(angle), jnp.exp(logs[2])]
    rows = []
    for _ in range(3):
        for n in range(3):
            high = rest[n].astype(BF16).astype(F32)
            rows.append(high)
            rest[n] = rest[n] - high
    table = jnp.concatenate(rows + [jnp.zeros((PARAM_ROWS - 9, per_s), F32)], axis=0)
    table = jnp.concatenate([table] * (width // per_s), axis=1)
    here = lax.broadcasted_iota(jnp.int32, (PARAM_ROWS, width), 1) // per_s == where_ref[2]
    a_ref[2 * per_s :, :] = jnp.where(here, table, 0.0).astype(BF16)
    for copy in halves:
        copy.wait()


def weight_pack_kernel(out_real, out_imag, up, gate, down, b_ref, g_ref, sems):
    per_s, per_f = out_real.shape[0], down.shape[0]
    fetch(
        [
            (out_real, b_ref.at[pl.ds(0, per_s), :]),
            (out_imag, b_ref.at[pl.ds(per_s, per_s), :]),
            (down, b_ref.at[pl.ds(2 * per_s, per_f), :]),
            (up, g_ref.at[:, pl.ds(0, per_f)]),
            (gate, g_ref.at[:, pl.ds(per_f, per_f)]),
        ],
        sems,
    )


def mask_rows(lens_ref, where_ref, seq, seqs, length, width):
    left = lens_ref[where_ref[1] * seqs + seq] - where_ref[0] * length
    return lax.broadcasted_iota(jnp.int32, (length, width), 0) < left


def norm_kernel(
    where_ref, tok, cot, gain_all, bias_all, lens_all, low_ref, normed_ref, inv_ref, cotm_ref,
    gain_ref, bias_ref, lens_ref, sems, *, length
):
    rows, width = low_ref.shape
    fetch([(gain_all, gain_ref), (bias_all, bias_ref), (lens_all, lens_ref)], sems)
    for block in range(rows // BLOCK):
        span = slice(block * BLOCK, (block + 1) * BLOCK)
        normed, inv_scale = layer_norm(tok[span, :].astype(F32))
        normed_ref[span, :] = normed
        inv_ref[span, :] = jnp.broadcast_to(inv_scale, (BLOCK, inv_ref.shape[1]))
        low_ref[span, :] = (normed * gain_ref[...] + bias_ref[...]).astype(BF16)
        for seq in range(block * BLOCK // length, (block + 1) * BLOCK // length):
            span = slice(seq * length, (seq + 1) * length)
            live = mask_rows(lens_ref, where_ref, seq, rows // length, length, width)
            cotm_ref[span, :] = jnp.where(live, cot[span, :].astype(F32), 0.0).astype(BF16)


def weighted_ends(drive_ref, weigh, length, first, ends_ref):
    rows, lanes = drive_ref.shape
    states = lanes // 2
    for s in range(rows // length):
        er = ei = jnp.zeros((TILE, states), F32)
        for n in range(length // TILE):
            at = s * length + n * TILE
            mr, mi = cmul(
                weigh[0, n * TILE : (n + 1) * TILE, :],
                weigh[1, n * TILE : (n + 1) * TILE, :],
                drive_ref[at : at + TILE, :states],
                drive_ref[at : at + TILE, states:],
            )
            er, ei = er + mr, ei + mi
        ends_ref[pl.ds(first + s, 1), :states] = jnp.sum(er, axis=0, keepdims=True)
        ends_ref[pl.ds(first + s, 1), states:] = jnp.sum(ei, axis=0, keepdims=True)


def drive_kernel(where_ref, low_all, a0, a1, a2, a3, drive_all, ends_ref, powers_ref, in_t, weigh, *, length):
    packs = (a0, a1, a2, a3)
    states = in_t.shape[0] // 2
    assemble_input(packs, where_ref[2], in_t)
    dr, di, gain = read_params(packs, a0.shape[0] - PARAM_ROWS)
    fill_powers(dr, di, True, 0, weigh)
    gam = jnp.concatenate([gain, gain], axis=1)
    lr, li = cmul(weigh[0, :1, :], weigh[1, :1, :], dr, di)
    rows = [(lr, li)] + [cmul(lr, li, lr, li)]
    for _ in range(2):
        rows.append(cmul(*rows[-1], *rows[-1]))
    rows.append((jnp.ones_like(lr), jnp.zeros_like(lr)))
    for _ in range(3):
        rows.append(cmul(*cmul(*rows[-1], *rows[-1]), *rows[1]))
    for k, (lr, li) in enumerate(rows):
        powers_ref[k : k + 1, :] = jnp.concatenate([lr, li], axis=1)
    per_block = LARGE // length

    def body(block, view):
        low_ref, drive_ref = view(low_all), view(drive_all)
        drive_ref[...] = dot_nt(low_ref[...], in_t[...]) * gam
        weighted_ends(drive_ref, weigh, length, block * per_block, ends_ref)

    each_block(low_all.shape[0], LARGE, body)


def scan_kernel(drive_all, a0, a1, a2, a3, local_all, step, *, length, backwards):
    dr, di, _ = read_params((a0, a1, a2, a3), a0.shape[0] - PARAM_ROWS)
    fill_steps(dr, di, backwards, step)
    each_block(
        drive_all.shape[0],
        BLOCK,
        lambda block, view: scan_block(view(drive_all), view(local_all), step, length, backwards),
    )


def hidden_kernel(where_ref, cotm_all, b0, b1, b2, b3, hg_all, *, per_s):
    shard = where_ref[2]
    per_f = hg_all.shape[1] // TENSOR

    def body(block, view):
        hg_ref, cotm = view(hg_all), view(cotm_all)[...]
        for k, pack in enumerate((b0, b1, b2, b3)):
            at = pl.multiple_of((shard ^ k) * per_f, per_f)
            hg_ref[:, pl.ds(at, per_f)] = dot_nt(cotm, pack[2 * per_s :, :]).astype(BF16)

    each_block(cotm_all.shape[0], LARGE, body)


def middle_kernel(where_ref, *refs, length, levels):
    far_refs, refs = refs[:levels], refs[levels:]
    beside_ref, powers_ref, local_all, normed_all, hg_all, cotm_all, a0, a1, a2, a3 = refs[:10]
    gain_ref, bias_ref, skip_ref, b0, b1, b2, b3, g0, g1, g2, g3 = refs[10:21]
    state_all, back_all, backends_ref, ylow_all, hid_all, own_ref, sent_ref = refs[21:28]
    c_all, ug_all, weigh, full, carry, act_ref, ul, acc_out, acc_down, acc_ug, sems = refs[28:]
    place, core, shard = where_ref[0], where_ref[1], where_ref[2]
    side = shard // 2
    states = c_all.shape[0] // 2
    rows, width = normed_all.shape
    per_block = LARGE // length
    per_s = states // TENSOR
    per_f = hid_all.shape[1] // TENSOR

    copies = []
    for k, (pack, gates) in enumerate(((b0, g0), (b1, g1), (b2, g2), (b3, g3))):
        t = shard ^ k
        moves = (
            (pack.at[pl.ds(0, per_s), :], c_all.at[pl.ds(pl.multiple_of(t * per_s, per_s), per_s), :]),
            (pack.at[pl.ds(per_s, per_s), :], c_all.at[pl.ds(pl.multiple_of(states + t * per_s, per_s), per_s), :]),
            (gates, ug_all.at[:, pl.ds(pl.multiple_of(t * 2 * per_f, 2 * per_f), 2 * per_f)]),
        )
        for n, (src, dst) in enumerate(moves):
            copies.append(pltpu.make_async_copy(src, dst, sems.at[k, n]))
    for copy in copies:
        copy.start()
    dr, di, _ = read_params((a0, a1, a2, a3), a0.shape[0] - PARAM_ROWS)
    fill_powers(dr, di, False, 1, full)
    incoming(far_refs, beside_ref, place % 2, powers_ref, False, carry)
    fill_powers(dr, di, False, 0, weigh)
    acc_out[...] = jnp.zeros(acc_out.shape, F32)
    acc_down[...] = jnp.zeros(acc_down.shape, F32)
    acc_ug[...] = jnp.zeros(acc_ug.shape, F32)
    for copy in copies:
        copy.wait()
    skip = skip_ref[...]
    skip_gain, skip_bias = gain_ref[...] * skip, bias_ref[...] * skip

    def body(block, view):
        local_ref, state_ref, hid_ref, ylow_ref = view(local_all), view(state_all), view(hid_all), view(ylow_all)
        hg_ref, back_ref = view(hg_all), view(back_all)
        for s in range(per_block):
            seq = block * per_block + s
            span = slice(s * length, (s + 1) * length)
            sr = carry[pl.ds(seq, 1), :states]
            si = carry[pl.ds(seq, 1), states:]
            mr, mi = cmul(full[0], full[1], sr, si)
            state_ref[span, :states] = (local_ref[span, :states] + mr).astype(BF16)
            state_ref[span, states:] = (-(local_ref[span, states:] + mi)).astype(BF16)
        y = dot(state_ref[...], c_all[...]) + (view(normed_all)[...] * skip_gain + skip_bias)
        square = y * y
        th = jnp.tanh(y * (GELU_K + (GELU_K * 0.044715) * square))
        half_y = 0.5 * y
        act_ref[...] = (half_y + half_y * th).astype(BF16)
        slope = (0.5 + 0.5 * th) + half_y * (1.0 - th * th) * (GELU_K + (GELU_K * 3 * 0.044715) * square)
        act = act_ref[...]
        for t in range(TENSOR):
            both = dot(act, ug_all[:, 2 * per_f * t : 2 * per_f * (t + 1)])
            up = both[:, :per_f]
            th = 0.5 * jnp.tanh(0.5 * both[:, per_f:])
            sig = 0.5 + th
            hid_ref[:, per_f * t : per_f * (t + 1)] = (up * sig).astype(BF16)
            up_grad = hg_ref[:, per_f * t : per_f * (t + 1)].astype(F32) * sig
            ul[:, 2 * per_f * t : 2 * per_f * t + per_f] = up_grad.astype(BF16)
            ul[:, 2 * per_f * t + per_f : 2 * per_f * (t + 1)] = (up_grad * up * (0.5 - th)).astype(BF16)
        y_grad = dot_nt(ul[...], ug_all[...]) * slope
        ylow_ref[...] = y_grad.astype(BF16)
        back_ref[...] = dot_nt(ylow_ref[...], c_all[...])
        acc_ug[...] += dot_tn(act, ul[:, pl.ds(pl.multiple_of(side * 4 * per_f, 4 * per_f), 4 * per_f)])
        hid = hid_ref[:, pl.ds(pl.multiple_of(side * 2 * per_f, 2 * per_f), 2 * per_f)]
        acc_down[...] += dot_tn(hid, view(cotm_all)[...])
        for k in range(2):
            cols = state_ref[:, pl.ds(pl.multiple_of(k * states + side * 2 * per_s, 2 * per_s), 2 * per_s)]
            acc_out[k * 2 * per_s : (k + 1) * 2 * per_s, :] += dot_tn(cols, ylow_ref[...])
        weighted_ends(back_ref, weigh, length, block * per_block, backends_ref)

    each_block(rows, LARGE, body)
    for n, ref in ((core, own_ref), (1 - core, sent_ref)):
        for k in range(2):
            part = acc_out[pl.ds(pl.multiple_of(2 * per_s * k + n * per_s, per_s), per_s), :]
            ref[k * per_s : (k + 1) * per_s, :] = part.astype(ref.dtype)
        part = acc_down[pl.ds(pl.multiple_of(n * per_f, per_f), per_f), :]
        ref[2 * per_s : 2 * per_s + per_f, :] = part.astype(ref.dtype)
        part = acc_ug[:, pl.ds(pl.multiple_of(n * 2 * per_f, 2 * per_f), 2 * per_f)]
        ref[2 * per_s + per_f : 2 * per_s + per_f + width, :] = part.astype(ref.dtype)


def down_kernel(where_ref, lens_ref, tok, hid_all, b0, b1, b2, b3, out_all, down_all, *, length, per_s):
    shard = where_ref[2]
    rows, width = out_all.shape
    per_block = LARGE // length
    per_f = down_all.shape[0] // TENSOR
    for k, pack in enumerate((b0, b1, b2, b3)):
        down_all[pl.ds(pl.multiple_of((shard ^ k) * per_f, per_f), per_f), :] = pack[2 * per_s :, :]

    def body(block, view):
        added = dot(view(hid_all)[...], down_all[...])
        out_ref, tok_ref = view(out_all), view(tok)
        for s in range(per_block):
            span = slice(s * length, (s + 1) * length)
            live = mask_rows(lens_ref, where_ref, block * per_block + s, rows // length, length, width)
            out_ref[span, :] = jnp.where(live, tok_ref[span, :].astype(F32) + added[span, :], 0.0).astype(BF16)

    each_block(rows, LARGE, body)


def last_kernel(where_ref, *refs, length, levels):
    far_refs, refs = refs[:levels], refs[levels:]
    beside_ref, powers_ref, low_all, normed_all, inv_all, cotm_all, back_all, state_all, ylow_all = refs[:9]
    a0, a1, a2, a3, gain_ref, bias_ref, skip_ref, grad_all, own_ref, sent_ref = refs[9:19]
    in_t, full, carry, dlow, in_grad, lam_grad, vec_grad = refs[19:]
    place, core, shard = where_ref[0], where_ref[1], where_ref[2]
    states = in_t.shape[0] // 2
    rows, width = low_all.shape
    per_block = LARGE // length
    per_s = states // TENSOR
    packs = (a0, a1, a2, a3)

    assemble_input(packs, shard, in_t)
    dr, di, gain = read_params(packs, a0.shape[0] - PARAM_ROWS)
    fill_powers(dr, di, True, 1, full)
    incoming(far_refs, beside_ref, place % 2, powers_ref, True, carry)
    in_grad[...] = jnp.zeros(in_grad.shape, F32)
    lam_grad[...] = jnp.zeros(lam_grad.shape, F32)
    vec_grad[...] = jnp.zeros(vec_grad.shape, F32)
    at = pl.multiple_of((shard // 2) * 2 * per_s, 2 * per_s)

    def body(block, view):
        back_ref, state_ref = view(back_all), view(state_all)
        for s in range(per_block):
            seq = block * per_block + s
            span = slice(s * length, (s + 1) * length)
            sr = carry[pl.ds(seq, 1), :states]
            si = carry[pl.ds(seq, 1), states:]
            mr, mi = cmul(full[0], full[1], sr, si)
            gr = back_ref[span, :states] + mr
            gi = back_ref[span, states:] + mi
            dlow[span, :states] = (gr * gain).astype(BF16)
            dlow[span, states:] = (gi * -gain).astype(BF16)
            nr = jnp.concatenate([gr[1:], sr], axis=0)
            ni = jnp.concatenate([gi[1:], si], axis=0)
            hr = state_ref[span, :states].astype(F32)
            hi = state_ref[span, states:].astype(F32)
            lam_grad[:, :states] += jnp.sum(nr * hr + ni * hi, axis=0, keepdims=True)
            lam_grad[:, states:] += jnp.sum(nr * hi - ni * hr, axis=0, keepdims=True)
        normed = view(normed_all)[...]
        ylow = view(ylow_all)[...].astype(F32)
        low = view(low_all)[...]
        u_grad = dot(dlow[...], in_t[...]) + ylow * skip_ref[...]
        vec_grad[0:1, :] += jnp.sum(u_grad * normed, axis=0, keepdims=True)
        vec_grad[1:2, :] += jnp.sum(u_grad, axis=0, keepdims=True)
        vec_grad[2:3, :] += jnp.sum(ylow * (normed * gain_ref[...] + bias_ref[...]), axis=0, keepdims=True)
        scaled = u_grad * gain_ref[...]
        grad = (
            scaled
            - jnp.mean(scaled, axis=-1, keepdims=True)
            - normed * jnp.mean(scaled * normed, axis=-1, keepdims=True)
        )
        view(grad_all)[...] = (view(cotm_all)[...].astype(F32) + view(inv_all)[:, :1] * grad).astype(BF16)
        for k in range(2):
            cols = dlow[:, pl.ds(k * states + at, 2 * per_s)]
            in_grad[2 * per_s * k : 2 * per_s * (k + 1), :] += dot_tn(cols, low)

    each_block(rows, LARGE, body)
    small = jnp.concatenate(
        [vec_grad[:3, :], lam_grad[...], jnp.zeros((PARAM_ROWS - 4, width), F32)], axis=0
    ).astype(BF16)
    for n, ref in ((core, own_ref), (1 - core, sent_ref)):
        for k in range(2):
            part = in_grad[pl.ds(pl.multiple_of(2 * per_s * k + n * per_s, per_s), per_s), :]
            ref[k * per_s : (k + 1) * per_s, :] = part.astype(BF16)
        ref[2 * per_s :, :] = small


def join_halves_kernel(where_ref, own_ref, other_ref, out_ref, sems):
    rows = own_ref.shape[0]
    copies = [
        pltpu.make_async_copy(ref, out_ref.at[pl.ds(pl.multiple_of(n * rows, BLOCK), rows), :], sems.at[k])
        for k, (n, ref) in enumerate(((where_ref[1], own_ref), (1 - where_ref[1], other_ref)))
    ]
    for copy in copies:
        copy.start()
    for copy in copies:
        copy.wait()


def widen_halves_kernel(where_ref, own_ref, other_ref, out_ref, wide, sems):
    rows = own_ref.shape[0]
    slots = wide.shape[0]
    flying = []
    for n in range(2 * rows // BLOCK):
        slot = n % slots
        if n >= slots:
            flying[n - slots].wait()
        at = (n // 2) * BLOCK
        half, ref = ((where_ref[1], own_ref), (1 - where_ref[1], other_ref))[n % 2]
        wide[slot] = ref[at : at + BLOCK, :].astype(F32)
        copy = pltpu.make_async_copy(
            wide.at[slot], out_ref.at[pl.ds(pl.multiple_of(half * rows + at, BLOCK), BLOCK), :], sems.at[slot]
        )
        copy.start()
        flying.append(copy)
    for copy in flying[-slots:]:
        copy.wait()


def fold_kernel(where_ref, own_ref, other_ref, keep_ref, send_ref):
    half = keep_ref.shape[0]
    odd = where_ref[0] % 2
    at = pl.multiple_of(odd * half, 16)
    keep_ref[...] = own_ref[pl.ds(at, half), :] + other_ref[pl.ds(at, half), :].astype(F32)
    at = pl.multiple_of((1 - odd) * half, 16)
    send_ref[...] = (own_ref[pl.ds(at, half), :] + other_ref[pl.ds(at, half), :].astype(F32)).astype(BF16)


def deal_kernel(where_ref, own_ref, other_ref, keep_ref, *send_refs):
    rows = keep_ref.shape[0]
    for k, ref in enumerate((keep_ref,) + send_refs):
        at = pl.multiple_of(((where_ref[0] // 2) ^ k) * rows, 16)
        ref[...] = (own_ref[pl.ds(at, rows), :] + other_ref[pl.ds(at, rows), :].astype(F32)).astype(ref.dtype)


def unpack_kernel(where_ref, *refs, ways):
    parts, (real_ref, imag_ref, up_ref, gate_ref, down_ref, total, sems) = refs[: ways + 3], refs[ways + 3 :]
    place = where_ref[0]
    rows = parts[0].shape[0]
    for n in range(2 * ways):
        k = n % ways
        half = place % 2 if n < ways else 1 - place % 2
        at = (half * ways + ((place // 2) ^ k)) * rows
        middle = ways // 2 + 1
        if n <= ways:
            part = parts[n][...]
        elif k >= middle:
            part = parts[ways + 1][(k - middle) * rows : (k - middle + 1) * rows, :]
        else:
            part = parts[ways + 2][(k - 1) * rows : k * rows, :]
        total[pl.ds(pl.multiple_of(at, 16), rows), :] = part.astype(F32)
    per_s, per_f, width = real_ref.shape[0], down_ref.shape[0], up_ref.shape[0]
    first = 2 * per_s + per_f
    moves = [
        (total.at[pl.ds(first, width), pl.ds(0, per_f)], up_ref),
        (total.at[pl.ds(first, width), pl.ds(per_f, per_f)], gate_ref),
        (total.at[pl.ds(2 * per_s, per_f), :], down_ref),
        (total.at[pl.ds(0, per_s), :], real_ref),
        (total.at[pl.ds(per_s, per_s), :], imag_ref),
    ]
    fetch(moves, sems)


def finish_kernel(where_ref, mine_ref, other_ref, a_ref, logs_ref, *refs):
    outs, (grads_ref, logs, sems) = refs[:8], refs[8:]
    width = grads_ref.shape[1]
    per_s = logs_ref.shape[2]
    grads = mine_ref[...].astype(F32) + other_ref[...].astype(F32)
    grads_ref[...] = grads
    lam = [jnp.zeros((1, per_s), F32), jnp.zeros((1, per_s), F32)]
    for t in range(TENSOR):
        for n in range(2):
            at = (n * TENSOR + t) * per_s
            part = grads[2 * per_s + 3 : 2 * per_s + 4, at : at + per_s]
            lam[n] = jnp.where(where_ref[2] == t, part, lam[n])
    decay = jnp.exp(logs_ref[0])
    modulus = jnp.exp(-decay)
    angle = jnp.exp(logs_ref[1])
    cos, sin = jnp.cos(angle), jnp.sin(angle)
    logs[0] = -decay * modulus * (lam[0] * cos + lam[1] * sin)
    logs[1] = angle * modulus * (lam[1] * cos - lam[0] * sin)
    terms = a_ref[:per_s, :].astype(F32) * grads[:per_s, :] + a_ref[per_s : 2 * per_s, :].astype(F32) * grads[per_s : 2 * per_s, :]
    logs[2] = jnp.sum(terms.T, axis=0, keepdims=True)
    moves = [(grads_ref.at[pl.ds(2 * per_s + n, 1), :], outs[n]) for n in range(3)]
    moves += [(grads_ref.at[pl.ds(n * per_s, per_s), :], outs[3 + n]) for n in range(2)]
    moves += [(logs.at[n], outs[5 + n]) for n in range(3)]
    fetch(moves, sems)


def near(value):
    return pltpu.with_memory_space_constraint(value, pltpu.VMEM)


def call(kernel, scalars, inputs, outs, scratch, vmem, far_inputs=(), far_outs=()):
    here, anywhere = pl.BlockSpec(memory_space=pltpu.VMEM), pl.BlockSpec(memory_space=pl.ANY)
    single = not isinstance(outs, list)
    listed = [outs] if single else outs
    shapes = [
        jax.ShapeDtypeStruct(*out) if n in far_outs else pltpu.VMEM(*out) for n, out in enumerate(listed)
    ]
    out_specs = [anywhere if n in far_outs else here for n in range(len(listed))]
    return pl.pallas_call(
        kernel,
        in_specs=[pl.BlockSpec(memory_space=pltpu.SMEM)] * len(scalars)
        + [anywhere if n in far_inputs else here for n in range(len(inputs))],
        out_specs=out_specs[0] if single else out_specs,
        out_shape=shapes[0] if single else shapes,
        scratch_shapes=scratch,
        compiler_params=pltpu.CompilerParams(vmem_limit_bytes=vmem * MIB),
    )(
        *scalars,
        *[
            pltpu.with_memory_space_constraint(v, pltpu.HBM) if n in far_inputs else near(v)
            for n, v in enumerate(inputs)
        ],
    )


def core_swap(value):
    return lax.ppermute(value, "tensor", [(t, t ^ 1) for t in range(TENSOR)])


def side_swap(value):
    return lax.ppermute(value, "tensor", [(t, t ^ 2) for t in range(TENSOR)])


def gather_tensor(own, *first):
    across = after(side_swap(own), *first)
    return own, core_swap(own), across, core_swap(across)


def after(value, *first):
    return lax.optimization_barrier((value,) + first)[0]


def flip_dp(value, bits, groups):
    return lax.ppermute(value, "dp", [(i, i ^ bits) for i in range(groups)])


def shift_dp(value, by, groups):
    return lax.ppermute(value, "dp", [(i, i + by) for i in range(groups) if 0 <= i + by < groups])


def shards(
    tokens,
    cotangent,
    ln_gain,
    ln_bias,
    skip_gain,
    in_real,
    in_imag,
    out_real,
    out_imag,
    nu_log,
    theta_log,
    gamma_log,
    up_weight,
    gate_weight,
    down_weight,
    lengths,
    *,
    groups,
):
    seqs, length, width = tokens.shape
    per_s = in_real.shape[1]
    per_f = up_weight.shape[1]
    states = per_s * TENSOR
    own_seqs = seqs // 2
    rows = own_seqs * length
    blocks = rows // BLOCK
    place = lax.axis_index("dp").astype(jnp.int32)
    shard = lax.axis_index("tensor").astype(jnp.int32)
    core = shard % 2
    where = jnp.stack([place, core, shard])

    tok_rows = tokens.reshape(seqs * length, width)
    cot_rows = cotangent.reshape(seqs * length, width)
    row = lambda v: v.reshape(1, width)
    gain_row, bias_row, skip_row = row(ln_gain), row(ln_bias), row(skip_gain)
    a_shape = (2 * per_s + PARAM_ROWS, width)
    b_shape = (2 * per_s + per_f, width)
    lanes = 2 * states
    units = TENSOR * per_f
    ends_shape = ((own_seqs, lanes), F32)
    dma = pltpu.SemaphoreType.DMA
    line = lambda v: v.reshape(1, per_s)

    pack_a, logs, own_tok, own_cot = call(
        input_pack_kernel,
        [where],
        [in_real.T, in_imag.T, line(nu_log), line(theta_log), line(gamma_log), tok_rows, cot_rows],
        [(a_shape, BF16), ((3, 1, per_s), F32), ((rows, width), BF16), ((rows, width), BF16)],
        [dma((5,)), dma((2,))],
        4,
        far_inputs=range(7),
    )
    pack_b, pack_g = call(
        weight_pack_kernel,
        [],
        [after(out_real, pack_a), out_imag, up_weight, gate_weight, down_weight],
        [(b_shape, BF16), ((width, 2 * per_f), BF16)],
        [dma((5,))],
        4,
        far_inputs=range(5),
    )
    low, normed, inv, cot_m = call(
        functools.partial(norm_kernel, length=length),
        [where],
        [own_tok, after(own_cot, pack_b), gain_row, bias_row, lengths],
        [((rows, width), BF16), ((rows, width), F32), ((rows, 128), F32), ((rows, width), BF16)],
        [
            pltpu.VMEM((1, width), F32),
            pltpu.VMEM((1, width), F32),
            pltpu.SMEM((seqs,), jnp.int32),
            dma((3,)),
        ],
        8,
        far_inputs=(2, 3, 4),
    )
    packs_a = gather_tensor(pack_a, low)
    pack_b, pack_g = after((pack_b, pack_g), packs_a[2])
    drive, ends, powers = call(
        functools.partial(drive_kernel, length=length),
        [where],
        [low, *packs_a],
        [((rows, lanes), F32), ends_shape, ((TILE, lanes), F32)],
        [pltpu.VMEM((lanes, width), BF16), pltpu.VMEM((2, length, states), F32)],
        8,
    )
    local = call(
        functools.partial(scan_kernel, length=length, backwards=False),
        [],
        [drive, *packs_a],
        ((rows, lanes), F32),
        [pltpu.VMEM((4, 2, TILE, states), F32)],
        8,
    )

    ways = groups // 2
    levels = (ways - 1).bit_length()

    def exchange(mine, backwards, beside_work, first_work=None):
        beside = after(flip_dp(mine, 1, groups), beside_work)
        both = call(
            functools.partial(pair_kernel, backwards=backwards), [where], [mine, beside, powers], ends_shape, [], 2
        )
        found = [both]
        from_far = []
        for k in range(levels):
            step = 2 << k
            from_far.append(shift_dp(found[-1], -step if backwards else step, groups))
            if k == 0 and first_work is not None:
                from_far[0] = after(from_far[0], first_work(both))
            if k + 1 < levels:
                found.append(
                    call(functools.partial(join_kernel, row=1 + k), [], [found[-1], from_far[-1], powers], ends_shape, [], 2)
                )
        return from_far, beside, found

    far_ends, beside_ends, found_ends = exchange(ends, False, local)
    packs_b = gather_tensor(pack_b, far_ends[0])
    hid_grad = call(
        functools.partial(hidden_kernel, per_s=per_s),
        [where],
        [after(cot_m, found_ends[-1]), *packs_b],
        ((rows, units), BF16),
        [],
        8,
    )
    packs_g = gather_tensor(pack_g, hid_grad, *far_ends)

    pack_rows = -(-(2 * per_s + per_f + width) // (16 * groups)) * 16 * groups
    state, back_drive, back_ends, y_low, hid, own_b, sent_b = call(
        functools.partial(middle_kernel, length=length, levels=levels),
        [where],
        [
            *far_ends,
            beside_ends,
            powers,
            local,
            normed,
            hid_grad,
            cot_m,
            *packs_a,
            gain_row,
            bias_row,
            skip_row,
            *packs_b,
            *packs_g,
        ],
        [
            ((rows, lanes), BF16),
            ((rows, lanes), F32),
            ends_shape,
            ((rows, width), BF16),
            ((rows, units), BF16),
            ((pack_rows, width), F32),
            ((pack_rows, width), BF16),
        ],
        [
            pltpu.VMEM((lanes, width), BF16),
            pltpu.VMEM((width, 2 * units), BF16),
            pltpu.VMEM((2, length, states), F32),
            pltpu.VMEM((2, length, states), F32),
            pltpu.VMEM((own_seqs, lanes), F32),
            pltpu.VMEM((LARGE, width), BF16),
            pltpu.VMEM((LARGE, 2 * units), BF16),
            pltpu.VMEM((states, width), F32),
            pltpu.VMEM((2 * per_f, width), F32),
            pltpu.VMEM((width, 4 * per_f), F32),
            dma((TENSOR, 3)),
        ],
        24,
    )
    half, part = pack_rows // 2, pack_rows // groups
    keep_b, send_b = call(
        fold_kernel,
        [where],
        [own_b, core_swap(sent_b)],
        [((half, width), F32), ((half, width), BF16)],
        [],
        4,
    )
    made = []

    def scan_work(pair_back):
        made.append(
            call(
                functools.partial(scan_kernel, length=length, backwards=True),
                [],
                [after(back_drive, pair_back), *packs_a],
                ((rows, lanes), F32),
                [pltpu.VMEM((4, 2, TILE, states), F32)],
                8,
            )
        )
        return made[0]

    far_back, beside_back, found_back = exchange(back_ends, True, send_b, scan_work)
    back = made[0]
    half_b = flip_dp(after(send_b, beside_back), 1, groups)
    out_own = call(
        functools.partial(down_kernel, length=length, per_s=per_s),
        [where, lengths],
        [own_tok, after(hid, found_back[-1]), *packs_b],
        ((rows, width), BF16),
        [pltpu.VMEM((units, width), BF16)],
        8,
    )
    dealt = call(
        deal_kernel,
        [where],
        [after(keep_b, out_own, *far_back), half_b],
        [((part, width), F32)] + [((part, width), BF16)] * (ways - 1),
        [],
        4,
    )

    grad_own, own_a, sent_a = call(
        functools.partial(last_kernel, length=length, levels=levels),
        [where],
        [
            *far_back,
            after(beside_back, dealt[0]),
            powers,
            low,
            normed,
            inv,
            cot_m,
            back,
            state,
            y_low,
            *packs_a,
            gain_row,
            bias_row,
            skip_row,
        ],
        [((rows, width), BF16), (a_shape, BF16), (a_shape, BF16)],
        [
            pltpu.VMEM((lanes, width), BF16),
            pltpu.VMEM((2, length, states), F32),
            pltpu.VMEM((own_seqs, lanes), F32),
            pltpu.VMEM((LARGE, lanes), BF16),
            pltpu.VMEM((states, width), F32),
            pltpu.VMEM((1, lanes), F32),
            pltpu.VMEM((TILE, width), F32),
        ],
        12,
    )

    mine_b = dealt[0]
    for k in range(1, ways):
        mine_b = mine_b + flip_dp(dealt[k], 2 * k, groups).astype(F32)
    mine_b = mine_b.astype(BF16)
    gathered = [mine_b] + [flip_dp(mine_b, 2 * k, groups) for k in range(1, ways)]
    middle = ways // 2 + 1
    beside = [
        flip_dp(jnp.concatenate(pieces, axis=0), 1, groups)
        for pieces in (gathered[:1], gathered[middle:], gathered[1:middle])
    ]

    grads_a = own_a.astype(F32) + after(core_swap(sent_a), mine_b).astype(F32)
    low_a = grads_a.astype(BF16)

    block_out = call(
        join_halves_kernel,
        [where],
        [out_own, core_swap(after(out_own, low_a))],
        [((seqs * length, width), BF16)],
        [dma((2,))],
        2,
        far_outs=(0,),
    )[0].reshape(seqs, length, width)
    input_grad = call(
        widen_halves_kernel,
        [where],
        [grad_own, core_swap(after(grad_own, low_a))],
        [((seqs * length, width), F32)],
        [pltpu.VMEM((4, BLOCK, width), F32), dma((4,))],
        4,
        far_outs=(0,),
    )[0].reshape(seqs, length, width)

    state_shape = ((per_s, width), F32)
    unpacked = call(
        functools.partial(unpack_kernel, ways=ways),
        [where],
        [*gathered, *beside[:2], after(beside[2], input_grad)],
        [state_shape] * 2 + [((width, per_f), F32)] * 2 + [((per_f, width), F32)],
        [pltpu.VMEM((pack_rows, width), F32), dma((5,))],
        8,
        far_outs=range(5),
    )
    works = {1: [block_out], 2: [beside[0]], 4: unpacked}
    bit = 1
    while bit < groups:
        other_a = after(flip_dp(low_a, bit, groups), *works.get(bit, []))
        bit *= 2
        if bit < groups:
            low_a = (low_a.astype(F32) + other_a.astype(F32)).astype(BF16)
        if bit == 4:
            low_a = after(low_a, *gathered)

    finished = call(
        finish_kernel,
        [where],
        [low_a, other_a, pack_a, logs],
        [((1, width), F32)] * 3 + [state_shape] * 2 + [((1, per_s), F32)] * 3,
        [pltpu.VMEM(a_shape, F32), pltpu.VMEM((3, 1, per_s), F32), dma((8,))],
        4,
        far_outs=range(8),
    )
    return (
        block_out,
        input_grad,
        *[v.reshape(width) for v in finished[:3]],
        *[v.T for v in finished[3:5]],
        *unpacked[:2],
        *[v.reshape(per_s) for v in finished[5:]],
        *unpacked[2:],
    )


def solution(mesh):
    rows = P(None, "dp", None)
    columns = P(None, "tensor")
    lines = P("tensor", None)
    vector = P("tensor")
    in_specs = (rows, rows, P(), P(), P(), columns, columns, lines, lines, vector, vector, vector, columns, columns, lines, P())
    out_specs = (rows, rows, P(), P(), P(), columns, columns, lines, lines, vector, vector, vector, columns, columns, lines)
    return jax.shard_map(
        functools.partial(shards, groups=mesh.shape["dp"]),
        mesh=mesh,
        in_specs=in_specs,
        out_specs=out_specs,
        check_vma=False,
    )
```

```python
import functools
import math

import jax
import jax.numpy as jnp
from jax import lax
from jax.experimental import pallas as pl
from jax.experimental.pallas import tpu as pltpu
from jax.sharding import PartitionSpec as P

EPSILON = 1e-05
TENSOR = 4
TILE = 8
BLOCK = 256
LARGE = 768
PARAM_ROWS = 16
F32 = jnp.float32
BF16 = jnp.bfloat16
GELU_K = math.sqrt(2.0 / math.pi)
MIB = 1024 * 1024


def dot(left, right):
    return jnp.dot(left, right, preferred_element_type=F32)


def dot_nt(left, right):
    return lax.dot_general(left, right, (((1,), (1,)), ((), ())), preferred_element_type=F32)


def dot_tn(left, right):
    return lax.dot_general(left, right, (((0,), (0,)), ((), ())), preferred_element_type=F32)


def layer_norm(rows):
    centre = jnp.mean(rows, axis=-1, keepdims=True)
    shifted = rows - centre
    variance = jnp.mean(shifted * shifted, axis=-1, keepdims=True)
    inv_scale = lax.rsqrt(variance + EPSILON)
    return shifted * inv_scale, inv_scale


def cmul(ar, ai, br, bi):
    return ar * br - ai * bi, ar * bi + ai * br


def read_params(packs, row):
    total = None
    for pack in packs:
        rows = pack[row : row + PARAM_ROWS, :].astype(F32)
        total = rows if total is None else total + rows
    states = total.shape[1] // 2
    at = lambda k: total[k : k + 1, :states] + total[k + 3 : k + 4, :states] + total[k + 6 : k + 7, :states]
    return at(0), at(1), at(2)


def powers_of(decay_real, decay_imag, exponent):
    out_r = jnp.ones(exponent.shape, F32)
    out_i = jnp.zeros(exponent.shape, F32)
    br, bi = decay_real, decay_imag
    for bit in range(4):
        mr, mi = cmul(out_r, out_i, br, bi)
        on = ((exponent >> bit) & 1) == 1
        out_r = jnp.where(on, mr, out_r)
        out_i = jnp.where(on, mi, out_i)
        br, bi = cmul(br, bi, br, bi)
    return out_r, out_i


def fill_steps(decay_real, decay_imag, backwards, step_ref):
    states = decay_real.shape[1]
    row = lax.broadcasted_iota(jnp.int32, (TILE, states), 0)
    if backwards:
        row = TILE - 1 - row
    zero = jnp.zeros((TILE, states), F32)
    for k, shift in enumerate((1, 2, 4)):
        pr, pi = powers_of(decay_real, decay_imag, jnp.full((TILE, states), shift, jnp.int32))
        step_ref[k, 0] = jnp.where(row >= shift, pr, zero)
        step_ref[k, 1] = jnp.where(row >= shift, pi, zero)
    step_ref[3, 0], step_ref[3, 1] = powers_of(decay_real, decay_imag, row + 1)


def fill_powers(decay_real, decay_imag, backwards, first, full_ref):
    states = decay_real.shape[1]
    row = lax.broadcasted_iota(jnp.int32, (TILE, states), 0)
    if backwards:
        row = TILE - 1 - row
    pr, pi = powers_of(decay_real, decay_imag, row + first)
    er, ei = powers_of(decay_real, decay_imag, jnp.full((TILE, states), TILE, jnp.int32))
    tiles = full_ref.shape[1] // TILE
    for n in range(tiles):
        at = (tiles - 1 - n if backwards else n) * TILE
        full_ref[0, at : at + TILE, :] = pr
        full_ref[1, at : at + TILE, :] = pi
        pr, pi = cmul(pr, pi, er, ei)


def scan_block(drive_ref, out_ref, step_ref, length, backwards):
    rows, lanes = drive_ref.shape
    states = lanes // 2
    tiles = length // TILE
    table = [(step_ref[k, 0], step_ref[k, 1]) for k in range(4)]
    edge = 0 if backwards else TILE - 1
    for s in range(rows // length):
        cr = ci = None
        for n in range(tiles):
            at = s * length + (tiles - 1 - n if backwards else n) * TILE
            hr = drive_ref[at : at + TILE, :states]
            hi = drive_ref[at : at + TILE, states:]
            for k, shift in enumerate((1, 2, 4)):
                turn = TILE - shift if backwards else shift
                sr = pltpu.roll(hr, turn, 0)
                si = pltpu.roll(hi, turn, 0)
                mr, mi = cmul(table[k][0], table[k][1], sr, si)
                hr, hi = hr + mr, hi + mi
            if cr is not None:
                mr, mi = cmul(table[3][0], table[3][1], cr, ci)
                hr, hi = hr + mr, hi + mi
            out_ref[at : at + TILE, :states] = hr
            out_ref[at : at + TILE, states:] = hi
            cr, ci = hr[edge : edge + 1], hi[edge : edge + 1]


def each_block(rows, size, body):
    def step(block, carry):
        at = pl.multiple_of(block * size, size)
        body(block, lambda ref: ref.at[pl.ds(at, size), :])
        return carry

    lax.fori_loop(0, rows // size, step, 0)


def fetch(pairs, sems, behind=()):
    copies = [pltpu.make_async_copy(src, dst, sems.at[n]) for n, (src, dst) in enumerate(pairs)]
    for copy in copies + list(behind):
        copy.start()
    for copy in copies:
        copy.wait()


def incoming(far_refs, beside_ref, odd, powers_ref, backwards, out_ref):
    states = out_ref.shape[1] // 2
    early, late = slice(0, states), slice(states, None)
    sr, si = far_refs[0][:, early], far_refs[0][:, late]
    for k in range(1, len(far_refs)):
        row = slice(4 + k, 5 + k)
        mr, mi = cmul(powers_ref[row, early], powers_ref[row, late], far_refs[k][:, early], far_refs[k][:, late])
        sr, si = sr + mr, si + mi
    mr, mi = cmul(powers_ref[0:1, early], powers_ref[0:1, late], sr, si)
    second = odd == (0 if backwards else 1)
    out_ref[:, early] = jnp.where(second, mr + beside_ref[:, early], sr)
    out_ref[:, late] = jnp.where(second, mi + beside_ref[:, late], si)


def join_kernel(mine_ref, other_ref, powers_ref, out_ref, *, row):
    states = out_ref.shape[1] // 2
    early, late = slice(0, states), slice(states, None)
    row = slice(row, row + 1)
    mr, mi = cmul(powers_ref[row, early], powers_ref[row, late], other_ref[:, early], other_ref[:, late])
    out_ref[:, early] = mine_ref[:, early] + mr
    out_ref[:, late] = mine_ref[:, late] + mi


def pair_kernel(where_ref, mine_ref, other_ref, powers_ref, out_ref, *, backwards):
    states = out_ref.shape[1] // 2
    second = where_ref[0] % 2 == (0 if backwards else 1)
    lr, li = powers_ref[0:1, :states], powers_ref[0:1, states:]
    pick = lambda first, part: jnp.where(second == first, other_ref[:, part], mine_ref[:, part])
    early, late = slice(0, states), slice(states, None)
    mr, mi = cmul(lr, li, pick(True, early), pick(True, late))
    out_ref[:, :states] = mr + pick(False, early)
    out_ref[:, states:] = mi + pick(False, late)


def assemble_input(packs, shard, out_ref):
    per = packs[0].shape[0] - PARAM_ROWS
    half = per // 2
    states = out_ref.shape[0] // 2
    for k, pack in enumerate(packs):
        at = pl.multiple_of((shard ^ k) * half, half)
        out_ref[pl.ds(at, half), :] = pack[:half, :]
        out_ref[pl.ds(states + at, half), :] = pack[half:per, :]


def input_pack_kernel(
    where_ref, in_real, in_imag, nu, theta, gamma, tok_all, cot_all, a_ref, logs, tok, cot, sems, row_sems
):
    per_s, width = in_real.shape
    rows = tok.shape[0]
    mine = pl.ds(pl.multiple_of(where_ref[1] * rows, BLOCK), rows)
    halves = [
        pltpu.make_async_copy(src.at[mine, :], dst, row_sems.at[n]) for n, (src, dst) in enumerate(((tok_all, tok), (cot_all, cot)))
    ]
    fetch(
        [(in_real, a_ref.at[pl.ds(0, per_s), :]), (in_imag, a_ref.at[pl.ds(per_s, per_s), :])]
        + [(ref, logs.at[n]) for n, ref in enumerate((nu, theta, gamma))],
        sems,
        halves,
    )
    modulus = jnp.exp(-jnp.exp(logs[0]))
    angle = jnp.exp(logs[1])
    rest = [modulus * jnp.cos(angle), modulus * jnp.sin(angle), jnp.exp(logs[2])]
    rows = []
    for _ in range(3):
        for n in range(3):
            high = rest[n].astype(BF16).astype(F32)
            rows.append(high)
            rest[n] = rest[n] - high
    table = jnp.concatenate(rows + [jnp.zeros((PARAM_ROWS - 9, per_s), F32)], axis=0)
    table = jnp.concatenate([table] * (width // per_s), axis=1)
    here = lax.broadcasted_iota(jnp.int32, (PARAM_ROWS, width), 1) // per_s == where_ref[2]
    a_ref[2 * per_s :, :] = jnp.where(here, table, 0.0).astype(BF16)
    for copy in halves:
        copy.wait()


def weight_pack_kernel(out_real, out_imag, up, gate, down, b_ref, g_ref, sems):
    per_s, per_f = out_real.shape[0], down.shape[0]
    fetch(
        [
            (out_real, b_ref.at[pl.ds(0, per_s), :]),
            (out_imag, b_ref.at[pl.ds(per_s, per_s), :]),
            (down, b_ref.at[pl.ds(2 * per_s, per_f), :]),
            (up, g_ref.at[:, pl.ds(0, per_f)]),
            (gate, g_ref.at[:, pl.ds(per_f, per_f)]),
        ],
        sems,
    )


def mask_rows(lens_ref, where_ref, seq, seqs, length, width):
    left = lens_ref[where_ref[1] * seqs + seq] - where_ref[0] * length
    return lax.broadcasted_iota(jnp.int32, (length, width), 0) < left


def norm_kernel(
    where_ref, tok, cot, gain_all, bias_all, lens_all, low_ref, normed_ref, inv_ref, cotm_ref,
    gain_ref, bias_ref, lens_ref, sems, *, length
):
    rows, width = low_ref.shape
    fetch([(gain_all, gain_ref), (bias_all, bias_ref), (lens_all, lens_ref)], sems)
    for block in range(rows // BLOCK):
        span = slice(block * BLOCK, (block + 1) * BLOCK)
        normed, inv_scale = layer_norm(tok[span, :].astype(F32))
        normed_ref[span, :] = normed
        inv_ref[span, :] = jnp.broadcast_to(inv_scale, (BLOCK, inv_ref.shape[1]))
        low_ref[span, :] = (normed * gain_ref[...] + bias_ref[...]).astype(BF16)
        for seq in range(block * BLOCK // length, (block + 1) * BLOCK // length):
            span = slice(seq * length, (seq + 1) * length)
            live = mask_rows(lens_ref, where_ref, seq, rows // length, length, width)
            cotm_ref[span, :] = jnp.where(live, cot[span, :].astype(F32), 0.0).astype(BF16)


def weighted_ends(drive_ref, weigh, length, first, ends_ref):
    rows, lanes = drive_ref.shape
    states = lanes // 2
    for s in range(rows // length):
        er = ei = jnp.zeros((TILE, states), F32)
        for n in range(length // TILE):
            at = s * length + n * TILE
            mr, mi = cmul(
                weigh[0, n * TILE : (n + 1) * TILE, :],
                weigh[1, n * TILE : (n + 1) * TILE, :],
                drive_ref[at : at + TILE, :states],
                drive_ref[at : at + TILE, states:],
            )
            er, ei = er + mr, ei + mi
        ends_ref[pl.ds(first + s, 1), :states] = jnp.sum(er, axis=0, keepdims=True)
        ends_ref[pl.ds(first + s, 1), states:] = jnp.sum(ei, axis=0, keepdims=True)


def drive_kernel(where_ref, low_all, a0, a1, a2, a3, drive_all, ends_ref, powers_ref, in_t, weigh, *, length):
    packs = (a0, a1, a2, a3)
    states = in_t.shape[0] // 2
    assemble_input(packs, where_ref[2], in_t)
    dr, di, gain = read_params(packs, a0.shape[0] - PARAM_ROWS)
    fill_powers(dr, di, True, 0, weigh)
    gam = jnp.concatenate([gain, gain], axis=1)
    lr, li = cmul(weigh[0, :1, :], weigh[1, :1, :], dr, di)
    rows = [(lr, li)] + [cmul(lr, li, lr, li)]
    for _ in range(2):
        rows.append(cmul(*rows[-1], *rows[-1]))
    rows.append((jnp.ones_like(lr), jnp.zeros_like(lr)))
    for _ in range(3):
        rows.append(cmul(*cmul(*rows[-1], *rows[-1]), *rows[1]))
    for k, (lr, li) in enumerate(rows):
        powers_ref[k : k + 1, :] = jnp.concatenate([lr, li], axis=1)
    per_block = LARGE // length

    def body(block, view):
        low_ref, drive_ref = view(low_all), view(drive_all)
        drive_ref[...] = dot_nt(low_ref[...], in_t[...]) * gam
        weighted_ends(drive_ref, weigh, length, block * per_block, ends_ref)

    each_block(low_all.shape[0], LARGE, body)


def scan_kernel(drive_all, a0, a1, a2, a3, local_all, step, *, length, backwards):
    dr, di, _ = read_params((a0, a1, a2, a3), a0.shape[0] - PARAM_ROWS)
    fill_steps(dr, di, backwards, step)
    each_block(
        drive_all.shape[0],
        BLOCK,
        lambda block, view: scan_block(view(drive_all), view(local_all), step, length, backwards),
    )


def hidden_kernel(where_ref, cotm_all, b0, b1, b2, b3, hg_all, *, per_s):
    shard = where_ref[2]
    per_f = hg_all.shape[1] // TENSOR

    def body(block, view):
        hg_ref, cotm = view(hg_all), view(cotm_all)[...]
        for k, pack in enumerate((b0, b1, b2, b3)):
            at = pl.multiple_of((shard ^ k) * per_f, per_f)
            hg_ref[:, pl.ds(at, per_f)] = dot_nt(cotm, pack[2 * per_s :, :]).astype(BF16)

    each_block(cotm_all.shape[0], LARGE, body)


def middle_kernel(where_ref, *refs, length, levels):
    far_refs, refs = refs[:levels], refs[levels:]
    beside_ref, powers_ref, local_all, normed_all, hg_all, cotm_all, a0, a1, a2, a3 = refs[:10]
    gain_ref, bias_ref, skip_ref, b0, b1, b2, b3, g0, g1, g2, g3 = refs[10:21]
    state_all, back_all, backends_ref, ylow_all, hid_all, own_ref, sent_ref = refs[21:28]
    c_all, ug_all, weigh, full, carry, act_ref, ul, acc_out, acc_down, acc_ug, sems = refs[28:]
    place, core, shard = where_ref[0], where_ref[1], where_ref[2]
    side = shard // 2
    states = c_all.shape[0] // 2
    rows, width = normed_all.shape
    per_block = LARGE // length
    per_s = states // TENSOR
    per_f = hid_all.shape[1] // TENSOR

    copies = []
    for k, (pack, gates) in enumerate(((b0, g0), (b1, g1), (b2, g2), (b3, g3))):
        t = shard ^ k
        moves = (
            (pack.at[pl.ds(0, per_s), :], c_all.at[pl.ds(pl.multiple_of(t * per_s, per_s), per_s), :]),
            (pack.at[pl.ds(per_s, per_s), :], c_all.at[pl.ds(pl.multiple_of(states + t * per_s, per_s), per_s), :]),
            (gates, ug_all.at[:, pl.ds(pl.multiple_of(t * 2 * per_f, 2 * per_f), 2 * per_f)]),
        )
        for n, (src, dst) in enumerate(moves):
            copies.append(pltpu.make_async_copy(src, dst, sems.at[k, n]))
    for copy in copies:
        copy.start()
    dr, di, _ = read_params((a0, a1, a2, a3), a0.shape[0] - PARAM_ROWS)
    fill_powers(dr, di, False, 1, full)
    incoming(far_refs, beside_ref, place % 2, powers_ref, False, carry)
    fill_powers(dr, di, False, 0, weigh)
    acc_out[...] = jnp.zeros(acc_out.shape, F32)
    acc_down[...] = jnp.zeros(acc_down.shape, F32)
    acc_ug[...] = jnp.zeros(acc_ug.shape, F32)
    for copy in copies:
        copy.wait()
    skip = skip_ref[...]
    skip_gain, skip_bias = gain_ref[...] * skip, bias_ref[...] * skip

    def body(block, view):
        local_ref, state_ref, hid_ref, ylow_ref = view(local_all), view(state_all), view(hid_all), view(ylow_all)
        hg_ref, back_ref = view(hg_all), view(back_all)
        for s in range(per_block):
            seq = block * per_block + s
            span = slice(s * length, (s + 1) * length)
            sr = carry[pl.ds(seq, 1), :states]
            si = carry[pl.ds(seq, 1), states:]
            mr, mi = cmul(full[0], full[1], sr, si)
            state_ref[span, :states] = (local_ref[span, :states] + mr).astype(BF16)
            state_ref[span, states:] = (-(local_ref[span, states:] + mi)).astype(BF16)
        y = dot(state_ref[...], c_all[...]) + (view(normed_all)[...] * skip_gain + skip_bias)
        square = y * y
        th = jnp.tanh(y * (GELU_K + (GELU_K * 0.044715) * square))
        half_y = 0.5 * y
        act_ref[...] = (half_y + half_y * th).astype(BF16)
        slope = (0.5 + 0.5 * th) + half_y * (1.0 - th * th) * (GELU_K + (GELU_K * 3 * 0.044715) * square)
        act = act_ref[...]
        for t in range(TENSOR):
            both = dot(act, ug_all[:, 2 * per_f * t : 2 * per_f * (t + 1)])
            up = both[:, :per_f]
            th = 0.5 * jnp.tanh(0.5 * both[:, per_f:])
            sig = 0.5 + th
            hid_ref[:, per_f * t : per_f * (t + 1)] = (up * sig).astype(BF16)
            up_grad = hg_ref[:, per_f * t : per_f * (t + 1)].astype(F32) * sig
            ul[:, 2 * per_f * t : 2 * per_f * t + per_f] = up_grad.astype(BF16)
            ul[:, 2 * per_f * t + per_f : 2 * per_f * (t + 1)] = (up_grad * up * (0.5 - th)).astype(BF16)
        y_grad = dot_nt(ul[...], ug_all[...]) * slope
        ylow_ref[...] = y_grad.astype(BF16)
        back_ref[...] = dot_nt(ylow_ref[...], c_all[...])
        acc_ug[...] += dot_tn(act, ul[:, pl.ds(pl.multiple_of(side * 4 * per_f, 4 * per_f), 4 * per_f)])
        hid = hid_ref[:, pl.ds(pl.multiple_of(side * 2 * per_f, 2 * per_f), 2 * per_f)]
        acc_down[...] += dot_tn(hid, view(cotm_all)[...])
        for k in range(2):
            cols = state_ref[:, pl.ds(pl.multiple_of(k * states + side * 2 * per_s, 2 * per_s), 2 * per_s)]
            acc_out[k * 2 * per_s : (k + 1) * 2 * per_s, :] += dot_tn(cols, ylow_ref[...])
        weighted_ends(back_ref, weigh, length, block * per_block, backends_ref)

    each_block(rows, LARGE, body)
    for n, ref in ((core, own_ref), (1 - core, sent_ref)):
        for k in range(2):
            part = acc_out[pl.ds(pl.multiple_of(2 * per_s * k + n * per_s, per_s), per_s), :]
            ref[k * per_s : (k + 1) * per_s, :] = part.astype(ref.dtype)
        part = acc_down[pl.ds(pl.multiple_of(n * per_f, per_f), per_f), :]
        ref[2 * per_s : 2 * per_s + per_f, :] = part.astype(ref.dtype)
        part = acc_ug[:, pl.ds(pl.multiple_of(n * 2 * per_f, 2 * per_f), 2 * per_f)]
        ref[2 * per_s + per_f : 2 * per_s + per_f + width, :] = part.astype(ref.dtype)


def down_kernel(where_ref, lens_ref, tok, hid_all, b0, b1, b2, b3, out_all, down_all, *, length, per_s):
    shard = where_ref[2]
    rows, width = out_all.shape
    per_block = LARGE // length
    per_f = down_all.shape[0] // TENSOR
    for k, pack in enumerate((b0, b1, b2, b3)):
        down_all[pl.ds(pl.multiple_of((shard ^ k) * per_f, per_f), per_f), :] = pack[2 * per_s :, :]

    def body(block, view):
        added = dot(view(hid_all)[...], down_all[...])
        out_ref, tok_ref = view(out_all), view(tok)
        for s in range(per_block):
            span = slice(s * length, (s + 1) * length)
            live = mask_rows(lens_ref, where_ref, block * per_block + s, rows // length, length, width)
            out_ref[span, :] = jnp.where(live, tok_ref[span, :].astype(F32) + added[span, :], 0.0).astype(BF16)

    each_block(rows, LARGE, body)


def last_kernel(where_ref, *refs, length, levels):
    far_refs, refs = refs[:levels], refs[levels:]
    beside_ref, powers_ref, low_all, normed_all, inv_all, cotm_all, back_all, state_all, ylow_all = refs[:9]
    a0, a1, a2, a3, gain_ref, bias_ref, skip_ref, grad_all, own_ref, sent_ref = refs[9:19]
    in_t, full, carry, dlow, in_grad, lam_grad, vec_grad = refs[19:]
    place, core, shard = where_ref[0], where_ref[1], where_ref[2]
    states = in_t.shape[0] // 2
    rows, width = low_all.shape
    per_block = LARGE // length
    per_s = states // TENSOR
    packs = (a0, a1, a2, a3)

    assemble_input(packs, shard, in_t)
    dr, di, gain = read_params(packs, a0.shape[0] - PARAM_ROWS)
    fill_powers(dr, di, True, 1, full)
    incoming(far_refs, beside_ref, place % 2, powers_ref, True, carry)
    in_grad[...] = jnp.zeros(in_grad.shape, F32)
    lam_grad[...] = jnp.zeros(lam_grad.shape, F32)
    vec_grad[...] = jnp.zeros(vec_grad.shape, F32)
    at = pl.multiple_of((shard // 2) * 2 * per_s, 2 * per_s)

    def body(block, view):
        back_ref, state_ref = view(back_all), view(state_all)
        for s in range(per_block):
            seq = block * per_block + s
            span = slice(s * length, (s + 1) * length)
            sr = carry[pl.ds(seq, 1), :states]
            si = carry[pl.ds(seq, 1), states:]
            mr, mi = cmul(full[0], full[1], sr, si)
            gr = back_ref[span, :states] + mr
            gi = back_ref[span, states:] + mi
            dlow[span, :states] = (gr * gain).astype(BF16)
            dlow[span, states:] = (gi * -gain).astype(BF16)
            nr = jnp.concatenate([gr[1:], sr], axis=0)
            ni = jnp.concatenate([gi[1:], si], axis=0)
            hr = state_ref[span, :states].astype(F32)
            hi = state_ref[span, states:].astype(F32)
            lam_grad[:, :states] += jnp.sum(nr * hr + ni * hi, axis=0, keepdims=True)
            lam_grad[:, states:] += jnp.sum(nr * hi - ni * hr, axis=0, keepdims=True)
        normed = view(normed_all)[...]
        ylow = view(ylow_all)[...].astype(F32)
        low = view(low_all)[...]
        u_grad = dot(dlow[...], in_t[...]) + ylow * skip_ref[...]
        vec_grad[0:1, :] += jnp.sum(u_grad * normed, axis=0, keepdims=True)
        vec_grad[1:2, :] += jnp.sum(u_grad, axis=0, keepdims=True)
        vec_grad[2:3, :] += jnp.sum(ylow * (normed * gain_ref[...] + bias_ref[...]), axis=0, keepdims=True)
        scaled = u_grad * gain_ref[...]
        grad = (
            scaled
            - jnp.mean(scaled, axis=-1, keepdims=True)
            - normed * jnp.mean(scaled * normed, axis=-1, keepdims=True)
        )
        view(grad_all)[...] = (view(cotm_all)[...].astype(F32) + view(inv_all)[:, :1] * grad).astype(BF16)
        for k in range(2):
            cols = dlow[:, pl.ds(k * states + at, 2 * per_s)]
            in_grad[2 * per_s * k : 2 * per_s * (k + 1), :] += dot_tn(cols, low)

    each_block(rows, LARGE, body)
    small = jnp.concatenate(
        [vec_grad[:3, :], lam_grad[...], jnp.zeros((PARAM_ROWS - 4, width), F32)], axis=0
    ).astype(BF16)
    for n, ref in ((core, own_ref), (1 - core, sent_ref)):
        for k in range(2):
            part = in_grad[pl.ds(pl.multiple_of(2 * per_s * k + n * per_s, per_s), per_s), :]
            ref[k * per_s : (k + 1) * per_s, :] = part.astype(BF16)
        ref[2 * per_s :, :] = small


def join_halves_kernel(where_ref, own_ref, other_ref, out_ref, sems):
    rows = own_ref.shape[0]
    copies = [
        pltpu.make_async_copy(ref, out_ref.at[pl.ds(pl.multiple_of(n * rows, BLOCK), rows), :], sems.at[k])
        for k, (n, ref) in enumerate(((where_ref[1], own_ref), (1 - where_ref[1], other_ref)))
    ]
    for copy in copies:
        copy.start()
    for copy in copies:
        copy.wait()


def widen_halves_kernel(where_ref, own_ref, other_ref, out_ref, wide, sems):
    rows = own_ref.shape[0]
    slots = wide.shape[0]
    flying = []
    for n in range(2 * rows // BLOCK):
        slot = n % slots
        if n >= slots:
            flying[n - slots].wait()
        at = (n // 2) * BLOCK
        half, ref = ((where_ref[1], own_ref), (1 - where_ref[1], other_ref))[n % 2]
        wide[slot] = ref[at : at + BLOCK, :].astype(F32)
        copy = pltpu.make_async_copy(
            wide.at[slot], out_ref.at[pl.ds(pl.multiple_of(half * rows + at, BLOCK), BLOCK), :], sems.at[slot]
        )
        copy.start()
        flying.append(copy)
    for copy in flying[-slots:]:
        copy.wait()


def fold_kernel(where_ref, own_ref, other_ref, keep_ref, send_ref):
    half = keep_ref.shape[0]
    odd = where_ref[0] % 2
    at = pl.multiple_of(odd * half, 16)
    keep_ref[...] = own_ref[pl.ds(at, half), :] + other_ref[pl.ds(at, half), :].astype(F32)
    at = pl.multiple_of((1 - odd) * half, 16)
    send_ref[...] = (own_ref[pl.ds(at, half), :] + other_ref[pl.ds(at, half), :].astype(F32)).astype(BF16)


def deal_kernel(where_ref, own_ref, other_ref, keep_ref, *send_refs):
    rows = keep_ref.shape[0]
    for k, ref in enumerate((keep_ref,) + send_refs):
        at = pl.multiple_of(((where_ref[0] // 2) ^ k) * rows, 16)
        ref[...] = (own_ref[pl.ds(at, rows), :] + other_ref[pl.ds(at, rows), :].astype(F32)).astype(ref.dtype)


def unpack_kernel(where_ref, *refs, ways):
    parts, (real_ref, imag_ref, up_ref, gate_ref, down_ref, total, sems) = refs[: ways + 3], refs[ways + 3 :]
    place = where_ref[0]
    rows = parts[0].shape[0]
    for n in range(2 * ways):
        k = n % ways
        half = place % 2 if n < ways else 1 - place % 2
        at = (half * ways + ((place // 2) ^ k)) * rows
        middle = ways // 2 + 1
        if n <= ways:
            part = parts[n][...]
        elif k >= middle:
            part = parts[ways + 1][(k - middle) * rows : (k - middle + 1) * rows, :]
        else:
            part = parts[ways + 2][(k - 1) * rows : k * rows, :]
        total[pl.ds(pl.multiple_of(at, 16), rows), :] = part.astype(F32)
    per_s, per_f, width = real_ref.shape[0], down_ref.shape[0], up_ref.shape[0]
    first = 2 * per_s + per_f
    moves = [
        (total.at[pl.ds(first, width), pl.ds(0, per_f)], up_ref),
        (total.at[pl.ds(first, width), pl.ds(per_f, per_f)], gate_ref),
        (total.at[pl.ds(2 * per_s, per_f), :], down_ref),
        (total.at[pl.ds(0, per_s), :], real_ref),
        (total.at[pl.ds(per_s, per_s), :], imag_ref),
    ]
    fetch(moves, sems)


def finish_kernel(where_ref, mine_ref, other_ref, a_ref, logs_ref, *refs):
    outs, (grads_ref, logs, sems) = refs[:8], refs[8:]
    width = grads_ref.shape[1]
    per_s = logs_ref.shape[2]
    grads = mine_ref[...].astype(F32) + other_ref[...].astype(F32)
    grads_ref[...] = grads
    lam = [jnp.zeros((1, per_s), F32), jnp.zeros((1, per_s), F32)]
    for t in range(TENSOR):
        for n in range(2):
            at = (n * TENSOR + t) * per_s
            part = grads[2 * per_s + 3 : 2 * per_s + 4, at : at + per_s]
            lam[n] = jnp.where(where_ref[2] == t, part, lam[n])
    decay = jnp.exp(logs_ref[0])
    modulus = jnp.exp(-decay)
    angle = jnp.exp(logs_ref[1])
    cos, sin = jnp.cos(angle), jnp.sin(angle)
    logs[0] = -decay * modulus * (lam[0] * cos + lam[1] * sin)
    logs[1] = angle * modulus * (lam[1] * cos - lam[0] * sin)
    terms = a_ref[:per_s, :].astype(F32) * grads[:per_s, :] + a_ref[per_s : 2 * per_s, :].astype(F32) * grads[per_s : 2 * per_s, :]
    logs[2] = jnp.sum(terms.T, axis=0, keepdims=True)
    moves = [(grads_ref.at[pl.ds(2 * per_s + n, 1), :], outs[n]) for n in range(3)]
    moves += [(grads_ref.at[pl.ds(n * per_s, per_s), :], outs[3 + n]) for n in range(2)]
    moves += [(logs.at[n], outs[5 + n]) for n in range(3)]
    fetch(moves, sems)


def near(value):
    return pltpu.with_memory_space_constraint(value, pltpu.VMEM)


def call(kernel, scalars, inputs, outs, scratch, vmem, far_inputs=(), far_outs=()):
    here, anywhere = pl.BlockSpec(memory_space=pltpu.VMEM), pl.BlockSpec(memory_space=pl.ANY)
    single = not isinstance(outs, list)
    listed = [outs] if single else outs
    shapes = [
        jax.ShapeDtypeStruct(*out) if n in far_outs else pltpu.VMEM(*out) for n, out in enumerate(listed)
    ]
    out_specs = [anywhere if n in far_outs else here for n in range(len(listed))]
    return pl.pallas_call(
        kernel,
        in_specs=[pl.BlockSpec(memory_space=pltpu.SMEM)] * len(scalars)
        + [anywhere if n in far_inputs else here for n in range(len(inputs))],
        out_specs=out_specs[0] if single else out_specs,
        out_shape=shapes[0] if single else shapes,
        scratch_shapes=scratch,
        compiler_params=pltpu.CompilerParams(vmem_limit_bytes=vmem * MIB),
    )(
        *scalars,
        *[
            pltpu.with_memory_space_constraint(v, pltpu.HBM) if n in far_inputs else near(v)
            for n, v in enumerate(inputs)
        ],
    )


def core_swap(value):
    return lax.ppermute(value, "tensor", [(t, t ^ 1) for t in range(TENSOR)])


def side_swap(value):
    return lax.ppermute(value, "tensor", [(t, t ^ 2) for t in range(TENSOR)])


def gather_tensor(own, *first):
    across = after(side_swap(own), *first)
    return own, core_swap(own), across, core_swap(across)


def after(value, *first):
    return lax.optimization_barrier((value,) + first)[0]


def flip_dp(value, bits, groups):
    return lax.ppermute(value, "dp", [(i, i ^ bits) for i in range(groups)])


def shift_dp(value, by, groups):
    return lax.ppermute(value, "dp", [(i, i + by) for i in range(groups) if 0 <= i + by < groups])


def shards(
    tokens,
    cotangent,
    ln_gain,
    ln_bias,
    skip_gain,
    in_real,
    in_imag,
    out_real,
    out_imag,
    nu_log,
    theta_log,
    gamma_log,
    up_weight,
    gate_weight,
    down_weight,
    lengths,
    *,
    groups,
):
    seqs, length, width = tokens.shape
    per_s = in_real.shape[1]
    per_f = up_weight.shape[1]
    states = per_s * TENSOR
    own_seqs = seqs // 2
    rows = own_seqs * length
    blocks = rows // BLOCK
    place = lax.axis_index("dp").astype(jnp.int32)
    shard = lax.axis_index("tensor").astype(jnp.int32)
    core = shard % 2
    where = jnp.stack([place, core, shard])

    tok_rows = tokens.reshape(seqs * length, width)
    cot_rows = cotangent.reshape(seqs * length, width)
    row = lambda v: v.reshape(1, width)
    gain_row, bias_row, skip_row = row(ln_gain), row(ln_bias), row(skip_gain)
    a_shape = (2 * per_s + PARAM_ROWS, width)
    b_shape = (2 * per_s + per_f, width)
    lanes = 2 * states
    units = TENSOR * per_f
    ends_shape = ((own_seqs, lanes), F32)
    dma = pltpu.SemaphoreType.DMA
    line = lambda v: v.reshape(1, per_s)

    pack_a, logs, own_tok, own_cot = call(
        input_pack_kernel,
        [where],
        [in_real.T, in_imag.T, line(nu_log), line(theta_log), line(gamma_log), tok_rows, cot_rows],
        [(a_shape, BF16), ((3, 1, per_s), F32), ((rows, width), BF16), ((rows, width), BF16)],
        [dma((5,)), dma((2,))],
        4,
        far_inputs=range(7),
    )
    pack_b, pack_g = call(
        weight_pack_kernel,
        [],
        [after(out_real, pack_a), out_imag, up_weight, gate_weight, down_weight],
        [(b_shape, BF16), ((width, 2 * per_f), BF16)],
        [dma((5,))],
        4,
        far_inputs=range(5),
    )
    low, normed, inv, cot_m = call(
        functools.partial(norm_kernel, length=length),
        [where],
        [own_tok, after(own_cot, pack_b), gain_row, bias_row, lengths],
        [((rows, width), BF16), ((rows, width), F32), ((rows, 128), F32), ((rows, width), BF16)],
        [
            pltpu.VMEM((1, width), F32),
            pltpu.VMEM((1, width), F32),
            pltpu.SMEM((seqs,), jnp.int32),
            dma((3,)),
        ],
        8,
        far_inputs=(2, 3, 4),
    )
    packs_a = gather_tensor(pack_a, low)
    pack_b, pack_g = after((pack_b, pack_g), packs_a[2])
    drive, ends, powers = call(
        functools.partial(drive_kernel, length=length),
        [where],
        [low, *packs_a],
        [((rows, lanes), F32), ends_shape, ((TILE, lanes), F32)],
        [pltpu.VMEM((lanes, width), BF16), pltpu.VMEM((2, length, states), F32)],
        8,
    )
    local = call(
        functools.partial(scan_kernel, length=length, backwards=False),
        [],
        [drive, *packs_a],
        ((rows, lanes), F32),
        [pltpu.VMEM((4, 2, TILE, states), F32)],
        8,
    )

    ways = groups // 2
    levels = (ways - 1).bit_length()

    def exchange(mine, backwards, beside_work, first_work=None):
        beside = after(flip_dp(mine, 1, groups), beside_work)
        both = call(
            functools.partial(pair_kernel, backwards=backwards), [where], [mine, beside, powers], ends_shape, [], 2
        )
        found = [both]
        from_far = []
        for k in range(levels):
            step = 2 << k
            from_far.append(shift_dp(found[-1], -step if backwards else step, groups))
            if k == 0 and first_work is not None:
                from_far[0] = after(from_far[0], first_work(both))
            if k + 1 < levels:
                found.append(
                    call(functools.partial(join_kernel, row=1 + k), [], [found[-1], from_far[-1], powers], ends_shape, [], 2)
                )
        return from_far, beside, found

    far_ends, beside_ends, found_ends = exchange(ends, False, local)
    packs_b = gather_tensor(pack_b, far_ends[0])
    hid_grad = call(
        functools.partial(hidden_kernel, per_s=per_s),
        [where],
        [after(cot_m, found_ends[-1]), *packs_b],
        ((rows, units), BF16),
        [],
        8,
    )
    packs_g = gather_tensor(pack_g, hid_grad, *far_ends)

    pack_rows = -(-(2 * per_s + per_f + width) // (16 * groups)) * 16 * groups
    state, back_drive, back_ends, y_low, hid, own_b, sent_b = call(
        functools.partial(middle_kernel, length=length, levels=levels),
        [where],
        [
            *far_ends,
            beside_ends,
            powers,
            local,
            normed,
            hid_grad,
            cot_m,
            *packs_a,
            gain_row,
            bias_row,
            skip_row,
            *packs_b,
            *packs_g,
        ],
        [
            ((rows, lanes), BF16),
            ((rows, lanes), F32),
            ends_shape,
            ((rows, width), BF16),
            ((rows, units), BF16),
            ((pack_rows, width), F32),
            ((pack_rows, width), BF16),
        ],
        [
            pltpu.VMEM((lanes, width), BF16),
            pltpu.VMEM((width, 2 * units), BF16),
            pltpu.VMEM((2, length, states), F32),
            pltpu.VMEM((2, length, states), F32),
            pltpu.VMEM((own_seqs, lanes), F32),
            pltpu.VMEM((LARGE, width), BF16),
            pltpu.VMEM((LARGE, 2 * units), BF16),
            pltpu.VMEM((states, width), F32),
            pltpu.VMEM((2 * per_f, width), F32),
            pltpu.VMEM((width, 4 * per_f), F32),
            dma((TENSOR, 3)),
        ],
        30,
    )
    half, part = pack_rows // 2, pack_rows // groups
    keep_b, send_b = call(
        fold_kernel,
        [where],
        [own_b, core_swap(sent_b)],
        [((half, width), F32), ((half, width), BF16)],
        [],
        4,
    )
    made = []

    def scan_work(pair_back):
        made.append(
            call(
                functools.partial(scan_kernel, length=length, backwards=True),
                [],
                [after(back_drive, pair_back), *packs_a],
                ((rows, lanes), F32),
                [pltpu.VMEM((4, 2, TILE, states), F32)],
                8,
            )
        )
        return made[0]

    far_back, beside_back, found_back = exchange(back_ends, True, send_b, scan_work)
    back = made[0]
    half_b = flip_dp(after(send_b, beside_back), 1, groups)
    out_own = call(
        functools.partial(down_kernel, length=length, per_s=per_s),
        [where, lengths],
        [own_tok, after(hid, found_back[-1]), *packs_b],
        ((rows, width), BF16),
        [pltpu.VMEM((units, width), BF16)],
        8,
    )
    dealt = call(
        deal_kernel,
        [where],
        [after(keep_b, out_own, *far_back), half_b],
        [((part, width), F32)] + [((part, width), BF16)] * (ways - 1),
        [],
        4,
    )

    grad_own, own_a, sent_a = call(
        functools.partial(last_kernel, length=length, levels=levels),
        [where],
        [
            *far_back,
            after(beside_back, dealt[0]),
            powers,
            low,
            normed,
            inv,
            cot_m,
            back,
            state,
            y_low,
            *packs_a,
            gain_row,
            bias_row,
            skip_row,
        ],
        [((rows, width), BF16), (a_shape, BF16), (a_shape, BF16)],
        [
            pltpu.VMEM((lanes, width), BF16),
            pltpu.VMEM((2, length, states), F32),
            pltpu.VMEM((own_seqs, lanes), F32),
            pltpu.VMEM((LARGE, lanes), BF16),
            pltpu.VMEM((states, width), F32),
            pltpu.VMEM((1, lanes), F32),
            pltpu.VMEM((TILE, width), F32),
        ],
        16,
    )

    mine_b = dealt[0]
    for k in range(1, ways):
        mine_b = mine_b + flip_dp(dealt[k], 2 * k, groups).astype(F32)
    mine_b = mine_b.astype(BF16)
    gathered = [mine_b] + [flip_dp(mine_b, 2 * k, groups) for k in range(1, ways)]
    middle = ways // 2 + 1
    beside = [
        flip_dp(jnp.concatenate(pieces, axis=0), 1, groups)
        for pieces in (gathered[:1], gathered[middle:], gathered[1:middle])
    ]

    grads_a = own_a.astype(F32) + after(core_swap(sent_a), mine_b).astype(F32)
    low_a = grads_a.astype(BF16)

    block_out = call(
        join_halves_kernel,
        [where],
        [out_own, core_swap(after(out_own, low_a))],
        [((seqs * length, width), BF16)],
        [dma((2,))],
        2,
        far_outs=(0,),
    )[0].reshape(seqs, length, width)
    input_grad = call(
        widen_halves_kernel,
        [where],
        [grad_own, core_swap(after(grad_own, low_a))],
        [((seqs * length, width), F32)],
        [pltpu.VMEM((4, BLOCK, width), F32), dma((4,))],
        4,
        far_outs=(0,),
    )[0].reshape(seqs, length, width)

    state_shape = ((per_s, width), F32)
    unpacked = call(
        functools.partial(unpack_kernel, ways=ways),
        [where],
        [*gathered, *beside[:2], after(beside[2], input_grad)],
        [state_shape] * 2 + [((width, per_f), F32)] * 2 + [((per_f, width), F32)],
        [pltpu.VMEM((pack_rows, width), F32), dma((5,))],
        8,
        far_outs=range(5),
    )
    works = {1: [block_out], 2: [beside[0]], 4: unpacked}
    bit = 1
    while bit < groups:
        other_a = after(flip_dp(low_a, bit, groups), *works.get(bit, []))
        bit *= 2
        if bit < groups:
            low_a = (low_a.astype(F32) + other_a.astype(F32)).astype(BF16)
        if bit == 4:
            low_a = after(low_a, *gathered)

    finished = call(
        finish_kernel,
        [where],
        [low_a, other_a, pack_a, logs],
        [((1, width), F32)] * 3 + [state_shape] * 2 + [((1, per_s), F32)] * 3,
        [pltpu.VMEM(a_shape, F32), pltpu.VMEM((3, 1, per_s), F32), dma((8,))],
        4,
        far_outs=range(8),
    )
    return (
        block_out,
        input_grad,
        *[v.reshape(width) for v in finished[:3]],
        *[v.T for v in finished[3:5]],
        *unpacked[:2],
        *[v.reshape(per_s) for v in finished[5:]],
        *unpacked[2:],
    )


def solution(mesh):
    rows = P(None, "dp", None)
    columns = P(None, "tensor")
    lines = P("tensor", None)
    vector = P("tensor")
    in_specs = (rows, rows, P(), P(), P(), columns, columns, lines, lines, vector, vector, vector, columns, columns, lines, P())
    out_specs = (rows, rows, P(), P(), P(), columns, columns, lines, lines, vector, vector, vector, columns, columns, lines)
    return jax.shard_map(
        functools.partial(shards, groups=mesh.shape["dp"]),
        mesh=mesh,
        in_specs=in_specs,
        out_specs=out_specs,
        check_vma=False,
    )
```
